32 devices in a mesh: tiles: 2 (over x), morton: 16 (over z, y, core).
Axes of the slice: x: 2, y: 2, z: 4, core: 2. Of those that a mesh axis runs over, the one named last changes fastest.
Arguments:
- features: bfloat16 [256, 512, 64], P(('tiles', 'morton')), parts along dimension 0, may hold values from -6 to 6
- neighbours: int32 [256, 27], P(('tiles', 'morton')), parts along dimension 0, may hold values from -1 to 127, as said below
- occupancy: int32 [256, 16], P(('tiles', 'morton')), parts along dimension 0, may hold values from -2147483648 to 2147483647, as said below
- conv_one: bfloat16 [27, 64, 64], replicated, may hold values from -0.21875 to 0.21875
- first_reduce_kernel: bfloat16 [8, 64, 128], replicated, may hold values from -0.5 to 0.5
- conv_two: bfloat16 [27, 128, 128], replicated, may hold values from -0.1875 to 0.1875
- second_reduce_kernel: bfloat16 [8, 128, 256], replicated, may hold values from -0.375 to 0.375
- conv_three: bfloat16 [27, 256, 256], replicated, may hold values from -0.125 to 0.125
Outputs:
- first_level_features: bfloat16 [256, 512, 64], P(('tiles', 'morton')), parts along dimension 0
- second_level_features: bfloat16 [256, 64, 128], P(('tiles', 'morton')), parts along dimension 0
- skip_three: bfloat16 [256, 8, 256], P(('tiles', 'morton')), parts along dimension 0
The draws below stay inside these ranges and needn't reach their ends.
There are 2 independent parts, one for each index of `tiles`. The reference program is written for one: setup_inputs(seed, part) draws one part's arguments, and reference() takes and returns one part's arrays. A program takes and returns all parts, laid end to end along the dimension named above; an argument that names none is the same for every part. Nothing has to cross between parts.
Inputs may be any that keep to these rules, and one draw needn't show every extreme that they name: `neighbours`: bricks are numbered by x slice, then by cell of the slice's 4 x 4 cross-section in rising order, 8 occupied bricks to a slice. Entry 9 (a+1) + 3 (c+1) + (e+1) of a brick's row is the number of the brick at offset (a, c, e), or -1 if that cell is empty or outside the tile; entry 13 is the brick itself. Every neighbour lies in the brick's own slice or in an adjacent one. Bit k, the lowest being bit 0, of word w of a brick's row is the occupancy of voxel 32 w + k; bit 31 is the sign bit of the word.
All inputs are finite; a program needn't handle non-finite values.
Results may differ from the reference program's by a relative error of at most 0.008.
Values may be sent and summed in bfloat16 or wider, within the bound.
No kernel may reach another device: no remote copies, remote signals or barrier semaphores. Data moves between devices by JAX's collectives and lax.ppermute only.
A program may use at most 128 MiB of HBM per device.

```python
import jax
import jax.numpy as jnp
from jax import lax

C1 = 64
C2 = 128
C3 = 256
BRICK_EDGE_VOXELS = 8
SLICE_BRICKS = 8
SLICES = 1
BRICKS = 128
V1 = 512
N_MORTON = 16


def draw_neighbours(key, part):
    slice_total = SLICES * N_MORTON
    scores = jax.random.randint(key, (slice_total, 16), 0, 1 << 20, dtype=jnp.int32) * 16 + jnp.arange(16, dtype=jnp.int32)
    order = jnp.argsort(scores, axis=1)
    ranks = jnp.argsort(order, axis=1)
    filled = (ranks < SLICE_BRICKS).astype(jnp.int32)
    rank_cell = (jnp.cumsum(filled, axis=1) - 1).astype(jnp.int32)
    cells = jnp.argsort(1 - filled, axis=1, stable=True)[:, :SLICE_BRICKS].astype(jnp.int32)
    slice_of = jnp.broadcast_to(jnp.arange(slice_total, dtype=jnp.int32)[:, None], cells.shape)
    row_pos = cells // 4
    col_pos = cells % 4
    entries = []
    for first in (-1, 0, 1):
        for second in (-1, 0, 1):
            for third in (-1, 0, 1):
                near_slice = slice_of + first
                near_row = row_pos + second
                near_col = col_pos + third
                inside = (near_slice >= 0) & (near_slice < slice_total) & (near_row >= 0) & (near_row < 4) & (near_col >= 0) & (near_col < 4)
                safe_slice = jnp.clip(near_slice, 0, slice_total - 1)
                safe_cell = jnp.clip(near_row, 0, 3) * 4 + jnp.clip(near_col, 0, 3)
                present = filled[safe_slice, safe_cell] == 1
                number = safe_slice * SLICE_BRICKS + rank_cell[safe_slice, safe_cell]
                entries.append(jnp.where(inside & present, number, -1).astype(jnp.int32))
    return jnp.stack(entries, axis=-1).reshape(slice_total * SLICE_BRICKS, 27)


def draw_occupancy(key, part):
    brick_side = BRICK_EDGE_VOXELS
    key_list = jax.random.split(key, 6)
    voxel_ids = jnp.arange(brick_side ** 3, dtype=jnp.int32)[None, :]
    depth_index = voxel_ids // (brick_side * brick_side)
    row_index = voxel_ids // brick_side % brick_side
    col_index = voxel_ids % brick_side
    facing = jax.random.randint(key_list[0], (BRICKS, 1), 0, 3, dtype=jnp.int32)
    height_base = jax.random.randint(key_list[1], (BRICKS, 1), 0, brick_side, dtype=jnp.int32)
    tilt_pair = jax.random.randint(key_list[2], (BRICKS, 2), -1, 2, dtype=jnp.int32)
    thickness = jax.random.randint(key_list[3], (BRICKS, 1), brick_side // 4, brick_side // 2 + 2, dtype=jnp.int32)
    present = jax.random.randint(key_list[4], (BRICKS, 1), 0, 8, dtype=jnp.int32) > 0
    retained = jax.random.randint(key_list[5], (BRICKS, brick_side ** 3), 0, 8, dtype=jnp.int32) > 0
    across = jnp.where(facing == 0, depth_index, jnp.where(facing == 1, row_index, col_index))
    along_one = jnp.where(facing == 0, row_index, depth_index)
    along_two = jnp.where(facing == 2, row_index, col_index)
    height = height_base - brick_side // 4 + (tilt_pair[:, 0:1] * along_one + tilt_pair[:, 1:2] * along_two) // 2
    offset = across - height
    occupied = (offset >= 0) & (offset < thickness) & retained & present
    bits = occupied.astype(jnp.int32).reshape(BRICKS, brick_side ** 3 // 32, 32)
    shifted = jnp.left_shift(bits, jnp.arange(32, dtype=jnp.int32))
    return jnp.sum(shifted, axis=-1, dtype=jnp.int32).astype(jnp.int32)


def block_levels(own_key, dims, pieces, least, largest):
    def one(axis_at, blocks):
        heights = jax.random.uniform(jax.random.fold_in(jax.random.fold_in(own_key, 6), axis_at), (blocks,), jnp.float32, least / len(pieces), largest / len(pieces))
        return jnp.repeat(jnp.exp(heights), dims[axis_at] // blocks).reshape((-1,) + (1,) * (len(dims) - axis_at - 1))

    factor_of = one(*pieces[0])
    for cut in pieces[1:]:
        factor_of = factor_of * one(*cut)
    return factor_of


def bell_draw(key, extent, width, bound, pieces=(), held_as=jnp.bfloat16):
    array = width * jax.random.normal(key, extent, jnp.float32)
    if pieces:
        array = array * block_levels(key, extent, pieces, -0.22, 0.18)
    return jnp.clip(array, -bound, bound).astype(held_as)


def setup_inputs(seed: int = 0, part: int = 0) -> dict:
    streams_of = jax.random.split(jax.random.key(seed), 9)
    part_splits = jax.random.split(jax.random.fold_in(streams_of[8], part), 9)
    features = bell_draw(part_splits[0], (BRICKS, V1, C1), 1.0, 6.0, ((0, 16),))
    neighbours = draw_neighbours(jax.random.fold_in(jax.random.fold_in(streams_of[8], part), 71), part)
    occupancy = draw_occupancy(jax.random.fold_in(jax.random.fold_in(streams_of[8], part), 71), part)
    conv_one = bell_draw(streams_of[3], (27, C1, C1), (27 * C1 // 2) ** -0.5, 0.21875)
    first_reduce_kernel = bell_draw(streams_of[4], (8, C1, C2), (2 * C1) ** -0.5, 0.5)
    conv_two = bell_draw(streams_of[5], (27, C2, C2), (9 * C2) ** -0.5, 0.1875)
    second_reduce_kernel = bell_draw(streams_of[6], (8, C2, C3), (2 * C2) ** -0.5, 0.375)
    conv_three = bell_draw(streams_of[7], (27, C3, C3), (9 * C3) ** -0.5, 0.125)
    return {"features": features, "neighbours": neighbours, "occupancy": occupancy, "conv_one": conv_one, "first_reduce_kernel": first_reduce_kernel, "conv_two": conv_two, "second_reduce_kernel": second_reduce_kernel, "conv_three": conv_three}


def unpack_bits(packed, voxel_count):
    shifts = jnp.arange(32, dtype=jnp.int32)
    bits = jnp.bitwise_and(jnp.right_shift(packed[:, :, None], shifts), 1)
    return bits.reshape(packed.shape[0], voxel_count).astype(jnp.float32)


def pool_mask(occupied_voxel_mask, brick_extent):
    count = occupied_voxel_mask.shape[0]
    half = brick_extent // 2
    blocks = occupied_voxel_mask.reshape(count, half, 2, half, 2, half, 2)
    blocks = blocks.transpose(0, 1, 3, 5, 2, 4, 6).reshape(count, half * half * half, 8)
    return jnp.max(blocks, axis=-1)


def reduce_resolution(feature_volume, kernel_weight, occupied_voxel_mask, brick_extent):
    count, voxels, chans = feature_volume.shape
    half = brick_extent // 2
    stacked = feature_volume.reshape(count, half, 2, half, 2, half, 2, chans)
    stacked = stacked.transpose(0, 1, 3, 5, 2, 4, 6, 7).reshape(count * voxels // 8, 8 * chans)
    summed = jnp.dot(stacked, kernel_weight.reshape(8 * chans, kernel_weight.shape[2]), preferred_element_type=jnp.float32)
    result = jnp.maximum(summed, 0.0) * occupied_voxel_mask.reshape(-1, 1)
    return result.astype(jnp.bfloat16).reshape(count, voxels // 8, kernel_weight.shape[2])


def pad_bricks(gathered, brick_extent):
    count, chans = gathered.shape[0], gathered.shape[-1]
    table = ((brick_extent - 1, 1, 0), (0, brick_extent, 1), (0, 1, brick_extent + 1))
    padded = jnp.zeros((count, brick_extent + 2, brick_extent + 2, brick_extent + 2, chans), gathered.dtype)
    for first in range(3):
        for second in range(3):
            for third in range(3):
                tap = first * 9 + second * 3 + third
                src_a, len_a, dst_a = table[first]
                src_b, len_b, dst_b = table[second]
                src_c, len_c, dst_c = table[third]
                piece = gathered[:, tap, src_a:src_a + len_a, src_b:src_b + len_b, src_c:src_c + len_c, :]
                padded = padded.at[:, dst_a:dst_a + len_a, dst_b:dst_b + len_b, dst_c:dst_c + len_c, :].set(piece)
    return padded


def convolve_block(extended, sources, occupied_voxel_mask, kernel_weight, brick_extent):
    count = sources.shape[0]
    chans = extended.shape[-1]
    gathered = extended[sources].reshape(count, 27, brick_extent, brick_extent, brick_extent, chans)
    padded = pad_bricks(gathered, brick_extent)
    windows = []
    for first in range(3):
        for second in range(3):
            for third in range(3):
                windows.append(padded[:, first:first + brick_extent, second:second + brick_extent, third:third + brick_extent, :])
    columns = jnp.concatenate(windows, axis=-1).reshape(count * brick_extent ** 3, 27 * chans)
    summed = jnp.dot(columns, kernel_weight.reshape(27 * chans, kernel_weight.shape[2]), preferred_element_type=jnp.float32)
    result = jnp.maximum(summed, 0.0) * occupied_voxel_mask.reshape(-1, 1)
    return result.astype(jnp.bfloat16).reshape(count, brick_extent ** 3, kernel_weight.shape[2])


def run_level(feature_volume, neighbours, occupied_voxel_mask, kernel_weight, brick_extent):
    total, voxels, chans = feature_volume.shape
    extended = jnp.concatenate([feature_volume, jnp.zeros((1, voxels, chans), feature_volume.dtype)], axis=0)
    sources = jnp.where(neighbours < 0, total, neighbours).astype(jnp.int32)
    groups = total // SLICE_BRICKS

    def one_block(pair):
        return convolve_block(extended, pair[0], pair[1], kernel_weight, brick_extent)

    blocks = (sources.reshape(groups, SLICE_BRICKS, 27), occupied_voxel_mask.reshape(groups, SLICE_BRICKS, voxels))
    return lax.map(one_block, blocks).reshape(total, voxels, kernel_weight.shape[2])


def reference(features, neighbours, occupancy, conv_one, first_reduce_kernel, conv_two, second_reduce_kernel, conv_three):
    mask_one = unpack_bits(occupancy, BRICK_EDGE_VOXELS ** 3)
    second_level_mask = pool_mask(mask_one, BRICK_EDGE_VOXELS)
    third_level_mask = pool_mask(second_level_mask, BRICK_EDGE_VOXELS // 2)
    input_one = (features.astype(jnp.float32) * mask_one[:, :, None]).astype(jnp.bfloat16)
    first_level_features = run_level(input_one, neighbours, mask_one, conv_one, BRICK_EDGE_VOXELS)
    second_level_input = reduce_resolution(first_level_features, first_reduce_kernel, second_level_mask, BRICK_EDGE_VOXELS)
    second_level_features = run_level(second_level_input, neighbours, second_level_mask, conv_two, BRICK_EDGE_VOXELS // 2)
    third_level_input = reduce_resolution(second_level_features, second_reduce_kernel, third_level_mask, BRICK_EDGE_VOXELS // 2)
    skip_three = run_level(third_level_input, neighbours, third_level_mask, conv_three, BRICK_EDGE_VOXELS // 4)
    return first_level_features, second_level_features, skip_three
```

```python
import jax
import jax.numpy as jnp
import numpy as np
from jax import lax
from jax.experimental import pallas as pl
from jax.experimental.pallas import tpu as pltpu
from jax.sharding import PartitionSpec as P

F32 = jnp.float32
BF16 = jnp.bfloat16
TAPS = [(a, c, e) for a in range(3) for c in range(3) for e in range(3)]


def dot(x, y):
    return jnp.dot(x, y, preferred_element_type=F32)


def iota(shape, axis):
    return lax.broadcasted_iota(jnp.int32, shape, axis)


def slot_of(neighbours, first, count, b, tap):
    number = neighbours[b, tap]
    shift = (1 - tap // 9) * count
    return jnp.where(number < 0, count, number - first[0] + shift)


def bits_of(words, shift):
    return jnp.bitwise_and(lax.shift_right_logical(words, shift), 1).astype(F32)


def column_mask(occupancy, b, column):
    lane = iota((1, 128), 1)
    w = [jnp.full((1, 128), occupancy[b, 4 * column + q], jnp.int32) for q in range(4)]
    words = jnp.where(
        lane < 64, jnp.where(lane < 32, w[0], w[1]), jnp.where(lane < 96, w[2], w[3])
    )
    return bits_of(words, jnp.bitwise_and(lane, 31))


def spread_pairs(word):
    word = jnp.bitwise_or(word, lax.shift_right_logical(word, 1))
    return jnp.bitwise_or(word, lax.shift_right_logical(word, 8))


def mask_two_word(occupancy, b, i, half):
    return spread_pairs(
        jnp.bitwise_or(occupancy[b, 4 * i + half], occupancy[b, 4 * i + 2 + half])
    )


def mask_two_tile(occupancy, b, i):
    row = iota((8, 128), 0)
    shift = 16 * (row // 4) + 2 * (row % 4)
    return jnp.concatenate(
        [
            bits_of(jnp.full((8, 128), mask_two_word(occupancy, b, i, half), jnp.int32), shift)
            for half in range(2)
        ],
        axis=0,
    )


def mask_three_tile(occupancy, b):
    row = iota((8, 128), 0)
    tile = jnp.zeros((8, 128), jnp.int32)
    for i in range(2):
        for j in range(2):
            word = jnp.bitwise_or(
                mask_two_word(occupancy, b, 2 * i, j), mask_two_word(occupancy, b, 2 * i + 1, j)
            )
            word = jnp.bitwise_or(word, lax.shift_right_logical(word, 16))
            word = jnp.bitwise_or(word, lax.shift_right_logical(word, 2))
            tile = jnp.where(row // 2 == 2 * i + j, word, tile)
    return bits_of(tile, 4 * (row % 2))


def faces_kernel(odd, occupancy, first_columns, last_columns, to_a, to_b):
    count = first_columns.shape[0]
    lane = iota((64, 128), 1)
    is_odd = odd[0] == 1
    for q in range(count // 2):
        low, high = [], []
        for b in (2 * q, 2 * q + 1):
            low.append(first_columns[b].astype(F32) * column_mask(occupancy, b, 0))
            high.append(last_columns[b].astype(F32) * column_mask(occupancy, b, 3))
        lows = jnp.where(lane < 64, low[0], pltpu.roll(low[1], 64, 1))
        highs = jnp.where(lane < 64, pltpu.roll(high[0], 64, 1), high[1])
        to_a[q] = jnp.where(is_odd, lows, highs).astype(BF16)
        to_b[q] = jnp.where(is_odd, highs, lows).astype(BF16)


def level_one_kernel(
    odd, first, neighbours, occupancy, features, from_a, from_b, kernel, reduce,
    out, second, to_a, to_b,
    pairs, wrap, halo, padded, taps, low_sums, high_sums,
):
    count = features.shape[0]
    lane = iota((64, 128), 1)
    small = iota((8, 128), 1)
    row = iota((8, 128), 0)
    is_odd = odd[0] == 1

    for c in range(3):
        for e in range(3):
            w = [kernel[9 * a + 3 * c + e].astype(F32) for a in range(3)]
            none = jnp.zeros((64, 64), F32)
            for p in range(4):
                left = w[p] if p < 3 else none
                right = w[p - 1] if p > 0 else none
                block = jnp.concatenate([left, right], axis=1).astype(BF16)
                taps[(3 * c + e) * 256 + p * 64 : (3 * c + e) * 256 + (p + 1) * 64, :] = block

    for table in (pairs.at[0], pairs.at[1], pairs.at[2], wrap, halo):
        table[count] = jnp.zeros((64, 128), F32)
    for b in range(count):
        cols = [
            features[b, :, 128 * q : 128 * (q + 1)].astype(F32) * column_mask(occupancy, b, q)
            for q in range(4)
        ]
        rolled = [pltpu.roll(col, 64, 1) for col in cols]
        m = jnp.concatenate(
            [
                jnp.where(lane < 64, rolled[0], cols[1]),
                jnp.where(lane < 64, cols[1], rolled[2]),
            ],
            axis=0,
        ).T
        pairs[0, b] = m[:64]
        pairs[1, b] = m[64:]
        m = jnp.concatenate(
            [
                jnp.where(lane < 64, rolled[2], cols[3]),
                jnp.where(lane < 64, cols[3], rolled[0]),
            ],
            axis=0,
        ).T
        pairs[2, b] = m[:64]
        wrap[b] = m[64:]
    for q in range(count // 2):
        one, two = from_a[q].astype(F32), from_b[q].astype(F32)
        m = jnp.concatenate(
            [jnp.where(is_odd, one, two), jnp.where(is_odd, two, one)], axis=0
        ).T
        halo[2 * q] = m[:64]
        halo[2 * q + 1] = m[64:]

    weights = jnp.concatenate(
        [
            jnp.concatenate(
                [
                    jnp.concatenate([reduce[4 * ci + 2 * cj], reduce[4 * ci + 2 * cj + 1]], axis=1)
                    for ci in range(2)
                ],
                axis=0,
            )
            for cj in range(2)
        ],
        axis=0,
    )

    def brick(b, carry):
        slot = [slot_of(neighbours, first, count, b, tap) for tap in range(27)]

        def source(pair, j, e):
            c, j = (0, 7) if j < 0 else (2, 0) if j > 7 else (1, j)
            rows = pl.ds(8 * j, 8)
            own = slot[9 + 3 * c + e]
            if pair == 0:
                return jnp.where(
                    small < 64, halo[slot[3 * c + e], rows, :], wrap[own, rows, :]
                )
            if pair == 4:
                return jnp.where(
                    small < 64, wrap[own, rows, :], halo[slot[18 + 3 * c + e], rows, :]
                )
            return pairs[pair - 1, own, rows, :]

        for pair in range(5):
            shifted = []
            for j in range(-1, 9):
                left, mid, right = [source(pair, j, e) for e in range(3)]
                shifted.append(
                    (
                        pltpu.roll(jnp.where(row == 7, left, mid), 1, 0),
                        mid,
                        pltpu.roll(jnp.where(row == 0, right, mid), 7, 0),
                    )
                )
            for jr in range(6):
                for e in range(3):
                    padded[e, pair, jr] = jnp.concatenate(
                        [shifted[jr][e], shifted[jr + 4][e]], axis=0
                    ).astype(BF16)

        columns = []
        for c in range(3):
            for e in range(3):
                for p in range(2):
                    columns.append(padded[e, p : p + 4, c : c + 4].reshape(256, 128))
        total = dot(jnp.concatenate(columns, axis=1), taps[...])

        tiles = {}
        for i in range(4):
            for jr in range(4):
                for half in range(2):
                    at = (i * 4 + jr) * 16 + half * 8
                    words = jnp.where(
                        small < 64, occupancy[b, 4 * i + half], occupancy[b, 4 * i + 2 + half]
                    )
                    tiles[i, 4 * half + jr] = jnp.maximum(total[at : at + 8], 0.0) * bits_of(
                        words, row + 8 * jr
                    )
        for i in (0, 2):
            m = jnp.concatenate(
                [tiles[i + q, j] for q in range(2) for j in range(8)], axis=0
            ).T
            top, bottom = m[:64], m[64:]
            out[b, :, 128 * i : 128 * (i + 1)] = jnp.where(
                lane < 64, top, pltpu.roll(bottom, 64, 1)
            ).astype(BF16)
            out[b, :, 128 * (i + 1) : 128 * (i + 2)] = jnp.where(
                lane < 64, pltpu.roll(top, 64, 1), bottom
            ).astype(BF16)

        left = jnp.concatenate(
            [
                jnp.concatenate(
                    [
                        jnp.concatenate([tiles[i, j], tiles[i, j + 1]], axis=1)
                        for j in (0, 2, 4, 6)
                    ],
                    axis=0,
                )
                for i in range(4)
            ],
            axis=0,
        ).astype(BF16)
        sums = dot(left, weights)
        low_sums[...] = sums[:, :128]
        high_sums[...] = sums[:, 128:]
        planes = []
        for i in range(4):
            plane = (
                low_sums[pl.ds(32 * i, 16, stride=2), :]
                + high_sums[pl.ds(32 * i + 1, 16, stride=2), :]
            )
            plane = (jnp.maximum(plane, 0.0) * mask_two_tile(occupancy, b, i)).astype(BF16)
            second[b, i] = plane
            planes.append(plane)
        to_a[b] = jnp.where(is_odd, planes[0], planes[3])
        to_b[b] = jnp.where(is_odd, planes[3], planes[0])
        return carry

    lax.fori_loop(0, count, brick, 0)


def level_two_kernel(
    odd, first, neighbours, occupancy, shifts, children, inputs, from_a, from_b, kernel, reduce,
    out, third,
    table, low, high, windows,
):
    count = inputs.shape[0]
    is_odd = odd[0] == 1
    for i in range(4):
        table[count, i] = jnp.zeros((16, 128), BF16)
    low[count] = jnp.zeros((16, 128), BF16)
    high[count] = jnp.zeros((16, 128), BF16)
    for b in range(count):
        table[b] = inputs[b]
        low[b] = jnp.where(is_odd, from_a[b], from_b[b])
        high[b] = jnp.where(is_odd, from_b[b], from_a[b])

    for b in range(count):
        slot = [slot_of(neighbours, first, count, b, tap) for tap in range(27)]
        planes = [jnp.concatenate([low[slot[q]] for q in range(9)], axis=0)]
        for i in range(4):
            planes.append(jnp.concatenate([table[slot[9 + q], i] for q in range(9)], axis=0))
        planes.append(jnp.concatenate([high[slot[18 + q]] for q in range(9)], axis=0))
        moved = dot(shifts[...], jnp.concatenate(planes, axis=1)).astype(BF16)
        for q in range(9):
            for i in range(6):
                windows[q, b, i] = moved[16 * q : 16 * (q + 1), 128 * i : 128 * (i + 1)]

    total = dot(
        jnp.concatenate(
            [
                windows[3 * c + e, :, a : a + 4].reshape(count * 64, 128)
                for a, c, e in TAPS
            ],
            axis=1,
        ),
        kernel[...].reshape(27 * 128, 128),
    )
    bricks = []
    for b in range(count):
        mask = jnp.concatenate([mask_two_tile(occupancy, b, i) for i in range(4)], axis=0)
        brick = (jnp.maximum(total[64 * b : 64 * (b + 1)], 0.0) * mask).astype(BF16)
        out[b] = brick
        bricks.append(brick)
    moved = dot(children[...], jnp.concatenate(bricks, axis=1))
    left = jnp.concatenate(
        [
            jnp.concatenate(
                [moved[8 * q : 8 * (q + 1), 128 * b : 128 * (b + 1)] for b in range(count)], axis=0
            )
            for q in range(8)
        ],
        axis=1,
    ).astype(BF16)
    sums = jnp.maximum(dot(left, reduce[...].reshape(8 * 128, 256)), 0.0)
    for b in range(count):
        mask = mask_three_tile(occupancy, b)
        mask = jnp.concatenate([mask, mask], axis=1)
        third[b] = (sums[8 * b : 8 * (b + 1)] * mask).astype(BF16)


def level_three_kernel(
    odd, first, neighbours, occupancy, shifts, inputs, from_a, from_b, kernel,
    out,
    table,
):
    count = inputs.shape[0]
    is_odd = odd[0] == 1
    for a in range(3):
        table[a, count] = jnp.zeros((8, 256), F32)
    for b in range(count):
        one, two = from_a[b].astype(F32), from_b[b].astype(F32)
        table[0, b] = jnp.where(is_odd, one, two)
        table[1, b] = inputs[b].astype(F32)
        table[2, b] = jnp.where(is_odd, two, one)
    bricks = []
    for b in range(count):
        bricks.append(
            jnp.concatenate(
                [
                    table[tap // 9, slot_of(neighbours, first, count, b, tap)]
                    for tap in range(27)
                ],
                axis=0,
            ).astype(BF16)
        )
    moved = dot(shifts[...], jnp.concatenate(bricks, axis=1))
    left = jnp.concatenate(
        [
            jnp.concatenate(
                [moved[8 * q : 8 * (q + 1), 256 * b : 256 * (b + 1)] for b in range(count)], axis=0
            )
            for q in range(27)
        ],
        axis=1,
    ).astype(BF16)
    sums = jnp.maximum(dot(left, kernel[...].reshape(27 * 256, 256)), 0.0)
    for b in range(count):
        mask = mask_three_tile(occupancy, b)
        mask = jnp.concatenate([mask, mask], axis=1)
        out[b] = (sums[8 * b : 8 * (b + 1)] * mask).astype(BF16)


def plane_shifts():
    pick = np.zeros((144, 144), np.float32)
    for c in range(3):
        for e in range(3):
            for j in range(4):
                for k in range(4):
                    y, z = j + c - 1, k + e - 1
                    brick = 3 * (y // 4 + 1) + z // 4 + 1
                    pick[(3 * c + e) * 16 + 4 * j + k, brick * 16 + 4 * (y % 4) + z % 4] = 1
    return jnp.asarray(pick, BF16)


def child_rows():
    pick = np.zeros((64, 64), np.float32)
    for q in range(8):
        for u in range(8):
            x, y, z = [2 * ((u >> s) & 1) + ((q >> s) & 1) for s in (2, 1, 0)]
            pick[8 * q + u, 16 * x + 4 * y + z] = 1
    return jnp.asarray(pick, BF16)


def brick_shifts():
    pick = np.zeros((216, 216), np.float32)
    for tap, (a, c, e) in enumerate(TAPS):
        for u in range(8):
            x, y, z = (u >> 2) + a - 1, ((u >> 1) & 1) + c - 1, (u & 1) + e - 1
            brick = 9 * (x // 2 + 1) + 3 * (y // 2 + 1) + z // 2 + 1
            pick[8 * tap + u, 8 * brick + 4 * (x % 2) + 2 * (y % 2) + z % 2] = 1
    return jnp.asarray(pick, BF16)


SMEM = pl.BlockSpec(memory_space=pltpu.SMEM)
VMEM = pl.BlockSpec(memory_space=pltpu.VMEM)
PARAMS = pltpu.CompilerParams(vmem_limit_bytes=48 * 1024 * 1024)


def swaps(tiles, count):
    inner, outer = [], []
    for t in range(tiles):
        for m in range(count):
            if m ^ 1 < count:
                inner.append((t * count + m, t * count + (m ^ 1)))
            other = ((m - 1) ^ 1) + 1 if m else -1
            if 0 <= other < count:
                outer.append((t * count + m, t * count + other))
            elif t ^ 1 < tiles:
                outer.append((t * count + m, (t ^ 1) * count + m))
    return inner, outer


def on_device(
    features,
    neighbours,
    occupancy,
    conv_one,
    first_reduce_kernel,
    conv_two,
    second_reduce_kernel,
    conv_three,
):
    axes = ("tiles", "morton")
    inner, outer = swaps(lax.axis_size("tiles"), lax.axis_size("morton"))
    count = features.shape[0]
    place = lax.axis_index("morton")
    odd = jnp.reshape(place % 2, (1,)).astype(jnp.int32)
    first = jnp.reshape(place * count, (1,)).astype(jnp.int32)
    features = jnp.swapaxes(features, 1, 2)

    def exchange(to_a, to_b):
        from_b = lax.ppermute(to_b, axes, outer)
        return lax.ppermute(to_a, axes, inner), from_b

    face = jax.ShapeDtypeStruct((count // 2, 64, 128), BF16)
    edge = pl.BlockSpec((count, 64, 128), lambda i: (0, 0, 0))
    to_a, to_b = pl.pallas_call(
        faces_kernel,
        grid=(1,),
        out_shape=(face, face),
        in_specs=[SMEM, SMEM, edge, pl.BlockSpec((count, 64, 128), lambda i: (0, 0, 3))],
        out_specs=(pl.BlockSpec((count // 2, 64, 128), lambda i: (0, 0, 0)),) * 2,
        compiler_params=PARAMS,
    )(odd, occupancy, features, features)
    from_a, from_b = exchange(to_a, to_b)

    plane = jax.ShapeDtypeStruct((count, 16, 128), BF16)
    first_level, second_input, to_a, to_b = pl.pallas_call(
        level_one_kernel,
        out_shape=(
            jax.ShapeDtypeStruct((count, 64, 512), BF16),
            jax.ShapeDtypeStruct((count, 4, 16, 128), BF16),
            plane,
            plane,
        ),
        in_specs=[SMEM] * 4 + [VMEM] * 5,
        out_specs=(VMEM,) * 4,
        scratch_shapes=[
            pltpu.VMEM((3, count + 1, 64, 128), F32),
            pltpu.VMEM((count + 1, 64, 128), F32),
            pltpu.VMEM((count + 1, 64, 128), F32),
            pltpu.VMEM((3, 5, 6, 16, 128), BF16),
            pltpu.VMEM((9 * 256, 128), BF16),
            pltpu.VMEM((128, 128), F32),
            pltpu.VMEM((128, 128), F32),
        ],
        compiler_params=PARAMS,
    )(
        odd, first, neighbours, occupancy, features, from_a, from_b, conv_one,
        first_reduce_kernel,
    )
    from_a, from_b = exchange(to_a, to_b)

    second_level, third_input = pl.pallas_call(
        level_two_kernel,
        out_shape=(
            jax.ShapeDtypeStruct((count, 64, 128), BF16),
            jax.ShapeDtypeStruct((count, 8, 256), BF16),
        ),
        in_specs=[SMEM] * 4 + [VMEM] * 7,
        out_specs=(VMEM,) * 2,
        scratch_shapes=[
            pltpu.VMEM((count + 1, 4, 16, 128), BF16),
            pltpu.VMEM((count + 1, 16, 128), BF16),
            pltpu.VMEM((count + 1, 16, 128), BF16),
            pltpu.VMEM((9, count, 6, 16, 128), BF16),
        ],
        compiler_params=PARAMS,
    )(
        odd, first, neighbours, occupancy, plane_shifts(), child_rows(), second_input,
        from_a, from_b, conv_two, second_reduce_kernel,
    )
    from_a, from_b = exchange(third_input, third_input)

    third_level = pl.pallas_call(
        level_three_kernel,
        out_shape=jax.ShapeDtypeStruct((count, 8, 256), BF16),
        in_specs=[SMEM] * 4 + [VMEM] * 5,
        out_specs=VMEM,
        scratch_shapes=[pltpu.VMEM((3, count + 1, 8, 256), F32)],
        compiler_params=PARAMS,
    )(
        odd, first, neighbours, occupancy, brick_shifts(), third_input, from_a, from_b,
        conv_three,
    )
    return jnp.swapaxes(first_level, 1, 2), second_level, third_level


def solution(mesh):
    split = P(("tiles", "morton"))
    return jax.shard_map(
        on_device,
        mesh=mesh,
        in_specs=(split, split, split, P(), P(), P(), P(), P()),
        out_specs=(split, split, split),
        check_vma=False,
    )
```

```python
import jax
import jax.numpy as jnp
import numpy as np
from jax import lax
from jax.experimental import pallas as pl
from jax.experimental.pallas import tpu as pltpu
from jax.sharding import PartitionSpec as P

F32 = jnp.float32
BF16 = jnp.bfloat16
TAPS = [(a, c, e) for a in range(3) for c in range(3) for e in range(3)]


def dot(x, y):
    return jnp.dot(x, y, preferred_element_type=F32)


def iota(shape, axis):
    return lax.broadcasted_iota(jnp.int32, shape, axis)


def slot_of(neighbours, first, count, b, tap):
    number = neighbours[b, tap]
    shift = (1 - tap // 9) * count
    return jnp.where(number < 0, count, number - first[0] + shift)


def bits_of(words, shift):
    return jnp.bitwise_and(lax.shift_right_logical(words, shift), 1).astype(F32)


def column_mask(occupancy, b, column):
    lane = iota((1, 128), 1)
    w = [jnp.full((1, 128), occupancy[b, 4 * column + q], jnp.int32) for q in range(4)]
    words = jnp.where(
        lane < 64, jnp.where(lane < 32, w[0], w[1]), jnp.where(lane < 96, w[2], w[3])
    )
    return bits_of(words, jnp.bitwise_and(lane, 31))


def spread_pairs(word):
    word = jnp.bitwise_or(word, lax.shift_right_logical(word, 1))
    return jnp.bitwise_or(word, lax.shift_right_logical(word, 8))


def mask_two_word(occupancy, b, i, half):
    return spread_pairs(
        jnp.bitwise_or(occupancy[b, 4 * i + half], occupancy[b, 4 * i + 2 + half])
    )


def mask_two_tile(occupancy, b, i):
    row = iota((8, 128), 0)
    shift = 16 * (row // 4) + 2 * (row % 4)
    return jnp.concatenate(
        [
            bits_of(jnp.full((8, 128), mask_two_word(occupancy, b, i, half), jnp.int32), shift)
            for half in range(2)
        ],
        axis=0,
    )


def mask_three_tile(occupancy, b):
    row = iota((8, 128), 0)
    tile = jnp.zeros((8, 128), jnp.int32)
    for i in range(2):
        for j in range(2):
            word = jnp.bitwise_or(
                mask_two_word(occupancy, b, 2 * i, j), mask_two_word(occupancy, b, 2 * i + 1, j)
            )
            word = jnp.bitwise_or(word, lax.shift_right_logical(word, 16))
            word = jnp.bitwise_or(word, lax.shift_right_logical(word, 2))
            tile = jnp.where(row // 2 == 2 * i + j, word, tile)
    return bits_of(tile, 4 * (row % 2))


def faces_kernel(odd, occupancy, first_columns, last_columns, to_a, to_b):
    count = first_columns.shape[0]
    lane = iota((64, 128), 1)
    is_odd = odd[0] == 1
    for q in range(count // 2):
        low, high = [], []
        for b in (2 * q, 2 * q + 1):
            low.append(first_columns[b].astype(F32) * column_mask(occupancy, b, 0))
            high.append(last_columns[b].astype(F32) * column_mask(occupancy, b, 3))
        lows = jnp.where(lane < 64, low[0], pltpu.roll(low[1], 64, 1))
        highs = jnp.where(lane < 64, pltpu.roll(high[0], 64, 1), high[1])
        to_a[q] = jnp.where(is_odd, lows, highs).astype(BF16)
        to_b[q] = jnp.where(is_odd, highs, lows).astype(BF16)


def level_one_kernel(
    odd, first, neighbours, occupancy, features, from_a, from_b, kernel, reduce,
    out, second, to_a, to_b,
    pairs, wrap, halo, padded, taps, low_sums, high_sums,
):
    count = features.shape[0]
    lane = iota((64, 128), 1)
    small = iota((8, 128), 1)
    row = iota((8, 128), 0)
    is_odd = odd[0] == 1

    for c in range(3):
        for e in range(3):
            w = [kernel[9 * a + 3 * c + e].astype(F32) for a in range(3)]
            none = jnp.zeros((64, 64), F32)
            for p in range(4):
                left = w[p] if p < 3 else none
                right = w[p - 1] if p > 0 else none
                block = jnp.concatenate([left, right], axis=1).astype(BF16)
                taps[(3 * c + e) * 256 + p * 64 : (3 * c + e) * 256 + (p + 1) * 64, :] = block

    for table in (pairs.at[0], pairs.at[1], pairs.at[2], wrap, halo):
        table[count] = jnp.zeros((64, 128), F32)
    for b in range(count):
        cols = [
            features[b, :, 128 * q : 128 * (q + 1)].astype(F32) * column_mask(occupancy, b, q)
            for q in range(4)
        ]
        rolled = [pltpu.roll(col, 64, 1) for col in cols]
        m = jnp.concatenate(
            [
                jnp.where(lane < 64, rolled[0], cols[1]),
                jnp.where(lane < 64, cols[1], rolled[2]),
            ],
            axis=0,
        ).T
        pairs[0, b] = m[:64]
        pairs[1, b] = m[64:]
        m = jnp.concatenate(
            [
                jnp.where(lane < 64, rolled[2], cols[3]),
                jnp.where(lane < 64, cols[3], rolled[0]),
            ],
            axis=0,
        ).T
        pairs[2, b] = m[:64]
        wrap[b] = m[64:]
    for q in range(count // 2):
        one, two = from_a[q].astype(F32), from_b[q].astype(F32)
        m = jnp.concatenate(
            [jnp.where(is_odd, one, two), jnp.where(is_odd, two, one)], axis=0
        ).T
        halo[2 * q] = m[:64]
        halo[2 * q + 1] = m[64:]

    weights = jnp.concatenate(
        [
            jnp.concatenate(
                [
                    jnp.concatenate([reduce[4 * ci + 2 * cj], reduce[4 * ci + 2 * cj + 1]], axis=1)
                    for ci in range(2)
                ],
                axis=0,
            )
            for cj in range(2)
        ],
        axis=0,
    )

    def brick(b, carry):
        slot = [slot_of(neighbours, first, count, b, tap) for tap in range(27)]

        def source(pair, j, e):
            c, j = (0, 7) if j < 0 else (2, 0) if j > 7 else (1, j)
            rows = pl.ds(8 * j, 8)
            own = slot[9 + 3 * c + e]
            if pair == 0:
                return jnp.where(
                    small < 64, halo[slot[3 * c + e], rows, :], wrap[own, rows, :]
                )
            if pair == 4:
                return jnp.where(
                    small < 64, wrap[own, rows, :], halo[slot[18 + 3 * c + e], rows, :]
                )
            return pairs[pair - 1, own, rows, :]

        for pair in range(5):
            shifted = []
            for j in range(-1, 9):
                left, mid, right = [source(pair, j, e) for e in range(3)]
                shifted.append(
                    (
                        pltpu.roll(jnp.where(row == 7, left, mid), 1, 0),
                        mid,
                        pltpu.roll(jnp.where(row == 0, right, mid), 7, 0),
                    )
                )
            for jr in range(6):
                for e in range(3):
                    padded[e, pair, jr] = jnp.concatenate(
                        [shifted[jr][e], shifted[jr + 4][e]], axis=0
                    ).astype(BF16)

        columns = []
        for c in range(3):
            for e in range(3):
                for p in range(2):
                    columns.append(padded[e, p : p + 4, c : c + 4].reshape(256, 128))
        total = dot(jnp.concatenate(columns, axis=1), taps[...])

        tiles = {}
        for i in range(4):
            for jr in range(4):
                for half in range(2):
                    at = (i * 4 + jr) * 16 + half * 8
                    words = jnp.where(
                        small < 64, occupancy[b, 4 * i + half], occupancy[b, 4 * i + 2 + half]
                    )
                    tiles[i, 4 * half + jr] = jnp.maximum(total[at : at + 8], 0.0) * bits_of(
                        words, row + 8 * jr
                    )
        for i in (0, 2):
            m = jnp.concatenate(
                [tiles[i + q, j] for q in range(2) for j in range(8)], axis=0
            ).T
            top, bottom = m[:64], m[64:]
            out[b, :, 128 * i : 128 * (i + 1)] = jnp.where(
                lane < 64, top, pltpu.roll(bottom, 64, 1)
            ).astype(BF16)
            out[b, :, 128 * (i + 1) : 128 * (i + 2)] = jnp.where(
                lane < 64, pltpu.roll(top, 64, 1), bottom
            ).astype(BF16)

        left = jnp.concatenate(
            [
                jnp.concatenate(
                    [
                        jnp.concatenate([tiles[i, j], tiles[i, j + 1]], axis=1)
                        for j in (0, 2, 4, 6)
                    ],
                    axis=0,
                )
                for i in range(4)
            ],
            axis=0,
        ).astype(BF16)
        sums = dot(left, weights)
        low_sums[...] = sums[:, :128]
        high_sums[...] = sums[:, 128:]
        planes = []
        for i in range(4):
            plane = (
                low_sums[pl.ds(32 * i, 16, stride=2), :]
                + high_sums[pl.ds(32 * i + 1, 16, stride=2), :]
            )
            plane = (jnp.maximum(plane, 0.0) * mask_two_tile(occupancy, b, i)).astype(BF16)
            second[b, i] = plane
            planes.append(plane)
        to_a[b] = jnp.where(is_odd, planes[0], planes[3])
        to_b[b] = jnp.where(is_odd, planes[3], planes[0])
        return carry

    lax.fori_loop(0, count, brick, 0, unroll=True)


def level_two_kernel(
    odd, first, neighbours, occupancy, shifts, children, inputs, from_a, from_b, kernel, reduce,
    out, third,
    table, low, high, windows,
):
    count = inputs.shape[0]
    is_odd = odd[0] == 1
    for i in range(4):
        table[count, i] = jnp.zeros((16, 128), BF16)
    low[count] = jnp.zeros((16, 128), BF16)
    high[count] = jnp.zeros((16, 128), BF16)
    for b in range(count):
        table[b] = inputs[b]
        low[b] = jnp.where(is_odd, from_a[b], from_b[b])
        high[b] = jnp.where(is_odd, from_b[b], from_a[b])

    for b in range(count):
        slot = [slot_of(neighbours, first, count, b, tap) for tap in range(27)]
        planes = [jnp.concatenate([low[slot[q]] for q in range(9)], axis=0)]
        for i in range(4):
            planes.append(jnp.concatenate([table[slot[9 + q], i] for q in range(9)], axis=0))
        planes.append(jnp.concatenate([high[slot[18 + q]] for q in range(9)], axis=0))
        moved = dot(shifts[...], jnp.concatenate(planes, axis=1)).astype(BF16)
        for q in range(9):
            for i in range(6):
                windows[q, b, i] = moved[16 * q : 16 * (q + 1), 128 * i : 128 * (i + 1)]

    total = dot(
        jnp.concatenate(
            [
                windows[3 * c + e, :, a : a + 4].reshape(count * 64, 128)
                for a, c, e in TAPS
            ],
            axis=1,
        ),
        kernel[...].reshape(27 * 128, 128),
    )
    bricks = []
    for b in range(count):
        mask = jnp.concatenate([mask_two_tile(occupancy, b, i) for i in range(4)], axis=0)
        brick = (jnp.maximum(total[64 * b : 64 * (b + 1)], 0.0) * mask).astype(BF16)
        out[b] = brick
        bricks.append(brick)
    moved = dot(children[...], jnp.concatenate(bricks, axis=1))
    left = jnp.concatenate(
        [
            jnp.concatenate(
                [moved[8 * q : 8 * (q + 1), 128 * b : 128 * (b + 1)] for b in range(count)], axis=0
            )
            for q in range(8)
        ],
        axis=1,
    ).astype(BF16)
    sums = jnp.maximum(dot(left, reduce[...].reshape(8 * 128, 256)), 0.0)
    for b in range(count):
        mask = mask_three_tile(occupancy, b)
        mask = jnp.concatenate([mask, mask], axis=1)
        third[b] = (sums[8 * b : 8 * (b + 1)] * mask).astype(BF16)


def level_three_kernel(
    odd, first, neighbours, occupancy, shifts, inputs, from_a, from_b, kernel,
    out,
    table,
):
    count = inputs.shape[0]
    is_odd = odd[0] == 1
    for a in range(3):
        table[a, count] = jnp.zeros((8, 256), F32)
    for b in range(count):
        one, two = from_a[b].astype(F32), from_b[b].astype(F32)
        table[0, b] = jnp.where(is_odd, one, two)
        table[1, b] = inputs[b].astype(F32)
        table[2, b] = jnp.where(is_odd, two, one)
    bricks = []
    for b in range(count):
        bricks.append(
            jnp.concatenate(
                [
                    table[tap // 9, slot_of(neighbours, first, count, b, tap)]
                    for tap in range(27)
                ],
                axis=0,
            ).astype(BF16)
        )
    moved = dot(shifts[...], jnp.concatenate(bricks, axis=1))
    left = jnp.concatenate(
        [
            jnp.concatenate(
                [moved[8 * q : 8 * (q + 1), 256 * b : 256 * (b + 1)] for b in range(count)], axis=0
            )
            for q in range(27)
        ],
        axis=1,
    ).astype(BF16)
    sums = jnp.maximum(dot(left, kernel[...].reshape(27 * 256, 256)), 0.0)
    for b in range(count):
        mask = mask_three_tile(occupancy, b)
        mask = jnp.concatenate([mask, mask], axis=1)
        out[b] = (sums[8 * b : 8 * (b + 1)] * mask).astype(BF16)


def plane_shifts():
    pick = np.zeros((144, 144), np.float32)
    for c in range(3):
        for e in range(3):
            for j in range(4):
                for k in range(4):
                    y, z = j + c - 1, k + e - 1
                    brick = 3 * (y // 4 + 1) + z // 4 + 1
                    pick[(3 * c + e) * 16 + 4 * j + k, brick * 16 + 4 * (y % 4) + z % 4] = 1
    return jnp.asarray(pick, BF16)


def child_rows():
    pick = np.zeros((64, 64), np.float32)
    for q in range(8):
        for u in range(8):
            x, y, z = [2 * ((u >> s) & 1) + ((q >> s) & 1) for s in (2, 1, 0)]
            pick[8 * q + u, 16 * x + 4 * y + z] = 1
    return jnp.asarray(pick, BF16)


def brick_shifts():
    pick = np.zeros((216, 216), np.float32)
    for tap, (a, c, e) in enumerate(TAPS):
        for u in range(8):
            x, y, z = (u >> 2) + a - 1, ((u >> 1) & 1) + c - 1, (u & 1) + e - 1
            brick = 9 * (x // 2 + 1) + 3 * (y // 2 + 1) + z // 2 + 1
            pick[8 * tap + u, 8 * brick + 4 * (x % 2) + 2 * (y % 2) + z % 2] = 1
    return jnp.asarray(pick, BF16)


SMEM = pl.BlockSpec(memory_space=pltpu.SMEM)
VMEM = pl.BlockSpec(memory_space=pltpu.VMEM)
PARAMS = pltpu.CompilerParams(vmem_limit_bytes=24 * 1024 * 1024)


def swaps(tiles, count):
    inner, outer = [], []
    for t in range(tiles):
        for m in range(count):
            if m ^ 1 < count:
                inner.append((t * count + m, t * count + (m ^ 1)))
            other = ((m - 1) ^ 1) + 1 if m else -1
            if 0 <= other < count:
                outer.append((t * count + m, t * count + other))
            elif t ^ 1 < tiles:
                outer.append((t * count + m, (t ^ 1) * count + m))
    return inner, outer


def on_device(
    features,
    neighbours,
    occupancy,
    conv_one,
    first_reduce_kernel,
    conv_two,
    second_reduce_kernel,
    conv_three,
):
    axes = ("tiles", "morton")
    inner, outer = swaps(lax.axis_size("tiles"), lax.axis_size("morton"))
    count = features.shape[0]
    place = lax.axis_index("morton")
    odd = jnp.reshape(place % 2, (1,)).astype(jnp.int32)
    first = jnp.reshape(place * count, (1,)).astype(jnp.int32)
    features = jnp.swapaxes(features, 1, 2)

    def exchange(to_a, to_b):
        from_b = lax.ppermute(to_b, axes, outer)
        return lax.ppermute(to_a, axes, inner), from_b

    face = jax.ShapeDtypeStruct((count // 2, 64, 128), BF16)
    edge = pl.BlockSpec((count, 64, 128), lambda i: (0, 0, 0))
    to_a, to_b = pl.pallas_call(
        faces_kernel,
        grid=(1,),
        out_shape=(face, face),
        in_specs=[SMEM, SMEM, edge, pl.BlockSpec((count, 64, 128), lambda i: (0, 0, 3))],
        out_specs=(pl.BlockSpec((count // 2, 64, 128), lambda i: (0, 0, 0)),) * 2,
        compiler_params=PARAMS,
        cost_estimate=pl.CostEstimate(flops=4 * 10**9, bytes_accessed=10**7, transcendentals=0),
    )(odd, occupancy, features, features)
    from_a, from_b = exchange(to_a, to_b)

    plane = jax.ShapeDtypeStruct((count, 16, 128), BF16)
    first_level, second_input, to_a, to_b = pl.pallas_call(
        level_one_kernel,
        out_shape=(
            jax.ShapeDtypeStruct((count, 64, 512), BF16),
            jax.ShapeDtypeStruct((count, 4, 16, 128), BF16),
            plane,
            plane,
        ),
        in_specs=[SMEM] * 4 + [VMEM] * 5,
        out_specs=(VMEM,) * 4,
        scratch_shapes=[
            pltpu.VMEM((3, count + 1, 64, 128), F32),
            pltpu.VMEM((count + 1, 64, 128), F32),
            pltpu.VMEM((count + 1, 64, 128), F32),
            pltpu.VMEM((3, 5, 6, 16, 128), BF16),
            pltpu.VMEM((9 * 256, 128), BF16),
            pltpu.VMEM((128, 128), F32),
            pltpu.VMEM((128, 128), F32),
        ],
        compiler_params=PARAMS,
        cost_estimate=pl.CostEstimate(flops=4 * 10**9, bytes_accessed=10**7, transcendentals=0),
    )(
        odd, first, neighbours, occupancy, features, from_a, from_b, conv_one,
        first_reduce_kernel,
    )
    from_a, from_b = exchange(to_a, to_b)

    second_level, third_input = pl.pallas_call(
        level_two_kernel,
        out_shape=(
            jax.ShapeDtypeStruct((count, 64, 128), BF16),
            jax.ShapeDtypeStruct((count, 8, 256), BF16),
        ),
        in_specs=[SMEM] * 4 + [VMEM] * 7,
        out_specs=(VMEM,) * 2,
        scratch_shapes=[
            pltpu.VMEM((count + 1, 4, 16, 128), BF16),
            pltpu.VMEM((count + 1, 16, 128), BF16),
            pltpu.VMEM((count + 1, 16, 128), BF16),
            pltpu.VMEM((9, count, 6, 16, 128), BF16),
        ],
        compiler_params=PARAMS,
        cost_estimate=pl.CostEstimate(flops=4 * 10**9, bytes_accessed=10**7, transcendentals=0),
    )(
        odd, first, neighbours, occupancy, plane_shifts(), child_rows(), second_input,
        from_a, from_b, conv_two, second_reduce_kernel,
    )
    from_a, from_b = exchange(third_input, third_input)

    third_level = pl.pallas_call(
        level_three_kernel,
        out_shape=jax.ShapeDtypeStruct((count, 8, 256), BF16),
        in_specs=[SMEM] * 4 + [VMEM] * 5,
        out_specs=VMEM,
        scratch_shapes=[pltpu.VMEM((3, count + 1, 8, 256), F32)],
        compiler_params=PARAMS,
        cost_estimate=pl.CostEstimate(flops=4 * 10**9, bytes_accessed=10**7, transcendentals=0),
    )(
        odd, first, neighbours, occupancy, brick_shifts(), third_input, from_a, from_b,
        conv_three,
    )
    return jnp.swapaxes(first_level, 1, 2), second_level, third_level


def solution(mesh):
    split = P(("tiles", "morton"))
    return jax.shard_map(
        on_device,
        mesh=mesh,
        in_specs=(split, split, split, P(), P(), P(), P(), P()),
        out_specs=(split, split, split),
        check_vma=False,
    )
```

```python
import jax
import jax.numpy as jnp
import numpy as np
from jax import lax
from jax.experimental import pallas as pl
from jax.experimental.pallas import tpu as pltpu
from jax.sharding import PartitionSpec as P

F32 = jnp.float32
BF16 = jnp.bfloat16
LINE = "morton"
TAPS = [(a, q) for a in range(3) for q in range(9)]


def dot(x, y):
    return jnp.dot(x, y, preferred_element_type=F32)


def iota(shape, axis):
    return lax.broadcasted_iota(jnp.int32, shape, axis)


def stack(parts):
    return jnp.concatenate(parts, axis=0)


def beside(parts):
    return jnp.concatenate(parts, axis=1)


def bits_of(words, shift):
    return jnp.bitwise_and(lax.shift_right_logical(words, shift), 1).astype(F32)


def either(x, y):
    return jnp.bitwise_or(x, y)


def on_odd_place():
    return lax.rem(lax.axis_index(LINE), 2) == 1


def word_lanes(words, w):
    return jnp.broadcast_to(words[:, w : w + 1], (words.shape[0], 128))


def column_bits(words, column):
    lane = iota((words.shape[0], 128), 1)
    w = [word_lanes(words, 4 * column + q) for q in range(4)]
    chosen = jnp.where(
        lane < 64, jnp.where(lane < 32, w[0], w[1]), jnp.where(lane < 96, w[2], w[3])
    )
    return bits_of(chosen, jnp.bitwise_and(lane, 31))


def slots_of(neighbours, first, count, b, tap):
    numbers = [neighbours[b, tap + q] for q in range(9)]
    shift = (1 - tap // 9) * count - first
    return [jnp.where(n < 0, count, n + shift) for n in numbers]


def edges_kernel(features, occupancy, to_a, to_b, columns, words, arrived):
    count = words.shape[0]
    last = features.shape[2] - 128
    copies = [
        pltpu.make_async_copy(occupancy, words, arrived.at[0]),
        pltpu.make_async_copy(features.at[:, :, pl.ds(0, 128)], columns.at[0], arrived.at[1]),
        pltpu.make_async_copy(features.at[:, :, pl.ds(last, 128)], columns.at[1], arrived.at[2]),
    ]
    for copy in copies:
        copy.start()
    for copy in copies:
        copy.wait()
    bits = [column_bits(words[...], 0), column_bits(words[...], last // 128)]
    lane = iota((64, 128), 1)
    odd = on_odd_place()
    for q in range(count // 2):
        low, high = [
            [columns[side, b].astype(F32) * bits[side][b : b + 1] for b in (2 * q, 2 * q + 1)]
            for side in range(2)
        ]
        lows = jnp.where(lane < 64, low[0], pltpu.roll(low[1], 64, 1))
        highs = jnp.where(lane < 64, pltpu.roll(high[0], 64, 1), high[1])
        to_a[q] = jnp.where(odd, lows, highs).astype(BF16)
        to_b[q] = jnp.where(odd, highs, lows).astype(BF16)


def tables_kernel(
    neighbours, occupancy, pick_two, add_two, pick_three, add_three,
    own_two, low_two, high_two, own_three, faces_three, pair_words, mask_two, mask_three,
):
    count = neighbours.shape[0]
    number = neighbours[...]
    tap = iota(number.shape, 1)
    shift = jnp.where(tap < 9, count, jnp.where(tap < 18, 0, -count))
    slot = jnp.where(
        number < 0, 4 * count, number + shift - lax.axis_index(LINE) * count
    ).astype(BF16)
    across = (((1,), (1,)), ((), ()))
    rows = lax.dot_general(pick_two[...], slot, across, preferred_element_type=F32)
    rows = (rows + add_two[...]).astype(jnp.int32)
    lane = iota((16, 16 * count), 1)
    for a, table in enumerate((low_two, own_two, high_two)):
        for q in range(9):
            for b in range(count):
                at = 16 * (9 * a + q)
                table[16 * (count * q + b) : 16 * (count * q + b + 1), :] = jnp.where(
                    rows[at : at + 16, b : b + 1] == lane, 1.0, 0.0
                ).astype(BF16)
    rows = lax.dot_general(pick_three[...], slot, across, preferred_element_type=F32)
    rows = (rows + add_three[...]).astype(jnp.int32)
    for table, begin in ((own_three, 0), (faces_three, 27)):
        lane = iota((8, table.shape[1]), 1)
        for q in range(table.shape[0] // (8 * count)):
            at = 8 * (begin + q)
            table[8 * count * q : 8 * count * (q + 1), :] = stack(
                [
                    jnp.where(rows[at : at + 8, b : b + 1] == lane, 1.0, 0.0)
                    for b in range(count)
                ]
            ).astype(BF16)

    words = [word_lanes(occupancy[...], w) for w in range(16)]
    lane = iota((count, 128), 1)
    row = iota((8, 128), 0)
    any_two = []
    for i in range(4):
        for half in range(2):
            low, high = words[4 * i + half], words[4 * i + 2 + half]
            pair_words[2 * i + half] = jnp.where(lane < 64, low, high)
            word = either(low, high)
            word = either(word, lax.shift_right_logical(word, 1))
            any_two.append(either(word, lax.shift_right_logical(word, 8)))
    two_shift = 16 * lax.shift_right_logical(row, 2) + 2 * jnp.bitwise_and(row, 3)
    for i in range(4):
        for b in range(count):
            mask_two[i, 16 * b : 16 * (b + 1)] = stack(
                [
                    bits_of(
                        jnp.broadcast_to(any_two[2 * i + half][b : b + 1], (8, 128)), two_shift
                    )
                    for half in range(2)
                ]
            )
    any_three = []
    for i in range(2):
        for j in range(2):
            word = either(any_two[4 * i + j], any_two[4 * i + 2 + j])
            word = either(word, lax.shift_right_logical(word, 16))
            any_three.append(either(word, lax.shift_right_logical(word, 2)))
    for b in range(count):
        tile = [jnp.broadcast_to(word[b : b + 1], (8, 128)) for word in any_three]
        tile = jnp.where(
            row < 4, jnp.where(row < 2, tile[0], tile[1]), jnp.where(row < 6, tile[2], tile[3])
        )
        mask = bits_of(tile, 4 * jnp.bitwise_and(row, 1))
        mask_three[8 * b : 8 * (b + 1)] = beside([mask, mask])


def shifted_windows(source, row):
    shifted = []
    for j in range(-1, 9):
        c, at = (0, 7) if j < 0 else (2, 0) if j > 7 else (1, j)
        left, mid, right = [source(3 * c + e, at) for e in range(3)]
        shifted.append(
            (
                pltpu.roll(jnp.where(row == 7, left, mid), 1, 0),
                mid,
                pltpu.roll(jnp.where(row == 0, right, mid), 7, 0),
            )
        )
    return [
        [stack([shifted[jr][e], shifted[jr + 4][e]]).astype(BF16) for e in range(3)]
        for jr in range(6)
    ]


def outer_kernel(
    neighbours, occupancy, features, kernel,
    padded, taps, face_taps, partial,
    pairs, low_edge, high_edge, numbers, arrived,
):
    count = features.shape[0]
    first = lax.axis_index(LINE) * count
    lane = iota((64, 128), 1)
    row = iota((8, 128), 0)
    copy = pltpu.make_async_copy(neighbours, numbers, arrived)
    copy.start()

    none = jnp.zeros((64, 64), F32)
    for q in range(9):
        w = [kernel[9 * a + q].astype(F32) for a in range(3)]
        taps[q * 256 : (q + 1) * 256, :] = stack(
            [beside([w[p] if p < 3 else none, w[p - 1] if p else none]) for p in range(4)]
        ).astype(BF16)
        face_taps[q * 128 : (q + 1) * 128, :] = stack(
            [beside([w[0], none]), beside([none, w[2]])]
        ).astype(BF16)

    for table in (pairs.at[0], pairs.at[1], pairs.at[2], low_edge, high_edge):
        table[count] = jnp.zeros((64, 128), F32)
    bits = [column_bits(occupancy[...], q) for q in range(4)]
    for b in range(count):
        cols = [
            features[b, :, 128 * q : 128 * (q + 1)].astype(F32) * bits[q][b : b + 1]
            for q in range(4)
        ]
        rolled = [pltpu.roll(col, 64, 1) for col in cols]
        m = stack(
            [
                jnp.where(lane < 64, rolled[0], cols[1]),
                jnp.where(lane < 64, cols[1], rolled[2]),
            ]
        ).T
        pairs[0, b] = m[:64]
        pairs[1, b] = m[64:]
        m = stack(
            [
                jnp.where(lane < 64, rolled[2], cols[3]),
                jnp.where(lane < 64, cols[3], rolled[0]),
            ]
        ).T
        pairs[2, b] = m[:64]
        low_edge[b] = jnp.where(lane < 64, 0.0, m[64:])
        high_edge[b] = jnp.where(lane < 64, m[64:], 0.0)

    copy.wait()
    tables = [low_edge, pairs.at[0], pairs.at[1], pairs.at[2], high_edge]
    for b in range(count):
        slot = slots_of(numbers, first, count, b, 9)
        for pair in range(5):
            windows = shifted_windows(
                lambda q, j: tables[pair][slot[q], pl.ds(8 * j, 8), :], row
            )
            for jr in range(6):
                for e in range(3):
                    padded[b, e, pair, jr] = windows[jr][e]

    group = count // 2
    for g in range(2):
        bricks = slice(g * group, (g + 1) * group)
        for side in range(2):
            partial[side, g * group * 64 : (g + 1) * group * 64] = dot(
                beside(
                    [
                        padded[bricks, e, 3 * side + p, c : c + 4].reshape(group * 64, 128)
                        for c in range(3)
                        for e in range(3)
                        for p in range(2)
                    ]
                ),
                taps[...],
            )


def masked_tiles(sums, pair_words, b, i):
    row = iota((8, 128), 0)
    tiles = {}
    for half in range(2):
        words = jnp.broadcast_to(pair_words[2 * i + half, b : b + 1, :], (8, 128))
        for jr in range(4):
            at = jr * 16 + half * 8
            tiles[4 * half + jr] = jnp.maximum(sums[at : at + 8], 0.0) * bits_of(
                words, row + 8 * jr
            )
    return [tiles[j] for j in range(8)]


def reduce_planes(groups, reduce, low_sums, high_sums):
    left = stack(
        [beside([tiles[j], tiles[j + 1]]) for tiles in groups for j in (0, 2, 4, 6)]
    ).astype(BF16)
    weights = stack(
        [
            beside([reduce[4 * ci + 2 * cj], reduce[4 * ci + 2 * cj + 1]])
            for cj in range(2)
            for ci in range(2)
        ]
    )
    sums = dot(left, weights)
    low_sums[...] = sums[:, :128]
    high_sums[...] = sums[:, 128:]
    return [
        low_sums[pl.ds(32 * g, 16, stride=2), :] + high_sums[pl.ds(32 * g + 1, 16, stride=2), :]
        for g in range(len(groups))
    ]


def faces_one_kernel(
    neighbours, from_a, from_b, face_taps, partial, reduce, pair_words, mask_two,
    outer, second, to_a, to_b,
    halo, windows, low_sums, high_sums, numbers, arrived,
):
    count = outer.shape[0]
    first = lax.axis_index(LINE) * count
    lane = iota((64, 128), 1)
    small = iota((8, 128), 1)
    row = iota((8, 128), 0)
    odd = on_odd_place()
    copy = pltpu.make_async_copy(neighbours, numbers, arrived)
    copy.start()
    halo[count] = jnp.zeros((64, 128), F32)
    for q in range(count // 2):
        one, two = from_a[q].astype(F32), from_b[q].astype(F32)
        m = stack([jnp.where(odd, one, two), jnp.where(odd, two, one)]).T
        halo[2 * q] = m[:64]
        halo[2 * q + 1] = m[64:]
    copy.wait()
    for b in range(count):
        low = slots_of(numbers, first, count, b, 0)
        high = slots_of(numbers, first, count, b, 18)

        def source(q, j):
            rows = pl.ds(8 * j, 8)
            return jnp.where(small < 64, halo[low[q], rows, :], halo[high[q], rows, :])

        tiles = shifted_windows(source, row)
        for jr in range(6):
            for e in range(3):
                windows[b, e, jr] = tiles[jr][e]
    added = dot(
        beside(
            [
                windows[:, e, c : c + 4].reshape(count * 64, 128)
                for c in range(3)
                for e in range(3)
            ]
        ),
        face_taps[...],
    )
    groups = []
    for b in range(count):
        at = slice(64 * b, 64 * (b + 1))
        for side in range(2):
            near = (lane < 64) == (side == 0)
            sums = partial[side, at] + jnp.where(near, added[at], 0.0)
            groups.append(masked_tiles(sums, pair_words, b, 3 * side))
            outer[b, side] = stack(groups[-1]).astype(BF16)
    sums = reduce_planes(groups, reduce, low_sums, high_sums)
    for b in range(count):
        at = slice(16 * b, 16 * (b + 1))
        planes = [
            (jnp.maximum(sums[2 * b + side], 0.0) * mask_two[3 * side, at]).astype(BF16)
            for side in range(2)
        ]
        second[0, at] = planes[0]
        second[1, at] = planes[1]
        to_a[at] = jnp.where(odd, planes[0], planes[1])
        to_b[at] = jnp.where(odd, planes[1], planes[0])


def inner_kernel(
    padded, taps, outer, reduce, pair_words, mask_two,
    result, second,
    out, low_sums, high_sums, stored,
):
    count = padded.shape[0]
    lane = iota((64, 128), 1)
    total = dot(
        beside(
            [
                padded[:, e, 1 + p : 3 + p, c : c + 4].reshape(count * 128, 128)
                for c in range(3)
                for e in range(3)
                for p in range(2)
            ]
        ),
        taps[...],
    )
    groups = []
    copies = []
    for b in range(count):
        for i in (1, 2):
            at = 128 * b + 64 * (i - 1)
            groups.append(masked_tiles(total[at : at + 64], pair_words, b, i))
        ordered = [
            outer[b, 0].astype(F32),
            stack(groups[2 * b]),
            stack(groups[2 * b + 1]),
            outer[b, 1].astype(F32),
        ]
        for i in (0, 2):
            m = stack(ordered[i : i + 2]).T
            top, bottom = m[:64], m[64:]
            out[b, :, 128 * i : 128 * (i + 1)] = jnp.where(
                lane < 64, top, pltpu.roll(bottom, 64, 1)
            ).astype(BF16)
            out[b, :, 128 * (i + 1) : 128 * (i + 2)] = jnp.where(
                lane < 64, pltpu.roll(top, 64, 1), bottom
            ).astype(BF16)
        copies.append(pltpu.make_async_copy(out.at[b], result.at[b], stored.at[b]))
        copies[-1].start()
    sums = reduce_planes(groups, reduce, low_sums, high_sums)
    for b in range(count):
        at = slice(16 * b, 16 * (b + 1))
        for i in (1, 2):
            second[i - 1, at] = (
                jnp.maximum(sums[2 * b + i - 1], 0.0) * mask_two[i, at]
            ).astype(BF16)
    for copy in copies:
        copy.wait()


def own_two_kernel(outer, inner, gather, kernel, partial):
    rows = outer.shape[1]
    planes = beside([outer[0], inner[0], inner[1], outer[1]])
    moved = dot(gather[...], planes).astype(BF16)
    none = jnp.zeros((rows, 128), BF16)
    left = beside(
        [
            stack(
                [
                    moved[q * rows : (q + 1) * rows, 128 * (i + a - 1) : 128 * (i + a)]
                    if 0 <= i + a - 1 < 4
                    else none
                    for i in range(4)
                ]
            )
            for a, q in TAPS
        ]
    )
    partial[...] = dot(left, kernel[...].reshape(27 * 128, 128))


def faces_two_kernel(
    low_gather, high_gather, children, partial, from_a, from_b, kernel, reduce,
    mask_two, mask_three,
    second, third,
):
    count = second.shape[0]
    rows = 16 * count
    odd = on_odd_place()
    one, two = from_a[...], from_b[...]
    added = []
    for gather, face, tap in (
        (low_gather, jnp.where(odd, one, two), 0),
        (high_gather, jnp.where(odd, two, one), 18),
    ):
        moved = dot(gather[...], face).astype(BF16)
        left = beside([moved[q * rows : (q + 1) * rows] for q in range(9)])
        added.append(dot(left, kernel[tap : tap + 9].reshape(9 * 128, 128)))
    planes = []
    for i in range(4):
        sums = partial[i * rows : (i + 1) * rows]
        if i == 0:
            sums = sums + added[0]
        if i == 3:
            sums = sums + added[1]
        planes.append((jnp.maximum(sums, 0.0) * mask_two[i]).astype(BF16))
    bricks = [
        stack([planes[i][16 * b : 16 * (b + 1)] for i in range(4)]) for b in range(count)
    ]
    for b in range(count):
        second[b] = bricks[b]
    moved = dot(children[...], beside(bricks))
    left = beside(
        [
            stack([moved[8 * q : 8 * (q + 1), 128 * b : 128 * (b + 1)] for b in range(count)])
            for q in range(8)
        ]
    ).astype(BF16)
    sums = dot(left, reduce[...].reshape(8 * 128, 256))
    third[...] = (jnp.maximum(sums, 0.0) * mask_three[...]).astype(BF16)


def own_three_kernel(gather, third, kernel, second, partial, result, stored):
    copy = pltpu.make_async_copy(second, result, stored)
    copy.start()
    rows = third.shape[0]
    moved = dot(gather[...], third[...]).astype(BF16)
    left = beside([moved[q * rows : (q + 1) * rows] for q in range(27)])
    partial[...] = dot(left, kernel[...].reshape(27 * 256, 256))
    copy.wait()


def faces_three_kernel(gather, partial, from_a, from_b, kernel, mask_three, out):
    rows = partial.shape[0]
    odd = on_odd_place()
    one, two = from_a[...], from_b[...]
    faces = stack([jnp.where(odd, one, two), jnp.where(odd, two, one)])
    moved = dot(gather[...], faces).astype(BF16)
    left = beside([moved[q * rows : (q + 1) * rows] for q in range(18)])
    weights = stack([kernel[:9].reshape(9 * 256, 256), kernel[18:].reshape(9 * 256, 256)])
    sums = partial[...] + dot(left, weights)
    out[...] = (jnp.maximum(sums, 0.0) * mask_three[...]).astype(BF16).reshape(out.shape)


def level_two_rows(count):
    pick = np.zeros((432, 27), np.float32)
    add = np.zeros((432, count), np.float32)
    for a in range(3):
        for q in range(9):
            for r in range(16):
                y, z = r // 4 + q // 3 - 1, r % 4 + q % 3 - 1
                at = 16 * (9 * a + q) + r
                pick[at, 9 * a + 3 * (y // 4 + 1) + z // 4 + 1] = 16
                add[at] = 4 * (y % 4) + z % 4
    return jnp.asarray(pick, BF16), jnp.asarray(add)


def level_three_rows(count):
    pick = np.zeros((360, 27), np.float32)
    add = np.full((360, count), -1, np.float32)
    for tap in range(27):
        for u in range(8):
            x, y, z = (u >> 2) + tap // 9 - 1, ((u >> 1) & 1) + tap // 3 % 3 - 1, (u & 1) + tap % 3 - 1
            side = x // 2
            at = 8 * tap if side == 0 else 8 * (27 + tap) if side < 0 else 8 * (36 + tap - 18)
            pick[at + u, 9 * (side + 1) + 3 * (y // 2 + 1) + z // 2 + 1] = 8
            add[at + u] = 4 * (x % 2) + 2 * (y % 2) + z % 2 + (8 * count if side > 0 else 0)
    return jnp.asarray(pick, BF16), jnp.asarray(add)


def child_rows():
    pick = np.zeros((64, 64), np.float32)
    for q in range(8):
        for u in range(8):
            x, y, z = [2 * ((u >> s) & 1) + ((q >> s) & 1) for s in (2, 1, 0)]
            pick[8 * q + u, 16 * x + 4 * y + z] = 1
    return jnp.asarray(pick, BF16)


ANY = pl.BlockSpec(memory_space=pl.ANY)
VMEM = pl.BlockSpec(memory_space=pltpu.VMEM)
DMA = pltpu.SemaphoreType.DMA


def call(kernel, cost, out_shape, scratch, *args, remain=(), store=()):
    single = not isinstance(out_shape, tuple)
    outs = (out_shape,) if single else out_shape
    specs = tuple(ANY if n in store else VMEM for n in range(len(outs)))
    return pl.pallas_call(
        kernel,
        out_shape=out_shape,
        in_specs=[ANY if n in remain else VMEM for n in range(len(args))],
        out_specs=specs[0] if single else specs,
        scratch_shapes=scratch,
        compiler_params=pltpu.CompilerParams(vmem_limit_bytes=24 * 1024 * 1024),
        cost_estimate=pl.CostEstimate(
            flops=cost * 10**9, bytes_accessed=10**7, transcendentals=0
        ),
    )(*args)


def swaps(tiles, count):
    within, across = [], []
    for t in range(tiles):
        for m in range(count):
            if m ^ 1 < count:
                within.append((t * count + m, t * count + (m ^ 1)))
            other = ((m - 1) ^ 1) + 1 if m else -1
            if 0 <= other < count:
                across.append((t * count + m, t * count + other))
            elif t ^ 1 < tiles:
                across.append((t * count + m, (t ^ 1) * count + m))
    return within, across


def on_device(
    features,
    neighbours,
    occupancy,
    conv_one,
    first_reduce_kernel,
    conv_two,
    second_reduce_kernel,
    conv_three,
):
    axes = ("tiles", LINE)
    within, across = swaps(lax.axis_size("tiles"), lax.axis_size(LINE))
    count = features.shape[0]
    features = jnp.swapaxes(features, 1, 2)
    shape = jax.ShapeDtypeStruct
    scalars = [pltpu.SMEM(neighbours.shape, jnp.int32), DMA(())]

    def exchange(to_a, to_b):
        from_b = lax.ppermute(to_b, axes, across)
        return lax.ppermute(to_a, axes, within), from_b

    face = shape((count // 2, 64, 128), BF16)
    from_a, from_b = exchange(
        *call(
            edges_kernel,
            1,
            (face, face),
            [
                pltpu.VMEM((2, count, 64, 128), BF16),
                pltpu.VMEM(occupancy.shape, jnp.int32),
                DMA((3,)),
            ],
            features, occupancy,
            remain=(0, 1),
        )
    )
    own_two, low_two, high_two, own_three, faces_three, pair_words, mask_two, mask_three = call(
        tables_kernel,
        1,
        (shape((9 * 16 * count, 16 * count), BF16),) * 3
        + (
            shape((27 * 8 * count, 8 * count), BF16),
            shape((18 * 8 * count, 16 * count), BF16),
            shape((8, count, 128), jnp.int32),
            shape((4, 16 * count, 128), F32),
            shape((8 * count, 256), F32),
        ),
        [],
        neighbours, occupancy, *level_two_rows(count), *level_three_rows(count),
    )
    padded, taps, face_taps, partial = call(
        outer_kernel,
        4,
        (
            shape((count, 3, 5, 6, 16, 128), BF16),
            shape((9 * 256, 128), BF16),
            shape((9 * 128, 128), BF16),
            shape((2, count * 64, 128), F32),
        ),
        [
            pltpu.VMEM((3, count + 1, 64, 128), F32),
            pltpu.VMEM((count + 1, 64, 128), F32),
            pltpu.VMEM((count + 1, 64, 128), F32),
        ]
        + scalars,
        neighbours, occupancy, features, conv_one,
        remain=(0,),
    )
    plane = shape((16 * count, 128), BF16)
    planes = shape((2, 16 * count, 128), BF16)
    sums = pltpu.VMEM((count * 64, 128), F32)
    outer, outer_two, to_a, to_b = call(
        faces_one_kernel,
        2,
        (shape((count, 2, 64, 128), BF16), planes, plane, plane),
        [
            pltpu.VMEM((count + 1, 64, 128), F32),
            pltpu.VMEM((count, 3, 6, 16, 128), BF16),
            sums,
            sums,
        ]
        + scalars,
        neighbours, from_a, from_b, face_taps, partial, first_reduce_kernel, pair_words, mask_two,
        remain=(0,),
    )
    from_a, from_b = exchange(to_a, to_b)

    first_level, inner_two = call(
        inner_kernel,
        4,
        (shape(features.shape, BF16), planes),
        [pltpu.VMEM(features.shape, BF16), sums, sums, DMA((count,))],
        padded, taps, outer, first_reduce_kernel, pair_words, mask_two,
        store=(0,),
    )
    partial = call(
        own_two_kernel,
        2,
        shape((4 * 16 * count, 128), F32),
        [],
        outer_two, inner_two, own_two, conv_two,
    )
    second_level, third = call(
        faces_two_kernel,
        2,
        (shape((count, 64, 128), BF16), shape((8 * count, 256), BF16)),
        [],
        low_two, high_two, child_rows(), partial, from_a, from_b, conv_two, second_reduce_kernel,
        mask_two, mask_three,
    )
    from_a, from_b = exchange(third, third)

    partial, second_level = call(
        own_three_kernel,
        2,
        (shape((8 * count, 256), F32), shape(second_level.shape, BF16)),
        [DMA(())],
        own_three, third, conv_three, second_level,
        store=(1,),
    )
    third_level = call(
        faces_three_kernel,
        1,
        shape((count, 8, 256), BF16),
        [],
        faces_three, partial, from_a, from_b, conv_three, mask_three,
    )
    return jnp.swapaxes(first_level, 1, 2), second_level, third_level


def solution(mesh):
    split = P(("tiles", LINE))
    return jax.shard_map(
        on_device,
        mesh=mesh,
        in_specs=(split, split, split, P(), P(), P(), P(), P()),
        out_specs=(split, split, split),
        check_vma=False,
    )
```

```python
import jax
import jax.numpy as jnp
import numpy as np
from jax import lax
from jax.experimental import pallas as pl
from jax.experimental.pallas import tpu as pltpu
from jax.sharding import PartitionSpec as P

F32 = jnp.float32
BF16 = jnp.bfloat16
LINE = "morton"


def dot(x, y):
    return jnp.dot(x, y, preferred_element_type=F32)


def iota(shape, axis):
    return lax.broadcasted_iota(jnp.int32, shape, axis)


def stack(parts):
    return jnp.concatenate(parts, axis=0)


def beside(parts):
    return jnp.concatenate(parts, axis=1)


def bits_of(words, shift):
    return jnp.bitwise_and(lax.shift_right_logical(words, shift), 1).astype(F32)


def either(x, y):
    return jnp.bitwise_or(x, y)


def on_odd_place():
    return lax.rem(lax.axis_index(LINE), 2) == 1


def word_lanes(words, w):
    return jnp.broadcast_to(words[:, w : w + 1], (words.shape[0], 128))


def column_bits(words, column):
    lane = iota((words.shape[0], 128), 1)
    w = [word_lanes(words, 4 * column + q) for q in range(4)]
    chosen = jnp.where(
        lane < 64, jnp.where(lane < 32, w[0], w[1]), jnp.where(lane < 96, w[2], w[3])
    )
    return bits_of(chosen, jnp.bitwise_and(lane, 31))


def slots_of(neighbours, first, count, b, tap):
    numbers = [neighbours[b, tap + q] for q in range(9)]
    shift = (1 - tap // 9) * count - first
    return [jnp.where(n < 0, count, n + shift) for n in numbers]


def masks_kernel(occupancy, bits, pair_words, mask_two, mask_three):
    count = occupancy.shape[0]
    for q in range(4):
        bits[q] = column_bits(occupancy[...], q)
    words = [word_lanes(occupancy[...], w) for w in range(16)]
    lane = iota((count, 128), 1)
    row = iota((8, 128), 0)
    any_two = []
    for i in range(4):
        for half in range(2):
            low, high = words[4 * i + half], words[4 * i + 2 + half]
            pair_words[2 * i + half] = jnp.where(lane < 64, low, high)
            word = either(low, high)
            word = either(word, lax.shift_right_logical(word, 1))
            any_two.append(either(word, lax.shift_right_logical(word, 8)))
    two_shift = 16 * lax.shift_right_logical(row, 2) + 2 * jnp.bitwise_and(row, 3)
    for i in range(4):
        for b in range(count):
            mask_two[i, 16 * b : 16 * (b + 1)] = stack(
                [
                    bits_of(
                        jnp.broadcast_to(any_two[2 * i + half][b : b + 1], (8, 128)), two_shift
                    )
                    for half in range(2)
                ]
            )
    any_three = []
    for i in range(2):
        for j in range(2):
            word = either(any_two[4 * i + j], any_two[4 * i + 2 + j])
            word = either(word, lax.shift_right_logical(word, 16))
            any_three.append(either(word, lax.shift_right_logical(word, 2)))
    for b in range(count):
        tile = [jnp.broadcast_to(word[b : b + 1], (8, 128)) for word in any_three]
        tile = jnp.where(
            row < 4, jnp.where(row < 2, tile[0], tile[1]), jnp.where(row < 6, tile[2], tile[3])
        )
        mask = bits_of(tile, 4 * jnp.bitwise_and(row, 1))
        mask_three[8 * b : 8 * (b + 1)] = beside([mask, mask])


def edges_kernel(features, bits, to_a, to_b):
    last = features.shape[2] - 128
    lane = iota((64, 128), 1)
    odd = on_odd_place()
    for q in range(features.shape[0] // 2):
        low, high = [
            [
                features[b, :, column * last : column * last + 128].astype(F32)
                * bits[3 * column, b : b + 1]
                for b in (2 * q, 2 * q + 1)
            ]
            for column in range(2)
        ]
        lows = jnp.where(lane < 64, low[0], pltpu.roll(low[1], 64, 1))
        highs = jnp.where(lane < 64, pltpu.roll(high[0], 64, 1), high[1])
        to_a[q] = jnp.where(odd, lows, highs).astype(BF16)
        to_b[q] = jnp.where(odd, highs, lows).astype(BF16)


def slot_rows(neighbours):
    count = neighbours.shape[0]
    number = neighbours[...]
    tap = iota(number.shape, 1)
    shift = jnp.where(tap < 9, count, jnp.where(tap < 18, 0, -count))
    slot = jnp.where(
        number < 0, 4 * count, number + shift - lax.axis_index(LINE) * count
    ).astype(F32)
    return stack(
        [jnp.broadcast_to(slot[b : b + 1], (128, number.shape[1])) for b in range(count)]
    ).astype(BF16)


def times_transposed(x, y):
    return lax.dot_general(x, y, (((1,), (1,)), ((), ())), preferred_element_type=F32)


def level_two_tables_kernel(neighbours, pick, own_two, low_two, high_two):
    count = neighbours.shape[0]
    rows = times_transposed(pick[...], slot_rows(neighbours))
    lane = iota((16, 16 * count), 1)
    row = iota((16, 16 * count), 0)
    j, k = lax.shift_right_logical(row, 2), jnp.bitwise_and(row, 3)
    for q in range(9):
        source = 4 * jnp.bitwise_and(j + q // 3 + 3, 3) + jnp.bitwise_and(k + q % 3 + 3, 3)
        wanted = (lane - source).astype(F32)
        for a, table in enumerate((low_two, own_two, high_two)):
            at = 16 * (9 * a + q)
            for b in range(count):
                table[16 * (count * q + b) : 16 * (count * q + b + 1), :] = jnp.where(
                    rows[at : at + 16, 128 * b : 128 * b + 16 * count] == wanted, 1.0, 0.0
                ).astype(BF16)


def level_three_tables_kernel(neighbours, pick, later, own_three, faces_three):
    count = neighbours.shape[0]
    rows = times_transposed(pick[...], slot_rows(neighbours))
    row = iota((8, 128), 0)
    voxel = [jnp.bitwise_and(lax.shift_right_logical(row, s), 1) for s in (2, 1, 0)]
    lane = iota((8, 128), 1)
    at = base = 0
    for table, sides in ((own_three, (0,)), (faces_three, (-1, 1))):
        for side in sides:
            for tap in range(27):
                if side and tap // 9 != side + 1:
                    continue
                shift = (tap // 9 - 1, tap // 3 % 3 - 1, tap % 3 - 1)
                x, y, z = [v + d for v, d in zip(voxel, shift)]
                here = (x < 0) if side < 0 else (x > 1) if side else (x >= 0) & (x <= 1)
                x, y, z = [jnp.bitwise_and(v + 2, 1) for v in (x, y, z)]
                source = 4 * x + 2 * y + z + (8 * count if side > 0 else 0)
                wanted = jnp.where(here, lane - source, -1).astype(F32)
                tiles = [
                    jnp.where(rows[at : at + 8, 128 * b : 128 * (b + 1)] == wanted, 1.0, 0.0)
                    for b in range(count)
                ]
                table[count * at - base : count * (at + 8) - base, :] = stack(tiles)[
                    :, : table.shape[1]
                ].astype(BF16)
                at += 8
        base = count * at


def shifted_windows(source, row):
    shifted = []
    for j in range(-1, 9):
        c, at = (0, 7) if j < 0 else (2, 0) if j > 7 else (1, j)
        left, mid, right = [source(3 * c + e, at) for e in range(3)]
        shifted.append(
            (
                pltpu.roll(jnp.where(row == 7, left, mid), 1, 0),
                mid,
                pltpu.roll(jnp.where(row == 0, right, mid), 7, 0),
            )
        )
    return [
        [stack([shifted[jr][e], shifted[jr + 4][e]]).astype(BF16) for e in range(3)]
        for jr in range(6)
    ]


def outer_kernel(
    neighbours, bits, features, kernel, reduce,
    middle, taps, face_taps, reduce_taps, partial,
    tables, windows, wrap_taps, numbers, arrived,
):
    count = features.shape[0]
    first = lax.axis_index(LINE) * count
    lane = iota((64, 128), 1)
    row = iota((8, 128), 0)
    copy = pltpu.make_async_copy(neighbours, numbers, arrived)
    copy.start()

    none = jnp.zeros((64, 64), F32)
    for q in range(9):
        w = [kernel[9 * a + q].astype(F32) for a in range(3)]
        rows = slice(q * 128, (q + 1) * 128)
        taps[rows, :] = stack(
            [beside([w[2], w[1], w[0], none]), beside([none, w[2], w[1], w[0]])]
        ).astype(BF16)
        wrap_taps[rows, :] = stack(
            [beside([w[2], w[1], none, none]), beside([none, none, w[1], w[0]])]
        ).astype(BF16)
        face_taps[rows, :] = stack([beside([w[0], none]), beside([none, w[2]])]).astype(BF16)

    reduce_taps[...] = stack(
        [
            beside([reduce[4 * ci + 2 * cj], reduce[4 * ci + 2 * cj + 1]])
            for cj in range(2)
            for ci in range(2)
        ]
    )

    for pair in range(4):
        tables[pair, count] = jnp.zeros((64, 128), F32)
    for b in range(count):
        cols = [
            features[b, :, 128 * q : 128 * (q + 1)].astype(F32) * bits[q, b : b + 1]
            for q in range(4)
        ]
        rolled = [pltpu.roll(col, 64, 1) for col in cols]
        for p in (0, 2):
            m = stack(
                [
                    jnp.where(lane < 64, rolled[p], cols[p + 1]),
                    jnp.where(lane < 64, cols[p + 1], rolled[(p + 2) % 4]),
                ]
            ).T
            tables[p, b] = m[:64]
            tables[p + 1, b] = m[64:]

    copy.wait()
    for b in range(count):
        slot = slots_of(numbers, first, count, b, 9)
        for pair in range(4):
            tiles = shifted_windows(lambda q, j: tables[pair, slot[q], pl.ds(8 * j, 8), :], row)
            for jr in range(6):
                for e in range(3):
                    if pair == 1:
                        middle[b, e, jr] = tiles[jr][e]
                    else:
                        windows[b, e, pair, jr] = tiles[jr][e]

    group = count // 2
    for g in range(2):
        bricks = slice(g * group, (g + 1) * group)
        rows = slice(g * group * 64, (g + 1) * group * 64)
        low, high, wrap = [
            dot(
                beside(
                    [
                        windows[bricks, e, pair, c : c + 4].reshape(group * 64, 128)
                        for c in range(3)
                        for e in range(3)
                    ]
                ),
                weights[...],
            )
            for pair, weights in ((0, taps), (2, taps), (3, wrap_taps))
        ]
        partial[0, rows] = low[:, :128] + wrap[:, 128:]
        partial[1, rows] = low[:, 128:]
        partial[2, rows] = high[:, :128]
        partial[3, rows] = high[:, 128:] + wrap[:, :128]


def masked_tiles(sums, pair_words, b, i):
    row = iota((8, 128), 0)
    tiles = {}
    for half in range(2):
        words = jnp.broadcast_to(pair_words[2 * i + half, b : b + 1, :], (8, 128))
        for jr in range(4):
            at = jr * 16 + half * 8
            tiles[4 * half + jr] = jnp.maximum(sums[at : at + 8], 0.0) * bits_of(
                words, row + 8 * jr
            )
    return [tiles[j] for j in range(8)]


def reduce_planes(groups, weights, low_sums, high_sums):
    left = stack(
        [beside([tiles[j], tiles[j + 1]]) for tiles in groups for j in (0, 2, 4, 6)]
    ).astype(BF16)
    sums = dot(left, weights[...])
    low_sums[...] = sums[:, :128]
    high_sums[...] = sums[:, 128:]
    return [
        low_sums[pl.ds(32 * g, 16, stride=2), :] + high_sums[pl.ds(32 * g + 1, 16, stride=2), :]
        for g in range(len(groups))
    ]


def faces_one_kernel(
    neighbours, from_a, from_b, face_taps, partial, reduce, pair_words, mask_two,
    outer, second, to_a, to_b,
    halo, windows, low_sums, high_sums, numbers, arrived,
):
    count = outer.shape[0]
    first = lax.axis_index(LINE) * count
    lane = iota((64, 128), 1)
    small = iota((8, 128), 1)
    row = iota((8, 128), 0)
    odd = on_odd_place()
    copy = pltpu.make_async_copy(neighbours, numbers, arrived)
    copy.start()
    halo[count] = jnp.zeros((64, 128), F32)
    for q in range(count // 2):
        one, two = from_a[q].astype(F32), from_b[q].astype(F32)
        m = stack([jnp.where(odd, one, two), jnp.where(odd, two, one)]).T
        halo[2 * q] = m[:64]
        halo[2 * q + 1] = m[64:]
    copy.wait()
    for b in range(count):
        low = slots_of(numbers, first, count, b, 0)
        high = slots_of(numbers, first, count, b, 18)

        def source(q, j):
            rows = pl.ds(8 * j, 8)
            return jnp.where(small < 64, halo[low[q], rows, :], halo[high[q], rows, :])

        tiles = shifted_windows(source, row)
        for jr in range(6):
            for e in range(3):
                windows[b, e, jr] = tiles[jr][e]
    added = dot(
        beside(
            [
                windows[:, e, c : c + 4].reshape(count * 64, 128)
                for c in range(3)
                for e in range(3)
            ]
        ),
        face_taps[...],
    )
    groups = []
    for b in range(count):
        at = slice(64 * b, 64 * (b + 1))
        for side in range(2):
            near = (lane < 64) == (side == 0)
            sums = partial[3 * side, at] + jnp.where(near, added[at], 0.0)
            groups.append(masked_tiles(sums, pair_words, b, 3 * side))
            outer[b, side] = stack(groups[-1]).astype(BF16)
    sums = reduce_planes(groups, reduce, low_sums, high_sums)
    for b in range(count):
        at = slice(16 * b, 16 * (b + 1))
        planes = [
            (jnp.maximum(sums[2 * b + side], 0.0) * mask_two[3 * side, at]).astype(BF16)
            for side in range(2)
        ]
        second[0, at] = planes[0]
        second[1, at] = planes[1]
        to_a[at] = jnp.where(odd, planes[0], planes[1])
        to_b[at] = jnp.where(odd, planes[1], planes[0])


def inner_kernel(
    middle, taps, partial, outer, reduce, pair_words, mask_two,
    out, second,
    low_sums, high_sums,
):
    count = middle.shape[0]
    lane = iota((64, 128), 1)
    added = dot(
        beside(
            [
                middle[:, e, c : c + 4].reshape(count * 64, 128)
                for c in range(3)
                for e in range(3)
            ]
        ),
        taps[...],
    )
    groups = []
    for b in range(count):
        for i in (1, 2):
            at = slice(64 * b, 64 * (b + 1))
            sums = partial[i, at] + added[at, 128 * (i - 1) : 128 * i]
            groups.append(masked_tiles(sums, pair_words, b, i))
        ordered = [
            outer[b, 0].astype(F32),
            stack(groups[2 * b]),
            stack(groups[2 * b + 1]),
            outer[b, 1].astype(F32),
        ]
        for i in (0, 2):
            m = stack(ordered[i : i + 2]).T
            top, bottom = m[:64], m[64:]
            out[b, :, 128 * i : 128 * (i + 1)] = jnp.where(
                lane < 64, top, pltpu.roll(bottom, 64, 1)
            ).astype(BF16)
            out[b, :, 128 * (i + 1) : 128 * (i + 2)] = jnp.where(
                lane < 64, pltpu.roll(top, 64, 1), bottom
            ).astype(BF16)
    sums = reduce_planes(groups, reduce, low_sums, high_sums)
    for b in range(count):
        at = slice(16 * b, 16 * (b + 1))
        for i in (1, 2):
            second[i - 1, at] = (
                jnp.maximum(sums[2 * b + i - 1], 0.0) * mask_two[i, at]
            ).astype(BF16)


def own_two_kernel(outer, inner, gather, kernel, first, partial, result, stored):
    copy = pltpu.make_async_copy(first, result, stored)
    copy.start()
    rows = outer.shape[1]
    planes = beside([outer[0], inner[0], inner[1], outer[1]])
    moved = dot(gather[...], planes).astype(BF16)
    left = beside(
        [
            stack(
                [
                    moved[q * rows : (q + 1) * rows, 128 * i : 128 * (i + 1)]
                    for i in range(4)
                ]
            )
            for q in range(9)
        ]
    )
    weights = [kernel[9 * a : 9 * (a + 1)].reshape(9 * 128, 128) for a in range(3)]
    sums = dot(left, beside(weights[:2]))
    later = dot(left[rows:], weights[2])
    for i in range(4):
        total = sums[i * rows : (i + 1) * rows, 128:]
        if i:
            total = total + sums[(i - 1) * rows : i * rows, :128]
        if i < 3:
            total = total + later[i * rows : (i + 1) * rows]
        partial[i * rows : (i + 1) * rows] = total
    copy.wait()


def faces_two_kernel(
    low_gather, high_gather, children, partial, from_a, from_b, kernel, reduce,
    mask_two, mask_three,
    second, third,
):
    count = second.shape[0]
    rows = 16 * count
    odd = on_odd_place()
    one, two = from_a[...], from_b[...]
    added = []
    for gather, face, tap in (
        (low_gather, jnp.where(odd, one, two), 0),
        (high_gather, jnp.where(odd, two, one), 18),
    ):
        moved = dot(gather[...], face).astype(BF16)
        left = beside([moved[q * rows : (q + 1) * rows] for q in range(9)])
        added.append(dot(left, kernel[tap : tap + 9].reshape(9 * 128, 128)))
    planes = []
    for i in range(4):
        sums = partial[i * rows : (i + 1) * rows]
        if i == 0:
            sums = sums + added[0]
        if i == 3:
            sums = sums + added[1]
        planes.append((jnp.maximum(sums, 0.0) * mask_two[i]).astype(BF16))
    bricks = [
        stack([planes[i][16 * b : 16 * (b + 1)] for i in range(4)]) for b in range(count)
    ]
    for b in range(count):
        second[b] = bricks[b]
    moved = dot(children[...], beside(bricks))
    left = beside(
        [
            stack([moved[8 * q : 8 * (q + 1), 128 * b : 128 * (b + 1)] for b in range(count)])
            for q in range(8)
        ]
    ).astype(BF16)
    sums = dot(left, reduce[...].reshape(8 * 128, 256))
    third[...] = (jnp.maximum(sums, 0.0) * mask_three[...]).astype(BF16)


def own_three_kernel(gather, third, kernel, second, partial, result, stored):
    copy = pltpu.make_async_copy(second, result, stored)
    copy.start()
    rows = third.shape[0]
    moved = dot(gather[...], third[...]).astype(BF16)
    left = beside([moved[q * rows : (q + 1) * rows] for q in range(27)])
    partial[...] = dot(left, kernel[...].reshape(27 * 256, 256))
    copy.wait()


def faces_three_kernel(gather, partial, from_a, from_b, kernel, mask_three, out):
    rows = partial.shape[0]
    odd = on_odd_place()
    one, two = from_a[...], from_b[...]
    faces = stack([jnp.where(odd, one, two), jnp.where(odd, two, one)])
    moved = dot(gather[...], faces).astype(BF16)
    left = beside([moved[q * rows : (q + 1) * rows] for q in range(18)])
    weights = stack([kernel[:9].reshape(9 * 256, 256), kernel[18:].reshape(9 * 256, 256)])
    sums = partial[...] + dot(left, weights)
    out[...] = (jnp.maximum(sums, 0.0) * mask_three[...]).astype(BF16).reshape(out.shape)


def level_two_picks():
    pick = np.zeros((432, 27), np.float32)
    for tap in range(27):
        for r in range(16):
            y, z = r // 4 + tap // 3 % 3 - 1, r % 4 + tap % 3 - 1
            pick[16 * tap + r, tap // 9 * 9 + 3 * (y // 4 + 1) + z // 4 + 1] = 16
    return jnp.asarray(pick, BF16)


def level_three_picks():
    pick = np.zeros((45 * 8, 27), np.float32)
    for tap in range(27):
        for u in range(8):
            x, y, z = [
                ((u >> s) & 1) + d - 1
                for s, d in ((2, tap // 9), (1, tap // 3 % 3), (0, tap % 3))
            ]
            side = x // 2
            at = 8 * (tap + (0, 18, 27)[side])
            pick[at + u, 9 * (side + 1) + 3 * (y // 2 + 1) + z // 2 + 1] = 8
    return jnp.asarray(pick, BF16)


def child_rows():
    pick = np.zeros((64, 64), np.float32)
    for q in range(8):
        for u in range(8):
            x, y, z = [2 * ((u >> s) & 1) + ((q >> s) & 1) for s in (2, 1, 0)]
            pick[8 * q + u, 16 * x + 4 * y + z] = 1
    return jnp.asarray(pick, BF16)


ANY = pl.BlockSpec(memory_space=pl.ANY)
VMEM = pl.BlockSpec(memory_space=pltpu.VMEM)
DMA = pltpu.SemaphoreType.DMA


def call(kernel, cost, out_shape, scratch, *args, remain=(), store=()):
    single = not isinstance(out_shape, tuple)
    outs = (out_shape,) if single else out_shape
    specs = tuple(ANY if n in store else VMEM for n in range(len(outs)))
    return pl.pallas_call(
        kernel,
        out_shape=out_shape,
        in_specs=[ANY if n in remain else VMEM for n in range(len(args))],
        out_specs=specs[0] if single else specs,
        scratch_shapes=scratch,
        compiler_params=pltpu.CompilerParams(vmem_limit_bytes=24 * 1024 * 1024),
        cost_estimate=pl.CostEstimate(
            flops=int(cost * 10**10), bytes_accessed=10**7, transcendentals=0
        ),
    )(*args)


def swaps(tiles, count):
    within, across = [], []
    for t in range(tiles):
        for m in range(count):
            if m ^ 1 < count:
                within.append((t * count + m, t * count + (m ^ 1)))
            other = ((m - 1) ^ 1) + 1 if m else -1
            if 0 <= other < count:
                across.append((t * count + m, t * count + other))
            elif t ^ 1 < tiles:
                across.append((t * count + m, (t ^ 1) * count + m))
    return within, across


def on_device(
    features,
    neighbours,
    occupancy,
    conv_one,
    first_reduce_kernel,
    conv_two,
    second_reduce_kernel,
    conv_three,
):
    axes = ("tiles", LINE)
    within, across = swaps(lax.axis_size("tiles"), lax.axis_size(LINE))
    count = features.shape[0]
    features = jnp.swapaxes(features, 1, 2)
    shape = jax.ShapeDtypeStruct
    scalars = [pltpu.SMEM(neighbours.shape, jnp.int32), DMA(())]

    def exchange(to_a, to_b):
        from_b = lax.ppermute(to_b, axes, across)
        return lax.ppermute(to_a, axes, within), from_b

    face = shape((count // 2, 64, 128), BF16)
    bits, pair_words, mask_two, mask_three = call(
        masks_kernel,
        0.3,
        (
            shape((4, count, 128), F32),
            shape((8, count, 128), jnp.int32),
            shape((4, 16 * count, 128), F32),
            shape((8 * count, 256), F32),
        ),
        [],
        occupancy,
    )
    from_a, from_b = exchange(*call(edges_kernel, 0.3, (face, face), [], features, bits))
    own_two, low_two, high_two = call(
        level_two_tables_kernel,
        0.4,
        (shape((9 * 16 * count, 16 * count), BF16),) * 3,
        [],
        neighbours, level_two_picks(),
    )
    middle, taps, face_taps, reduce_taps, partial = call(
        outer_kernel,
        2.0,
        (
            shape((count, 3, 6, 16, 128), BF16),
            shape((9 * 128, 256), BF16),
            shape((9 * 128, 128), BF16),
            shape((256, 256), BF16),
            shape((4, count * 64, 128), F32),
        ),
        [
            pltpu.VMEM((4, count + 1, 64, 128), F32),
            pltpu.VMEM((count, 3, 4, 6, 16, 128), BF16),
            pltpu.VMEM((9 * 128, 256), BF16),
        ]
        + scalars,
        neighbours, bits, features, conv_one, first_reduce_kernel,
        remain=(0,),
    )
    plane = shape((16 * count, 128), BF16)
    planes = shape((2, 16 * count, 128), BF16)
    sums = pltpu.VMEM((count * 64, 128), F32)
    outer, outer_two, to_a, to_b = call(
        faces_one_kernel,
        1.5,
        (shape((count, 2, 64, 128), BF16), planes, plane, plane),
        [
            pltpu.VMEM((count + 1, 64, 128), F32),
            pltpu.VMEM((count, 3, 6, 16, 128), BF16),
            sums,
            sums,
        ]
        + scalars,
        neighbours, from_a, from_b, face_taps, partial, reduce_taps, pair_words, mask_two,
        remain=(0,),
    )
    from_a, from_b = exchange(to_a, to_b)

    first_level, inner_two = call(
        inner_kernel,
        1.2,
        (shape(features.shape, BF16), planes),
        [sums, sums],
        middle, taps, partial, outer, reduce_taps, pair_words, mask_two,
    )
    partial, first_level = call(
        own_two_kernel,
        1.0,
        (shape((4 * 16 * count, 128), F32), shape(features.shape, BF16)),
        [DMA(())],
        outer_two, inner_two, own_two, conv_two, first_level,
        store=(1,),
    )
    second_level, third = call(
        faces_two_kernel,
        0.9,
        (shape((count, 64, 128), BF16), shape((8 * count, 256), BF16)),
        [],
        low_two, high_two, child_rows(), partial, from_a, from_b, conv_two, second_reduce_kernel,
        mask_two, mask_three,
    )
    from_a, from_b = exchange(third, third)

    own_three, faces_three = call(
        level_three_tables_kernel,
        0.4,
        (shape((27 * 8 * count, 8 * count), BF16), shape((18 * 8 * count, 16 * count), BF16)),
        [],
        neighbours, level_three_picks(), third,
    )
    partial, second_level = call(
        own_three_kernel,
        1.0,
        (shape((8 * count, 256), F32), shape(second_level.shape, BF16)),
        [DMA(())],
        own_three, third, conv_three, second_level,
        store=(1,),
    )
    third_level = call(
        faces_three_kernel,
        1,
        shape((count, 8, 256), BF16),
        [],
        faces_three, partial, from_a, from_b, conv_three, mask_three,
    )
    return jnp.swapaxes(first_level, 1, 2), second_level, third_level


def solution(mesh):
    split = P(("tiles", LINE))
    return jax.shard_map(
        on_device,
        mesh=mesh,
        in_specs=(split, split, split, P(), P(), P(), P(), P()),
        out_specs=(split, split, split),
        check_vma=False,
    )
```

```python
import jax
import jax.numpy as jnp
import numpy as np
from jax import lax
from jax.experimental import pallas as pl
from jax.experimental.pallas import tpu as pltpu
from jax.sharding import PartitionSpec as P

F32 = jnp.float32
BF16 = jnp.bfloat16
LINE = "morton"


def dot(x, y):
    return jnp.dot(x, y, preferred_element_type=F32)


def iota(shape, axis):
    return lax.broadcasted_iota(jnp.int32, shape, axis)


def stack(parts):
    return jnp.concatenate(parts, axis=0)


def beside(parts):
    return jnp.concatenate(parts, axis=1)


def bits_of(words, shift):
    return jnp.bitwise_and(lax.shift_right_logical(words, shift), 1).astype(F32)


def either(x, y):
    return jnp.bitwise_or(x, y)


def on_odd_place():
    return lax.rem(lax.axis_index(LINE), 2) == 1


def word_lanes(words, w):
    return jnp.broadcast_to(words[:, w : w + 1], (words.shape[0], 128))


def column_bits(words, column):
    lane = iota((words.shape[0], 128), 1)
    w = [word_lanes(words, 4 * column + q) for q in range(4)]
    chosen = jnp.where(
        lane < 64, jnp.where(lane < 32, w[0], w[1]), jnp.where(lane < 96, w[2], w[3])
    )
    return bits_of(chosen, jnp.bitwise_and(lane, 31))


def slot_numbers(neighbours):
    count = neighbours.shape[0]
    number = neighbours[...]
    tap = iota(number.shape, 1)
    shift = jnp.where(tap < 9, count, jnp.where(tap < 18, 0, -count))
    return jnp.where(number < 0, count, number + shift - lax.axis_index(LINE) * count)


def masks_kernel(occupancy, bits, pair_words, mask_two, mask_three):
    count = occupancy.shape[0]
    for q in range(4):
        bits[q] = column_bits(occupancy[...], q)
    words = [word_lanes(occupancy[...], w) for w in range(16)]
    lane = iota((count, 128), 1)
    row = iota((8, 128), 0)
    any_two = []
    for i in range(4):
        for half in range(2):
            low, high = words[4 * i + half], words[4 * i + 2 + half]
            pair_words[2 * i + half] = jnp.where(lane < 64, low, high)
            word = either(low, high)
            word = either(word, lax.shift_right_logical(word, 1))
            any_two.append(either(word, lax.shift_right_logical(word, 8)))
    two_shift = 16 * lax.shift_right_logical(row, 2) + 2 * jnp.bitwise_and(row, 3)
    for i in range(4):
        for b in range(count):
            mask_two[i, 16 * b : 16 * (b + 1)] = stack(
                [
                    bits_of(
                        jnp.broadcast_to(any_two[2 * i + half][b : b + 1], (8, 128)), two_shift
                    )
                    for half in range(2)
                ]
            )
    any_three = []
    for i in range(2):
        for j in range(2):
            word = either(any_two[4 * i + j], any_two[4 * i + 2 + j])
            word = either(word, lax.shift_right_logical(word, 16))
            any_three.append(either(word, lax.shift_right_logical(word, 2)))
    for i in range(2):
        for b in range(0, count, 2):
            tile = [
                jnp.broadcast_to(any_three[2 * i + j][n : n + 1], (8, 128))
                for n in (b, b + 1)
                for j in range(2)
            ]
            tile = jnp.where(
                row < 4, jnp.where(row < 2, tile[0], tile[1]), jnp.where(row < 6, tile[2], tile[3])
            )
            mask = bits_of(tile, 4 * jnp.bitwise_and(row, 1))
            at = 4 * (count * i + b)
            mask_three[at : at + 8] = beside([mask, mask])


def edges_kernel(features, bits, to_a, to_b):
    last = features.shape[2] - 128
    lane = iota((64, 128), 1)
    odd = on_odd_place()
    for q in range(features.shape[0] // 2):
        low, high = [
            [
                features[b, :, column * last : column * last + 128].astype(F32)
                * bits[3 * column, b : b + 1]
                for b in (2 * q, 2 * q + 1)
            ]
            for column in range(2)
        ]
        lows = jnp.where(lane < 64, low[0], pltpu.roll(low[1], 64, 1))
        highs = jnp.where(lane < 64, pltpu.roll(high[0], 64, 1), high[1])
        to_a[q] = jnp.where(odd, lows, highs).astype(BF16)
        to_b[q] = jnp.where(odd, highs, lows).astype(BF16)


def slot_rows(neighbours):
    count = neighbours.shape[0]
    slot = jnp.where(neighbours[...] < 0, 4 * count, slot_numbers(neighbours)).astype(F32)
    return stack(
        [jnp.broadcast_to(slot[b : b + 1], (128, slot.shape[1])) for b in range(count)]
    ).astype(BF16)


def times_transposed(x, y):
    return lax.dot_general(x, y, (((1,), (1,)), ((), ())), preferred_element_type=F32)


def level_two_tables_kernel(neighbours, pick, own_two, sides_two):
    count = neighbours.shape[0]
    rows = times_transposed(pick[...], slot_rows(neighbours))
    lane = iota((16, 16 * count), 1)
    row = iota((16, 16 * count), 0)
    j, k = lax.shift_right_logical(row, 2), jnp.bitwise_and(row, 3)
    for q in range(9):
        source = 4 * jnp.bitwise_and(j + q // 3 + 3, 3) + jnp.bitwise_and(k + q % 3 + 3, 3)
        wanted = (lane - source).astype(F32)
        for a, table in enumerate((sides_two.at[0], own_two, sides_two.at[1])):
            at = 16 * (9 * a + q)
            for b in range(count):
                table[16 * (count * q + b) : 16 * (count * q + b + 1), :] = jnp.where(
                    rows[at : at + 16, 128 * b : 128 * b + 16 * count] == wanted, 1.0, 0.0
                ).astype(BF16)


def level_three_tables_kernel(neighbours, pick, later, own_three, far_three):
    count = neighbours.shape[0]
    odd = on_odd_place()
    rows = times_transposed(pick[...], slot_rows(neighbours))
    row = iota((8, 128), 0)
    lane = iota((8, 128), 1)
    j, k = [jnp.bitwise_and(lax.shift_right_logical(row, n), 1) for n in (1, 0)]

    def block(tap, i, begin):
        c, e = tap // 3 % 3, tap % 3
        source = 2 * jnp.bitwise_and(j + c + 1, 1) + jnp.bitwise_and(k + e + 1, 1)
        wanted = (lane - source - begin).astype(F32)
        at = 8 * (2 * tap + i)
        tiles = []
        for b in range(0, count, 2):
            first, second = [rows[at : at + 8, 128 * n : 128 * (n + 1)] for n in (b, b + 1)]
            hit = jnp.where(row < 4, first, second) == wanted
            tiles.append(jnp.where(hit, 1.0, 0.0))
        return stack(tiles)

    nowhere = 16 * 4 * count
    for tap in range(27):
        for i in range(2):
            x = i + tap // 9 - 1
            if x < 0:
                begin = jnp.where(odd, 8 * count, nowhere)
            elif x > 1:
                begin = jnp.where(odd, nowhere, 8 * count)
            else:
                begin = 4 * count * x
            at = 8 * count * tap + 4 * count * i
            own_three[at : at + 4 * count, :] = block(tap, i, begin)[:, : 12 * count].astype(BF16)
    for q in range(9):
        tile = jnp.where(odd, block(18 + q, 1, 0), block(q, 0, 0))
        far_three[4 * count * q : 4 * count * (q + 1), :] = tile[:, : 4 * count].astype(BF16)


def shifted_windows(source, row):
    shifted = []
    for j in range(-1, 9):
        c, at = (0, 7) if j < 0 else (2, 0) if j > 7 else (1, j)
        left, mid, right = [source(3 * c + e, at) for e in range(3)]
        shifted.append(
            (
                pltpu.roll(jnp.where(row == 7, left, mid), 1, 0),
                mid,
                pltpu.roll(jnp.where(row == 0, right, mid), 7, 0),
            )
        )
    return [
        [stack([shifted[jr][e], shifted[jr + 4][e]]).astype(BF16) for e in range(3)]
        for jr in range(6)
    ]


def outer_kernel(
    neighbours, bits, features, kernel, reduce,
    middle, taps, face_taps, reduce_taps, partial,
    tables, windows, wrap_taps,
):
    count = features.shape[0]
    lane = iota((64, 128), 1)
    row = iota((8, 128), 0)
    numbers = slot_numbers(neighbours)

    none = jnp.zeros((64, 64), F32)
    for q in range(9):
        w = [kernel[9 * a + q].astype(F32) for a in range(3)]
        rows = slice(q * 128, (q + 1) * 128)
        taps[rows, :] = stack(
            [beside([w[2], w[1], w[0], none]), beside([none, w[2], w[1], w[0]])]
        ).astype(BF16)
        wrap_taps[rows, :] = stack(
            [beside([w[2], w[1], none, none]), beside([none, none, w[1], w[0]])]
        ).astype(BF16)
        face_taps[rows, :] = stack([beside([w[0], none]), beside([none, w[2]])]).astype(BF16)

    reduce_taps[...] = stack(
        [
            beside([reduce[4 * ci + 2 * cj], reduce[4 * ci + 2 * cj + 1]])
            for cj in range(2)
            for ci in range(2)
        ]
    )

    for pair in range(4):
        tables[pair, count] = jnp.zeros((64, 128), F32)
    for b in range(count):
        cols = [
            features[b, :, 128 * q : 128 * (q + 1)].astype(F32) * bits[q, b : b + 1]
            for q in range(4)
        ]
        rolled = [pltpu.roll(col, 64, 1) for col in cols]
        for p in (0, 2):
            m = stack(
                [
                    jnp.where(lane < 64, rolled[p], cols[p + 1]),
                    jnp.where(lane < 64, cols[p + 1], rolled[(p + 2) % 4]),
                ]
            ).T
            tables[p, b] = m[:64]
            tables[p + 1, b] = m[64:]

    for b in range(count):
        slot = [numbers[b, 9 + q] for q in range(9)]
        for pair in range(4):
            tiles = shifted_windows(lambda q, j: tables[pair, slot[q], pl.ds(8 * j, 8), :], row)
            for jr in range(6):
                for e in range(3):
                    if pair == 1:
                        middle[b, e, jr] = tiles[jr][e]
                    else:
                        windows[b, e, pair, jr] = tiles[jr][e]

    group = count // 2
    for g in range(2):
        bricks = slice(g * group, (g + 1) * group)
        rows = slice(g * group * 64, (g + 1) * group * 64)
        low, high, wrap = [
            dot(
                beside(
                    [
                        windows[bricks, e, pair, c : c + 4].reshape(group * 64, 128)
                        for c in range(3)
                        for e in range(3)
                    ]
                ),
                weights[...],
            )
            for pair, weights in ((0, taps), (2, taps), (3, wrap_taps))
        ]
        partial[0, rows] = low[:, :128] + wrap[:, 128:]
        partial[1, rows] = low[:, 128:]
        partial[2, rows] = high[:, :128]
        partial[3, rows] = high[:, 128:] + wrap[:, :128]


def masked_tiles(sums, pair_words, b, i):
    row = iota((8, 128), 0)
    tiles = {}
    for half in range(2):
        words = jnp.broadcast_to(pair_words[2 * i + half, b : b + 1, :], (8, 128))
        for jr in range(4):
            at = jr * 16 + half * 8
            tiles[4 * half + jr] = jnp.maximum(sums[at : at + 8], 0.0) * bits_of(
                words, row + 8 * jr
            )
    return [tiles[j] for j in range(8)]


def reduce_planes(groups, weights, low_sums, high_sums):
    left = stack(
        [beside([tiles[j], tiles[j + 1]]) for tiles in groups for j in (0, 2, 4, 6)]
    ).astype(BF16)
    sums = dot(left, weights[...])
    low_sums[...] = sums[:, :128]
    high_sums[...] = sums[:, 128:]
    return [
        low_sums[pl.ds(32 * g, 16, stride=2), :] + high_sums[pl.ds(32 * g + 1, 16, stride=2), :]
        for g in range(len(groups))
    ]


def faces_one_kernel(
    neighbours, from_a, from_b, face_taps, partial, reduce, pair_words, mask_two,
    outer, second, to_a, to_b,
    halo, windows, low_sums, high_sums,
):
    count = outer.shape[0]
    lane = iota((64, 128), 1)
    small = iota((8, 128), 1)
    row = iota((8, 128), 0)
    odd = on_odd_place()
    slot = slot_numbers(neighbours)
    halo[count] = jnp.zeros((64, 128), F32)
    for q in range(count // 2):
        one, two = from_a[q].astype(F32), from_b[q].astype(F32)
        m = stack([jnp.where(odd, one, two), jnp.where(odd, two, one)]).T
        halo[2 * q] = m[:64]
        halo[2 * q + 1] = m[64:]
    for b in range(count):
        low = [slot[b, q] for q in range(9)]
        high = [slot[b, 18 + q] for q in range(9)]

        def source(q, j):
            rows = pl.ds(8 * j, 8)
            return jnp.where(small < 64, halo[low[q], rows, :], halo[high[q], rows, :])

        tiles = shifted_windows(source, row)
        for jr in range(6):
            for e in range(3):
                windows[b, e, jr] = tiles[jr][e]
    added = dot(
        beside(
            [
                windows[:, e, c : c + 4].reshape(count * 64, 128)
                for c in range(3)
                for e in range(3)
            ]
        ),
        face_taps[...],
    )
    groups = []
    for b in range(count):
        at = slice(64 * b, 64 * (b + 1))
        for side in range(2):
            near = (lane < 64) == (side == 0)
            sums = partial[3 * side, at] + jnp.where(near, added[at], 0.0)
            groups.append(masked_tiles(sums, pair_words, b, 3 * side))
            outer[b, side] = stack(groups[-1]).astype(BF16)
    sums = reduce_planes(groups, reduce, low_sums, high_sums)
    for b in range(count):
        at = slice(16 * b, 16 * (b + 1))
        planes = [
            (jnp.maximum(sums[2 * b + side], 0.0) * mask_two[3 * side, at]).astype(BF16)
            for side in range(2)
        ]
        second[0, at] = planes[0]
        second[1, at] = planes[1]
        to_a[at] = jnp.where(odd, planes[0], planes[1])
        to_b[at] = jnp.where(odd, planes[1], planes[0])


def inner_kernel(
    middle, taps, partial, outer, reduce, pair_words, mask_two,
    out, second,
    low_sums, high_sums,
):
    count = middle.shape[0]
    lane = iota((64, 128), 1)
    added = dot(
        beside(
            [
                middle[:, e, c : c + 4].reshape(count * 64, 128)
                for c in range(3)
                for e in range(3)
            ]
        ),
        taps[...],
    )
    groups = []
    for b in range(count):
        for i in (1, 2):
            at = slice(64 * b, 64 * (b + 1))
            sums = partial[i, at] + added[at, 128 * (i - 1) : 128 * i]
            groups.append(masked_tiles(sums, pair_words, b, i))
        ordered = [
            outer[b, 0].astype(F32),
            stack(groups[2 * b]),
            stack(groups[2 * b + 1]),
            outer[b, 1].astype(F32),
        ]
        for i in (0, 2):
            m = stack(ordered[i : i + 2]).T
            top, bottom = m[:64], m[64:]
            out[b, :, 128 * i : 128 * (i + 1)] = jnp.where(
                lane < 64, top, pltpu.roll(bottom, 64, 1)
            ).astype(BF16)
            out[b, :, 128 * (i + 1) : 128 * (i + 2)] = jnp.where(
                lane < 64, pltpu.roll(top, 64, 1), bottom
            ).astype(BF16)
    sums = reduce_planes(groups, reduce, low_sums, high_sums)
    for b in range(count):
        at = slice(16 * b, 16 * (b + 1))
        for i in (1, 2):
            second[i - 1, at] = (
                jnp.maximum(sums[2 * b + i - 1], 0.0) * mask_two[i, at]
            ).astype(BF16)


def face_part(gather, face, kernel, high):
    moved = dot(gather, face).astype(BF16)
    rows = moved.shape[0] // 9
    left = beside([moved[q * rows : (q + 1) * rows] for q in range(9)])
    weights = kernel[pl.ds(18 * high, 9)]
    return dot(left, weights.reshape(9 * weights.shape[1], weights.shape[2]))


def own_two_kernel(
    outer, inner, own_gather, gathers, from_a, kernel, first,
    partial, result, stored,
):
    copy = pltpu.make_async_copy(first, result, stored)
    copy.start()
    rows = outer.shape[1]
    planes = beside([outer[0], inner[0], inner[1], outer[1]])
    moved = dot(own_gather[...], planes).astype(BF16)
    left = beside(
        [
            stack(
                [
                    moved[q * rows : (q + 1) * rows, 128 * i : 128 * (i + 1)]
                    for i in range(4)
                ]
            )
            for q in range(9)
        ]
    )
    weights = [kernel[9 * a : 9 * (a + 1)].reshape(9 * 128, 128) for a in range(3)]
    sums = dot(left, beside(weights[:2]))
    later = dot(left[rows:], weights[2])
    high = jnp.where(on_odd_place(), 0, 1)
    near = face_part(gathers[high], from_a[...], kernel, high)
    for i in range(4):
        total = sums[i * rows : (i + 1) * rows, 128:]
        if i:
            total = total + sums[(i - 1) * rows : i * rows, :128]
        if i < 3:
            total = total + later[i * rows : (i + 1) * rows]
        if i in (0, 3):
            total = total + jnp.where(high == i // 3, near, 0.0)
        partial[i * rows : (i + 1) * rows] = total
    copy.wait()


def faces_two_kernel(
    gathers, children, partial, from_b, kernel, reduce, mask_two, mask_three,
    second, third, to_a, to_b,
):
    count = second.shape[0]
    rows = 16 * count
    odd = on_odd_place()
    high = jnp.where(odd, 1, 0)
    far = face_part(gathers[high], from_b[...], kernel, high)
    planes = []
    for i in range(4):
        sums = partial[i * rows : (i + 1) * rows]
        if i in (0, 3):
            sums = sums + jnp.where(high == i // 3, far, 0.0)
        planes.append((jnp.maximum(sums, 0.0) * mask_two[i]).astype(BF16))
    bricks = [
        stack([planes[i][16 * b : 16 * (b + 1)] for i in range(4)]) for b in range(count)
    ]
    for b in range(count):
        second[b] = bricks[b]
    moved = dot(
        children[...], beside([stack(bricks[b : b + 2]) for b in range(0, count, 2)])
    )
    left = beside(
        [
            stack(
                [
                    moved[16 * q + 8 * i : 16 * q + 8 * (i + 1), 128 * n : 128 * (n + 1)]
                    for i in range(2)
                    for n in range(count // 2)
                ]
            )
            for q in range(8)
        ]
    ).astype(BF16)
    sums = dot(left, reduce[...].reshape(8 * 128, 256))
    value = jnp.maximum(sums, 0.0) * mask_three[...]
    third[...] = value.astype(BF16)
    low, high = value[: 4 * count], value[4 * count :]
    to_a[...] = jnp.where(odd, low, high).astype(BF16)
    to_b[...] = jnp.where(odd, high, low).astype(BF16)


def own_three_kernel(gather, third, from_a, kernel, second, partial, result, stored):
    copy = pltpu.make_async_copy(second, result, stored)
    copy.start()
    rows = third.shape[0]
    moved = dot(gather[...], stack([third[...], from_a[...]])).astype(BF16)
    left = beside([moved[q * rows : (q + 1) * rows] for q in range(27)])
    partial[...] = dot(left, kernel[...].reshape(27 * 256, 256))
    copy.wait()


def faces_three_kernel(gather, partial, from_b, kernel, mask_three, out):
    rows = from_b.shape[0]
    odd = on_odd_place()
    far = face_part(gather[...], from_b[...], kernel, jnp.where(odd, 1, 0))
    low = partial[:rows] + jnp.where(odd, 0.0, far)
    high = partial[rows:] + jnp.where(odd, far, 0.0)
    low = jnp.maximum(low, 0.0) * mask_three[:rows]
    high = jnp.maximum(high, 0.0) * mask_three[rows:]
    row = iota((8, 256), 0)
    for n in range(rows // 8):
        near, past = low[8 * n : 8 * (n + 1)], high[8 * n : 8 * (n + 1)]
        out[2 * n] = jnp.where(row < 4, near, pltpu.roll(past, 4, 0)).astype(BF16)
        out[2 * n + 1] = jnp.where(row < 4, pltpu.roll(near, 4, 0), past).astype(BF16)


def level_two_picks():
    pick = np.zeros((432, 27), np.float32)
    for tap in range(27):
        for r in range(16):
            y, z = r // 4 + tap // 3 % 3 - 1, r % 4 + tap % 3 - 1
            pick[16 * tap + r, tap // 9 * 9 + 3 * (y // 4 + 1) + z // 4 + 1] = 16
    return jnp.asarray(pick, BF16)


def level_three_picks():
    pick = np.zeros((27 * 16, 27), np.float32)
    for tap in range(27):
        for r in range(16):
            x, y, z = [
                n + d - 1
                for n, d in (
                    (r // 8, tap // 9), (r // 2 % 2, tap // 3 % 3), (r % 2, tap % 3)
                )
            ]
            pick[16 * tap + r, 9 * (x // 2 + 1) + 3 * (y // 2 + 1) + z // 2 + 1] = 4
    return jnp.asarray(pick, BF16)


def child_rows():
    pick = np.zeros((128, 128), np.float32)
    for q in range(8):
        for r in range(16):
            x, y, z = [
                2 * n + (q >> s & 1) for n, s in ((r // 8, 2), (r // 2 % 2, 1), (r % 2, 0))
            ]
            pick[16 * q + r, 64 * (r // 4 % 2) + 16 * x + 4 * y + z] = 1
    return jnp.asarray(pick, BF16)


ANY = pl.BlockSpec(memory_space=pl.ANY)
VMEM = pl.BlockSpec(memory_space=pltpu.VMEM)
DMA = pltpu.SemaphoreType.DMA


def call(kernel, cost, out_shape, scratch, *args, remain=(), store=()):
    single = not isinstance(out_shape, tuple)
    outs = (out_shape,) if single else out_shape
    specs = tuple(ANY if n in store else VMEM for n in range(len(outs)))
    return pl.pallas_call(
        kernel,
        out_shape=out_shape,
        in_specs=[ANY if n in remain else VMEM for n in range(len(args))],
        out_specs=specs[0] if single else specs,
        scratch_shapes=scratch,
        compiler_params=pltpu.CompilerParams(vmem_limit_bytes=24 * 1024 * 1024),
        cost_estimate=pl.CostEstimate(
            flops=int(cost * 10**10), bytes_accessed=10**7, transcendentals=0
        ),
    )(*args)


def swaps(tiles, count):
    within, across = [], []
    for t in range(tiles):
        for m in range(count):
            if m ^ 1 < count:
                within.append((t * count + m, t * count + (m ^ 1)))
            other = ((m - 1) ^ 1) + 1 if m else -1
            if 0 <= other < count:
                across.append((t * count + m, t * count + other))
            elif t ^ 1 < tiles:
                across.append((t * count + m, (t ^ 1) * count + m))
    return within, across


def on_device(
    features,
    neighbours,
    occupancy,
    conv_one,
    first_reduce_kernel,
    conv_two,
    second_reduce_kernel,
    conv_three,
):
    axes = ("tiles", LINE)
    within, across = swaps(lax.axis_size("tiles"), lax.axis_size(LINE))
    count = features.shape[0]
    features = jnp.swapaxes(features, 1, 2)
    shape = jax.ShapeDtypeStruct

    def exchange(to_a, to_b):
        from_b = lax.ppermute(to_b, axes, across)
        return lax.ppermute(to_a, axes, within), from_b

    face = shape((count // 2, 64, 128), BF16)
    bits, pair_words, mask_two, mask_three = call(
        masks_kernel,
        0.3,
        (
            shape((4, count, 128), F32),
            shape((8, count, 128), jnp.int32),
            shape((4, 16 * count, 128), F32),
            shape((8 * count, 256), F32),
        ),
        [],
        occupancy,
    )
    from_a, from_b = exchange(*call(edges_kernel, 0.02, (face, face), [], features, bits))
    own_two, sides_two = call(
        level_two_tables_kernel,
        0.4,
        (
            shape((9 * 16 * count, 16 * count), BF16),
            shape((2, 9 * 16 * count, 16 * count), BF16),
        ),
        [],
        neighbours, level_two_picks(),
    )
    middle, taps, face_taps, reduce_taps, partial = call(
        outer_kernel,
        2.0,
        (
            shape((count, 3, 6, 16, 128), BF16),
            shape((9 * 128, 256), BF16),
            shape((9 * 128, 128), BF16),
            shape((256, 256), BF16),
            shape((4, count * 64, 128), F32),
        ),
        [
            pltpu.VMEM((4, count + 1, 64, 128), F32),
            pltpu.VMEM((count, 3, 4, 6, 16, 128), BF16),
            pltpu.VMEM((9 * 128, 256), BF16),
        ],
        neighbours, bits, features, conv_one, first_reduce_kernel,
    )
    plane = shape((16 * count, 128), BF16)
    planes = shape((2, 16 * count, 128), BF16)
    sums = pltpu.VMEM((count * 64, 128), F32)
    outer, outer_two, to_a, to_b = call(
        faces_one_kernel,
        1.5,
        (shape((count, 2, 64, 128), BF16), planes, plane, plane),
        [
            pltpu.VMEM((count + 1, 64, 128), F32),
            pltpu.VMEM((count, 3, 6, 16, 128), BF16),
            sums,
            sums,
        ],
        neighbours, from_a, from_b, face_taps, partial, reduce_taps, pair_words, mask_two,
    )
    from_a, from_b = exchange(to_a, to_b)

    first_level, inner_two = call(
        inner_kernel,
        0.05,
        (shape(features.shape, BF16), planes),
        [sums, sums],
        middle, taps, partial, outer, reduce_taps, pair_words, mask_two,
    )
    partial, first_level = call(
        own_two_kernel,
        1.0,
        (shape((4 * 16 * count, 128), F32), shape(features.shape, BF16)),
        [DMA(())],
        outer_two, inner_two, own_two, sides_two, from_a, conv_two, first_level,
        store=(1,),
    )
    face = shape((4 * count, 256), BF16)
    second_level, third, to_a, to_b = call(
        faces_two_kernel,
        0.9,
        (shape((count, 64, 128), BF16), shape((8 * count, 256), BF16), face, face),
        [],
        sides_two, child_rows(), partial, from_b, conv_two, second_reduce_kernel, mask_two,
        mask_three,
    )
    from_a, from_b = exchange(to_a, to_b)

    own_three, far_three = call(
        level_three_tables_kernel,
        0.02,
        (shape((27 * 8 * count, 12 * count), BF16), shape((9 * 4 * count, 4 * count), BF16)),
        [],
        neighbours, level_three_picks(), third,
    )
    partial, second_level = call(
        own_three_kernel,
        1.0,
        (shape((8 * count, 256), F32), shape(second_level.shape, BF16)),
        [DMA(())],
        own_three, third, from_a, conv_three, second_level,
        store=(1,),
    )
    third_level = call(
        faces_three_kernel,
        1,
        shape((count, 8, 256), BF16),
        [],
        far_three, partial, from_b, conv_three, mask_three,
    )
    return jnp.swapaxes(first_level, 1, 2), second_level, third_level


def solution(mesh):
    split = P(("tiles", LINE))
    return jax.shard_map(
        on_device,
        mesh=mesh,
        in_specs=(split, split, split, P(), P(), P(), P(), P()),
        out_specs=(split, split, split),
        check_vma=False,
    )
```

```python
import jax
import jax.numpy as jnp
import numpy as np
from jax import lax
from jax.experimental import pallas as pl
from jax.experimental.pallas import tpu as pltpu
from jax.sharding import PartitionSpec as P

F32 = jnp.float32
BF16 = jnp.bfloat16
LINE = "morton"


def dot(x, y):
    return jnp.dot(x, y, preferred_element_type=F32)


def iota(shape, axis):
    return lax.broadcasted_iota(jnp.int32, shape, axis)


def stack(parts):
    return jnp.concatenate(parts, axis=0)


def beside(parts):
    return jnp.concatenate(parts, axis=1)


def bits_of(words, shift):
    return jnp.bitwise_and(lax.shift_right_logical(words, shift), 1).astype(F32)


def either(x, y):
    return jnp.bitwise_or(x, y)


def on_odd_place():
    return lax.rem(lax.axis_index(LINE), 2) == 1


def word_lanes(words, w):
    return jnp.broadcast_to(words[:, w : w + 1], (words.shape[0], 128))


def column_bits(words, column):
    lane = iota((words.shape[0], 128), 1)
    w = [word_lanes(words, 4 * column + q) for q in range(4)]
    chosen = jnp.where(
        lane < 64, jnp.where(lane < 32, w[0], w[1]), jnp.where(lane < 96, w[2], w[3])
    )
    return bits_of(chosen, jnp.bitwise_and(lane, 31))


def slot_numbers(neighbours):
    count = neighbours.shape[0]
    number = neighbours[...]
    tap = iota(number.shape, 1)
    shift = jnp.where(tap < 9, count, jnp.where(tap < 18, 0, -count))
    return jnp.where(number < 0, count, number + shift - lax.axis_index(LINE) * count)


def masks_kernel(occupancy, bits, pair_words, mask_two, mask_three):
    count = occupancy.shape[0]
    for q in range(4):
        bits[q] = column_bits(occupancy[...], q)
    words = [word_lanes(occupancy[...], w) for w in range(16)]
    lane = iota((count, 128), 1)
    row = iota((8, 128), 0)
    any_two = []
    for i in range(4):
        for half in range(2):
            low, high = words[4 * i + half], words[4 * i + 2 + half]
            pair_words[2 * i + half] = jnp.where(lane < 64, low, high)
            word = either(low, high)
            word = either(word, lax.shift_right_logical(word, 1))
            any_two.append(either(word, lax.shift_right_logical(word, 8)))
    two_shift = 16 * lax.shift_right_logical(row, 2) + 2 * jnp.bitwise_and(row, 3)
    for i in range(4):
        for b in range(count):
            mask_two[i, 16 * b : 16 * (b + 1)] = stack(
                [
                    bits_of(
                        jnp.broadcast_to(any_two[2 * i + half][b : b + 1], (8, 128)), two_shift
                    )
                    for half in range(2)
                ]
            )
    any_three = []
    for i in range(2):
        for j in range(2):
            word = either(any_two[4 * i + j], any_two[4 * i + 2 + j])
            word = either(word, lax.shift_right_logical(word, 16))
            any_three.append(either(word, lax.shift_right_logical(word, 2)))
    for i in range(2):
        for b in range(0, count, 2):
            tile = [
                jnp.broadcast_to(any_three[2 * i + j][n : n + 1], (8, 128))
                for n in (b, b + 1)
                for j in range(2)
            ]
            tile = jnp.where(
                row < 4, jnp.where(row < 2, tile[0], tile[1]), jnp.where(row < 6, tile[2], tile[3])
            )
            mask = bits_of(tile, 4 * jnp.bitwise_and(row, 1))
            at = 4 * (count * i + b)
            mask_three[at : at + 8] = beside([mask, mask])


def edges_kernel(features, bits, edge, *, near):
    last = features.shape[2] - 128
    lane = iota((64, 128), 1)
    low_wanted = on_odd_place() == near
    for q in range(features.shape[0] // 2):
        low, high = [
            [
                features[b, :, column * last : column * last + 128].astype(F32)
                * bits[3 * column, b : b + 1]
                for b in (2 * q, 2 * q + 1)
            ]
            for column in range(2)
        ]
        lows = jnp.where(lane < 64, low[0], pltpu.roll(low[1], 64, 1))
        highs = jnp.where(lane < 64, pltpu.roll(high[0], 64, 1), high[1])
        edge[q] = jnp.where(low_wanted, lows, highs).astype(BF16)


def far_edge_kernel(features, bits, edge):
    edges_kernel(features, bits, edge, near=False)


def near_edge_kernel(features, bits, earlier, edge):
    edges_kernel(features, bits, edge, near=True)


def near_face_kernel(planes, earlier, face):
    rows = face.shape[0]
    begin = pl.multiple_of(jnp.where(on_odd_place(), 0, rows), rows)
    face[...] = planes[pl.ds(begin, rows), :]


def slot_rows(neighbours):
    count = neighbours.shape[0]
    slot = jnp.where(neighbours[...] < 0, 4 * count, slot_numbers(neighbours)).astype(F32)
    return stack(
        [jnp.broadcast_to(slot[b : b + 1], (128, slot.shape[1])) for b in range(count)]
    ).astype(BF16)


def times_transposed(x, y):
    return lax.dot_general(x, y, (((1,), (1,)), ((), ())), preferred_element_type=F32)


def level_two_tables_kernel(neighbours, pick, own_two, sides_two):
    count = neighbours.shape[0]
    rows = times_transposed(pick[...], slot_rows(neighbours))
    lane = iota((16, 16 * count), 1)
    row = iota((16, 16 * count), 0)
    j, k = lax.shift_right_logical(row, 2), jnp.bitwise_and(row, 3)
    for q in range(9):
        source = 4 * jnp.bitwise_and(j + q // 3 + 3, 3) + jnp.bitwise_and(k + q % 3 + 3, 3)
        wanted = (lane - source).astype(F32)
        for a, table in enumerate((sides_two.at[0], own_two, sides_two.at[1])):
            at = 16 * (9 * a + q)
            for b in range(count):
                table[16 * (count * q + b) : 16 * (count * q + b + 1), :] = jnp.where(
                    rows[at : at + 16, 128 * b : 128 * b + 16 * count] == wanted, 1.0, 0.0
                ).astype(BF16)


def level_three_tables_kernel(neighbours, pick, later, own_three, far_three):
    count = neighbours.shape[0]
    odd = on_odd_place()
    rows = times_transposed(pick[...], slot_rows(neighbours))
    row = iota((8, 128), 0)
    lane = iota((8, 128), 1)
    j, k = [jnp.bitwise_and(lax.shift_right_logical(row, n), 1) for n in (1, 0)]

    def block(tap, i, begin):
        c, e = tap // 3 % 3, tap % 3
        source = 2 * jnp.bitwise_and(j + c + 1, 1) + jnp.bitwise_and(k + e + 1, 1)
        wanted = (lane - source - begin).astype(F32)
        at = 8 * (2 * tap + i)
        tiles = []
        for b in range(0, count, 2):
            first, second = [rows[at : at + 8, 128 * n : 128 * (n + 1)] for n in (b, b + 1)]
            hit = jnp.where(row < 4, first, second) == wanted
            tiles.append(jnp.where(hit, 1.0, 0.0))
        return stack(tiles)

    nowhere = 16 * 4 * count
    for tap in range(27):
        for i in range(2):
            x = i + tap // 9 - 1
            if x < 0:
                begin = jnp.where(odd, 8 * count, nowhere)
            elif x > 1:
                begin = jnp.where(odd, nowhere, 8 * count)
            else:
                begin = 4 * count * x
            at = 8 * count * tap + 4 * count * i
            own_three[at : at + 4 * count, :] = block(tap, i, begin)[:, : 12 * count].astype(BF16)
    for q in range(9):
        tile = jnp.where(odd, block(18 + q, 1, 0), block(q, 0, 0))
        far_three[4 * count * q : 4 * count * (q + 1), :] = tile[:, : 4 * count].astype(BF16)


def shifted_windows(source, row):
    shifted = []
    for j in range(-1, 9):
        c, at = (0, 7) if j < 0 else (2, 0) if j > 7 else (1, j)
        left, mid, right = [source(3 * c + e, at) for e in range(3)]
        shifted.append(
            (
                pltpu.roll(jnp.where(row == 7, left, mid), 1, 0),
                mid,
                pltpu.roll(jnp.where(row == 0, right, mid), 7, 0),
            )
        )
    return [
        [stack([shifted[jr][e], shifted[jr + 4][e]]).astype(BF16) for e in range(3)]
        for jr in range(6)
    ]


def outer_kernel(
    neighbours, bits, features, kernel, reduce,
    middle, taps, face_taps, reduce_taps, partial,
    tables, windows, wrap_taps,
):
    count = features.shape[0]
    lane = iota((64, 128), 1)
    row = iota((8, 128), 0)
    numbers = slot_numbers(neighbours)

    none = jnp.zeros((64, 64), F32)
    for q in range(9):
        w = [kernel[9 * a + q].astype(F32) for a in range(3)]
        rows = slice(q * 128, (q + 1) * 128)
        taps[rows, :] = stack(
            [beside([w[2], w[1], w[0], none]), beside([none, w[2], w[1], w[0]])]
        ).astype(BF16)
        wrap_taps[rows, :] = stack(
            [beside([w[2], w[1], none, none]), beside([none, none, w[1], w[0]])]
        ).astype(BF16)
        face_taps[rows, :] = stack([beside([w[0], none]), beside([none, w[2]])]).astype(BF16)

    reduce_taps[...] = stack(
        [
            beside([reduce[4 * ci + 2 * cj], reduce[4 * ci + 2 * cj + 1]])
            for cj in range(2)
            for ci in range(2)
        ]
    )

    for pair in range(4):
        tables[pair, count] = jnp.zeros((64, 128), F32)
    for b in range(count):
        cols = [
            features[b, :, 128 * q : 128 * (q + 1)].astype(F32) * bits[q, b : b + 1]
            for q in range(4)
        ]
        rolled = [pltpu.roll(col, 64, 1) for col in cols]
        for p in (0, 2):
            m = stack(
                [
                    jnp.where(lane < 64, rolled[p], cols[p + 1]),
                    jnp.where(lane < 64, cols[p + 1], rolled[(p + 2) % 4]),
                ]
            ).T
            tables[p, b] = m[:64]
            tables[p + 1, b] = m[64:]

    for b in range(count):
        slot = [numbers[b, 9 + q] for q in range(9)]
        for pair in range(4):
            tiles = shifted_windows(lambda q, j: tables[pair, slot[q], pl.ds(8 * j, 8), :], row)
            for jr in range(6):
                for e in range(3):
                    if pair == 1:
                        middle[b, e, jr] = tiles[jr][e]
                    else:
                        windows[b, e, pair, jr] = tiles[jr][e]

    group = count // 2
    for g in range(2):
        bricks = slice(g * group, (g + 1) * group)
        rows = slice(g * group * 64, (g + 1) * group * 64)
        low, high, wrap = [
            dot(
                beside(
                    [
                        windows[bricks, e, pair, c : c + 4].reshape(group * 64, 128)
                        for c in range(3)
                        for e in range(3)
                    ]
                ),
                weights[...],
            )
            for pair, weights in ((0, taps), (2, taps), (3, wrap_taps))
        ]
        partial[0, rows] = low[:, :128] + wrap[:, 128:]
        partial[1, rows] = low[:, 128:]
        partial[2, rows] = high[:, :128]
        partial[3, rows] = high[:, 128:] + wrap[:, :128]


def masked_tiles(sums, pair_words, b, i):
    row = iota((8, 128), 0)
    tiles = {}
    for half in range(2):
        words = jnp.broadcast_to(pair_words[2 * i + half, b : b + 1, :], (8, 128))
        for jr in range(4):
            at = jr * 16 + half * 8
            tiles[4 * half + jr] = jnp.maximum(sums[at : at + 8], 0.0) * bits_of(
                words, row + 8 * jr
            )
    return [tiles[j] for j in range(8)]


def reduce_planes(groups, weights, low_sums, high_sums):
    left = stack(
        [beside([tiles[j], tiles[j + 1]]) for tiles in groups for j in (0, 2, 4, 6)]
    ).astype(BF16)
    sums = dot(left, weights[...])
    low_sums[...] = sums[:, :128]
    high_sums[...] = sums[:, 128:]
    return [
        low_sums[pl.ds(32 * g, 16, stride=2), :] + high_sums[pl.ds(32 * g + 1, 16, stride=2), :]
        for g in range(len(groups))
    ]


def faces_one_kernel(
    neighbours, from_a, from_b, face_taps, partial, reduce, pair_words, mask_two,
    outer, second, to_b,
    halo, windows, low_sums, high_sums,
):
    count = outer.shape[0]
    lane = iota((64, 128), 1)
    small = iota((8, 128), 1)
    row = iota((8, 128), 0)
    odd = on_odd_place()
    slot = slot_numbers(neighbours)
    halo[count] = jnp.zeros((64, 128), F32)
    for q in range(count // 2):
        one, two = from_a[q].astype(F32), from_b[q].astype(F32)
        m = stack([jnp.where(odd, one, two), jnp.where(odd, two, one)]).T
        halo[2 * q] = m[:64]
        halo[2 * q + 1] = m[64:]
    for b in range(count):
        low = [slot[b, q] for q in range(9)]
        high = [slot[b, 18 + q] for q in range(9)]

        def source(q, j):
            rows = pl.ds(8 * j, 8)
            return jnp.where(small < 64, halo[low[q], rows, :], halo[high[q], rows, :])

        tiles = shifted_windows(source, row)
        for jr in range(6):
            for e in range(3):
                windows[b, e, jr] = tiles[jr][e]
    added = dot(
        beside(
            [
                windows[:, e, c : c + 4].reshape(count * 64, 128)
                for c in range(3)
                for e in range(3)
            ]
        ),
        face_taps[...],
    )
    groups = []
    for b in range(count):
        at = slice(64 * b, 64 * (b + 1))
        for side in range(2):
            near = (lane < 64) == (side == 0)
            sums = partial[3 * side, at] + jnp.where(near, added[at], 0.0)
            groups.append(masked_tiles(sums, pair_words, b, 3 * side))
            outer[b, side] = stack(groups[-1]).astype(BF16)
    sums = reduce_planes(groups, reduce, low_sums, high_sums)
    for b in range(count):
        at = slice(16 * b, 16 * (b + 1))
        planes = [
            (jnp.maximum(sums[2 * b + side], 0.0) * mask_two[3 * side, at]).astype(BF16)
            for side in range(2)
        ]
        second[16 * b : 16 * (b + 1)] = planes[0]
        second[16 * (count + b) : 16 * (count + b + 1)] = planes[1]
        to_b[at] = jnp.where(odd, planes[1], planes[0])


def inner_kernel(
    middle, taps, partial, outer, reduce, pair_words, mask_two,
    out, second,
    low_sums, high_sums,
):
    count = middle.shape[0]
    lane = iota((64, 128), 1)
    added = dot(
        beside(
            [
                middle[:, e, c : c + 4].reshape(count * 64, 128)
                for c in range(3)
                for e in range(3)
            ]
        ),
        taps[...],
    )
    groups = []
    for b in range(count):
        for i in (1, 2):
            at = slice(64 * b, 64 * (b + 1))
            sums = partial[i, at] + added[at, 128 * (i - 1) : 128 * i]
            groups.append(masked_tiles(sums, pair_words, b, i))
        ordered = [
            outer[b, 0].astype(F32),
            stack(groups[2 * b]),
            stack(groups[2 * b + 1]),
            outer[b, 1].astype(F32),
        ]
        for i in (0, 2):
            m = stack(ordered[i : i + 2]).T
            top, bottom = m[:64], m[64:]
            out[b, :, 128 * i : 128 * (i + 1)] = jnp.where(
                lane < 64, top, pltpu.roll(bottom, 64, 1)
            ).astype(BF16)
            out[b, :, 128 * (i + 1) : 128 * (i + 2)] = jnp.where(
                lane < 64, pltpu.roll(top, 64, 1), bottom
            ).astype(BF16)
    sums = reduce_planes(groups, reduce, low_sums, high_sums)
    for b in range(count):
        at = slice(16 * b, 16 * (b + 1))
        for i in (1, 2):
            second[i - 1, at] = (
                jnp.maximum(sums[2 * b + i - 1], 0.0) * mask_two[i, at]
            ).astype(BF16)


def face_part(gather, face, kernel, high):
    moved = dot(gather, face).astype(BF16)
    rows = moved.shape[0] // 9
    left = beside([moved[q * rows : (q + 1) * rows] for q in range(9)])
    weights = kernel[pl.ds(18 * high, 9)]
    return dot(left, weights.reshape(9 * weights.shape[1], weights.shape[2]))


def own_two_kernel(
    outer, inner, own_gather, gathers, from_a, kernel, first,
    partial, result, stored,
):
    copy = pltpu.make_async_copy(first, result, stored)
    copy.start()
    rows = inner.shape[1]
    planes = beside([outer[:rows], inner[0], inner[1], outer[rows:]])
    moved = dot(own_gather[...], planes).astype(BF16)
    left = beside(
        [
            stack(
                [
                    moved[q * rows : (q + 1) * rows, 128 * i : 128 * (i + 1)]
                    for i in range(4)
                ]
            )
            for q in range(9)
        ]
    )
    weights = [kernel[9 * a : 9 * (a + 1)].reshape(9 * 128, 128) for a in range(3)]
    sums = dot(left, beside(weights[:2]))
    later = dot(left[rows:], weights[2])
    high = jnp.where(on_odd_place(), 0, 1)
    near = face_part(gathers[high], from_a[...], kernel, high)
    for i in range(4):
        total = sums[i * rows : (i + 1) * rows, 128:]
        if i:
            total = total + sums[(i - 1) * rows : i * rows, :128]
        if i < 3:
            total = total + later[i * rows : (i + 1) * rows]
        if i in (0, 3):
            total = total + jnp.where(high == i // 3, near, 0.0)
        partial[i * rows : (i + 1) * rows] = total
    copy.wait()


def faces_two_kernel(
    gathers, children, partial, from_b, kernel, reduce, mask_two, mask_three,
    second, third, to_b,
):
    count = second.shape[0]
    rows = 16 * count
    odd = on_odd_place()
    high = jnp.where(odd, 1, 0)
    far = face_part(gathers[high], from_b[...], kernel, high)
    planes = []
    for i in range(4):
        sums = partial[i * rows : (i + 1) * rows]
        if i in (0, 3):
            sums = sums + jnp.where(high == i // 3, far, 0.0)
        planes.append((jnp.maximum(sums, 0.0) * mask_two[i]).astype(BF16))
    bricks = [
        stack([planes[i][16 * b : 16 * (b + 1)] for i in range(4)]) for b in range(count)
    ]
    for b in range(count):
        second[b] = bricks[b]
    moved = dot(
        children[...], beside([stack(bricks[b : b + 2]) for b in range(0, count, 2)])
    )
    left = beside(
        [
            stack(
                [
                    moved[16 * q + 8 * i : 16 * q + 8 * (i + 1), 128 * n : 128 * (n + 1)]
                    for i in range(2)
                    for n in range(count // 2)
                ]
            )
            for q in range(8)
        ]
    ).astype(BF16)
    sums = dot(left, reduce[...].reshape(8 * 128, 256))
    value = jnp.maximum(sums, 0.0) * mask_three[...]
    third[...] = value.astype(BF16)
    low, high = value[: 4 * count], value[4 * count :]
    to_b[...] = jnp.where(odd, high, low).astype(BF16)


def own_three_kernel(gather, third, from_a, kernel, second, partial, result, stored):
    copy = pltpu.make_async_copy(second, result, stored)
    copy.start()
    rows = third.shape[0]
    moved = dot(gather[...], stack([third[...], from_a[...]])).astype(BF16)
    left = beside([moved[q * rows : (q + 1) * rows] for q in range(27)])
    partial[...] = dot(left, kernel[...].reshape(27 * 256, 256))
    copy.wait()


def faces_three_kernel(gather, partial, from_b, kernel, mask_three, out):
    rows = from_b.shape[0]
    odd = on_odd_place()
    far = face_part(gather[...], from_b[...], kernel, jnp.where(odd, 1, 0))
    low = partial[:rows] + jnp.where(odd, 0.0, far)
    high = partial[rows:] + jnp.where(odd, far, 0.0)
    low = jnp.maximum(low, 0.0) * mask_three[:rows]
    high = jnp.maximum(high, 0.0) * mask_three[rows:]
    row = iota((8, 256), 0)
    for n in range(rows // 8):
        near, past = low[8 * n : 8 * (n + 1)], high[8 * n : 8 * (n + 1)]
        out[2 * n] = jnp.where(row < 4, near, pltpu.roll(past, 4, 0)).astype(BF16)
        out[2 * n + 1] = jnp.where(row < 4, pltpu.roll(near, 4, 0), past).astype(BF16)


def level_two_picks():
    pick = np.zeros((432, 27), np.float32)
    for tap in range(27):
        for r in range(16):
            y, z = r // 4 + tap // 3 % 3 - 1, r % 4 + tap % 3 - 1
            pick[16 * tap + r, tap // 9 * 9 + 3 * (y // 4 + 1) + z // 4 + 1] = 16
    return jnp.asarray(pick, BF16)


def level_three_picks():
    pick = np.zeros((27 * 16, 27), np.float32)
    for tap in range(27):
        for r in range(16):
            x, y, z = [
                n + d - 1
                for n, d in (
                    (r // 8, tap // 9), (r // 2 % 2, tap // 3 % 3), (r % 2, tap % 3)
                )
            ]
            pick[16 * tap + r, 9 * (x // 2 + 1) + 3 * (y // 2 + 1) + z // 2 + 1] = 4
    return jnp.asarray(pick, BF16)


def child_rows():
    pick = np.zeros((128, 128), np.float32)
    for q in range(8):
        for r in range(16):
            x, y, z = [
                2 * n + (q >> s & 1) for n, s in ((r // 8, 2), (r // 2 % 2, 1), (r % 2, 0))
            ]
            pick[16 * q + r, 64 * (r // 4 % 2) + 16 * x + 4 * y + z] = 1
    return jnp.asarray(pick, BF16)


ANY = pl.BlockSpec(memory_space=pl.ANY)
VMEM = pl.BlockSpec(memory_space=pltpu.VMEM)
DMA = pltpu.SemaphoreType.DMA


def call(kernel, cost, out_shape, scratch, *args, remain=(), store=()):
    single = not isinstance(out_shape, tuple)
    outs = (out_shape,) if single else out_shape
    specs = tuple(ANY if n in store else VMEM for n in range(len(outs)))
    return pl.pallas_call(
        kernel,
        out_shape=out_shape,
        in_specs=[ANY if n in remain else VMEM for n in range(len(args))],
        out_specs=specs[0] if single else specs,
        scratch_shapes=scratch,
        compiler_params=pltpu.CompilerParams(vmem_limit_bytes=24 * 1024 * 1024),
        cost_estimate=pl.CostEstimate(
            flops=int(cost * 10**10), bytes_accessed=10**7, transcendentals=0
        ),
    )(*args)


def swaps(tiles, count):
    within, across = [], []
    for t in range(tiles):
        for m in range(count):
            if m ^ 1 < count:
                within.append((t * count + m, t * count + (m ^ 1)))
            other = ((m - 1) ^ 1) + 1 if m else -1
            if 0 <= other < count:
                across.append((t * count + m, t * count + other))
            elif t ^ 1 < tiles:
                across.append((t * count + m, (t ^ 1) * count + m))
    return within, across


def on_device(
    features,
    neighbours,
    occupancy,
    conv_one,
    first_reduce_kernel,
    conv_two,
    second_reduce_kernel,
    conv_three,
):
    axes = ("tiles", LINE)
    within, across = swaps(lax.axis_size("tiles"), lax.axis_size(LINE))
    count = features.shape[0]
    features = jnp.swapaxes(features, 1, 2)
    shape = jax.ShapeDtypeStruct

    def exchange(to_a, to_b):
        from_b = lax.ppermute(to_b, axes, across)
        return lax.ppermute(to_a, axes, within), from_b

    face = shape((count // 2, 64, 128), BF16)
    bits, pair_words, mask_two, mask_three = call(
        masks_kernel,
        0.3,
        (
            shape((4, count, 128), F32),
            shape((8, count, 128), jnp.int32),
            shape((4, 16 * count, 128), F32),
            shape((8 * count, 256), F32),
        ),
        [],
        occupancy,
    )
    to_b = call(far_edge_kernel, 0.02, face, [], features, bits)
    to_a = call(near_edge_kernel, 0.02, face, [], features, bits, to_b)
    from_a, from_b = exchange(to_a, to_b)
    own_two, sides_two = call(
        level_two_tables_kernel,
        0.4,
        (
            shape((9 * 16 * count, 16 * count), BF16),
            shape((2, 9 * 16 * count, 16 * count), BF16),
        ),
        [],
        neighbours, level_two_picks(),
    )
    middle, taps, face_taps, reduce_taps, partial = call(
        outer_kernel,
        2.0,
        (
            shape((count, 3, 6, 16, 128), BF16),
            shape((9 * 128, 256), BF16),
            shape((9 * 128, 128), BF16),
            shape((256, 256), BF16),
            shape((4, count * 64, 128), F32),
        ),
        [
            pltpu.VMEM((4, count + 1, 64, 128), F32),
            pltpu.VMEM((count, 3, 4, 6, 16, 128), BF16),
            pltpu.VMEM((9 * 128, 256), BF16),
        ],
        neighbours, bits, features, conv_one, first_reduce_kernel,
    )
    plane = shape((16 * count, 128), BF16)
    planes = shape((2, 16 * count, 128), BF16)
    sums = pltpu.VMEM((count * 64, 128), F32)
    outer, outer_two, to_b = call(
        faces_one_kernel,
        1.5,
        (shape((count, 2, 64, 128), BF16), shape((2 * 16 * count, 128), BF16), plane),
        [
            pltpu.VMEM((count + 1, 64, 128), F32),
            pltpu.VMEM((count, 3, 6, 16, 128), BF16),
            sums,
            sums,
        ],
        neighbours, from_a, from_b, face_taps, partial, reduce_taps, pair_words, mask_two,
    )
    to_a = call(near_face_kernel, 0.02, plane, [], outer_two, to_b)
    from_a, from_b = exchange(to_a, to_b)

    first_level, inner_two = call(
        inner_kernel,
        0.05,
        (shape(features.shape, BF16), planes),
        [sums, sums],
        middle, taps, partial, outer, reduce_taps, pair_words, mask_two,
    )
    partial, first_level = call(
        own_two_kernel,
        1.0,
        (shape((4 * 16 * count, 128), F32), shape(features.shape, BF16)),
        [DMA(())],
        outer_two, inner_two, own_two, sides_two, from_a, conv_two, first_level,
        store=(1,),
    )
    face = shape((4 * count, 256), BF16)
    second_level, third, to_b = call(
        faces_two_kernel,
        0.9,
        (shape((count, 64, 128), BF16), shape((8 * count, 256), BF16), face),
        [],
        sides_two, child_rows(), partial, from_b, conv_two, second_reduce_kernel, mask_two,
        mask_three,
    )
    to_a = call(near_face_kernel, 0.02, face, [], third, to_b)
    from_a, from_b = exchange(to_a, to_b)

    own_three, far_three = call(
        level_three_tables_kernel,
        0.02,
        (shape((27 * 8 * count, 12 * count), BF16), shape((9 * 4 * count, 4 * count), BF16)),
        [],
        neighbours, level_three_picks(), third,
    )
    partial, second_level = call(
        own_three_kernel,
        1.0,
        (shape((8 * count, 256), F32), shape(second_level.shape, BF16)),
        [DMA(())],
        own_three, third, from_a, conv_three, second_level,
        store=(1,),
    )
    third_level = call(
        faces_three_kernel,
        1,
        shape((count, 8, 256), BF16),
        [],
        far_three, partial, from_b, conv_three, mask_three,
    )
    return jnp.swapaxes(first_level, 1, 2), second_level, third_level


def solution(mesh):
    split = P(("tiles", LINE))
    return jax.shard_map(
        on_device,
        mesh=mesh,
        in_specs=(split, split, split, P(), P(), P(), P(), P()),
        out_specs=(split, split, split),
        check_vma=False,
    )
```

```python
import jax
import jax.numpy as jnp
import numpy as np
from jax import lax
from jax.experimental import pallas as pl
from jax.experimental.pallas import tpu as pltpu
from jax.sharding import PartitionSpec as P

F32 = jnp.float32
BF16 = jnp.bfloat16
LINE = "morton"


def dot(x, y):
    return jnp.dot(x, y, preferred_element_type=F32)


def iota(shape, axis):
    return lax.broadcasted_iota(jnp.int32, shape, axis)


def stack(parts):
    return jnp.concatenate(parts, axis=0)


def beside(parts):
    return jnp.concatenate(parts, axis=1)


def bits_of(words, shift):
    return jnp.bitwise_and(lax.shift_right_logical(words, shift), 1).astype(F32)


def either(x, y):
    return jnp.bitwise_or(x, y)


def on_odd_place():
    return lax.rem(lax.axis_index(LINE), 2) == 1


def word_lanes(words, w):
    return jnp.broadcast_to(words[:, w : w + 1], (words.shape[0], 128))


def column_bits(words, column):
    lane = iota((words.shape[0], 128), 1)
    w = [word_lanes(words, 4 * column + q) for q in range(4)]
    chosen = jnp.where(
        lane < 64, jnp.where(lane < 32, w[0], w[1]), jnp.where(lane < 96, w[2], w[3])
    )
    return bits_of(chosen, jnp.bitwise_and(lane, 31))


def slot_numbers(neighbours):
    count = neighbours.shape[0]
    number = neighbours[...]
    tap = iota(number.shape, 1)
    shift = jnp.where(tap < 9, count, jnp.where(tap < 18, 0, -count))
    return jnp.where(number < 0, count, number + shift - lax.axis_index(LINE) * count)


def blank_kernel(notes):
    notes[...] = jnp.zeros(notes.shape, F32)


def masks_kernel(occupancy, blank, bits, edge_bits, pair_words, mask_two, mask_three):
    count = occupancy.shape[0]
    for q in range(4):
        bits[q] = column_bits(occupancy[...], q)
    words = [word_lanes(occupancy[...], w) for w in range(16)]
    lane = iota((count, 128), 1)
    row = iota((8, 128), 0)
    any_two = []
    for i in range(4):
        for half in range(2):
            low, high = words[4 * i + half], words[4 * i + 2 + half]
            pair_words[2 * i + half] = jnp.where(lane < 64, low, high)
            word = either(low, high)
            word = either(word, lax.shift_right_logical(word, 1))
            any_two.append(either(word, lax.shift_right_logical(word, 8)))
    two_shift = 16 * lax.shift_right_logical(row, 2) + 2 * jnp.bitwise_and(row, 3)
    for i in range(4):
        for b in range(count):
            mask_two[i, 16 * b : 16 * (b + 1)] = stack(
                [
                    bits_of(
                        jnp.broadcast_to(any_two[2 * i + half][b : b + 1], (8, 128)), two_shift
                    )
                    for half in range(2)
                ]
            )
    plane, half, m = [jnp.bitwise_and(lax.shift_right_logical(lane, n), 1) for n in (4, 3, 2)]
    for side in range(2):
        word = [any_two[4 * side + n] for n in range(4)]
        word = jnp.where(
            plane == 0, jnp.where(half == 0, word[0], word[1]), jnp.where(half == 0, word[2], word[3])
        )
        edge_bits[side] = bits_of(word, 16 * m + 2 * jnp.bitwise_and(lane, 3))
    any_three = []
    for i in range(2):
        for j in range(2):
            word = either(any_two[4 * i + j], any_two[4 * i + 2 + j])
            word = either(word, lax.shift_right_logical(word, 16))
            any_three.append(either(word, lax.shift_right_logical(word, 2)))
    for i in range(2):
        for b in range(0, count, 2):
            tile = [
                jnp.broadcast_to(any_three[2 * i + j][n : n + 1], (8, 128))
                for n in (b, b + 1)
                for j in range(2)
            ]
            tile = jnp.where(
                row < 4, jnp.where(row < 2, tile[0], tile[1]), jnp.where(row < 6, tile[2], tile[3])
            )
            mask = bits_of(tile, 4 * jnp.bitwise_and(row, 1))
            at = 4 * (count * i + b)
            mask_three[at : at + 8] = beside([mask, mask])


def edge_planes(features, bits, low_wanted):
    last = features.shape[2] - 128
    lane = iota((64, 128), 1)
    planes = []
    for q in range(features.shape[0] // 2):
        low, high = [
            [
                features[b, :, column * last : column * last + 128].astype(F32)
                * bits[3 * column, b : b + 1]
                for b in (2 * q, 2 * q + 1)
            ]
            for column in range(2)
        ]
        lows = jnp.where(lane < 64, low[0], pltpu.roll(low[1], 64, 1))
        highs = jnp.where(lane < 64, pltpu.roll(high[0], 64, 1), high[1])
        planes.append(jnp.where(low_wanted, lows, highs).astype(BF16))
    return planes


def far_edge_kernel(features, bits, neighbours, edge_bits, blank, edge, notes):
    count = features.shape[0]
    odd = on_odd_place()
    for q, plane in enumerate(edge_planes(features, bits, jnp.logical_not(odd))):
        edge[64 * q : 64 * (q + 1), :] = plane
    notes[...] = blank[...]
    notes[:count, : neighbours.shape[1]] = jnp.where(
        neighbours[...] < 0, 4 * count, slot_numbers(neighbours)
    ).astype(F32)
    notes[count:, :] = edge_bits[jnp.where(odd, 1, 0)]
    edge[32 * count :, :] = notes[...].astype(BF16)


def near_edge_kernel(features, bits, earlier, edge):
    for q, plane in enumerate(edge_planes(features, bits, on_odd_place())):
        edge[q] = plane


def near_face_kernel(planes, earlier, face):
    rows = face.shape[0]
    begin = pl.multiple_of(jnp.where(on_odd_place(), 0, rows), rows)
    face[...] = planes[pl.ds(begin, rows), :]


def slot_rows(slot):
    return stack(
        [jnp.broadcast_to(slot[b : b + 1], (128, slot.shape[1])) for b in range(slot.shape[0])]
    ).astype(BF16)


def own_slot_rows(neighbours):
    slot = jnp.where(neighbours[...] < 0, 4 * neighbours.shape[0], slot_numbers(neighbours))
    return slot_rows(slot.astype(F32))


def times_transposed(x, y):
    return lax.dot_general(x, y, (((1,), (1,)), ((), ())), preferred_element_type=F32)


def fill_level_two_tables(tables, rows, count):
    lane = iota((16, 16 * count), 1)
    row = iota((16, 16 * count), 0)
    j, k = lax.shift_right_logical(row, 2), jnp.bitwise_and(row, 3)
    for q in range(9):
        source = 4 * jnp.bitwise_and(j + q // 3 + 3, 3) + jnp.bitwise_and(k + q % 3 + 3, 3)
        wanted = (lane - source).astype(F32)
        for a, table in enumerate(tables):
            at = 16 * (9 * a + q)
            for b in range(count):
                table[16 * (count * q + b) : 16 * (count * q + b + 1), :] = jnp.where(
                    rows[at : at + 16, 128 * b : 128 * b + 16 * count] == wanted, 1.0, 0.0
                ).astype(BF16)


def level_two_tables_kernel(neighbours, pick, later, own_two, sides_two):
    rows = times_transposed(pick[...], own_slot_rows(neighbours))
    fill_level_two_tables(
        (sides_two.at[0], own_two, sides_two.at[1]), rows, neighbours.shape[0]
    )


def far_tables_kernel(message, pick, later, own_two, toward_two, mask_two, mask_three):
    count = own_two.shape[1] // 16
    notes = message[32 * count :, :].astype(F32)
    slots = slot_rows(notes[:count, : pick.shape[1]])
    begin = pl.multiple_of(jnp.where(on_odd_place(), 0, 288), 16)
    rows = stack(
        [
            times_transposed(pick[pl.ds(begin, 144), :], slots),
            times_transposed(pick[144:288, :], slots),
        ]
    )
    fill_level_two_tables((toward_two, own_two), rows, count)

    every = jnp.ones((128, 256), BF16)
    lane = iota((16, 128), 1)
    row = iota((16, 128), 0)
    bits = [notes[count + b : count + b + 1] for b in range(count)]
    chosen = stack(
        [
            jnp.where(lane == 16 * plane + row, jnp.broadcast_to(bits[b], (16, 128)), 0.0)
            for plane in range(2)
            for b in range(count)
        ]
    ).astype(BF16)
    mask_two[...] = dot(chosen, every[:, :128])
    lane, row = lane[:8], row[:8]
    child = jnp.bitwise_and(lax.shift_right_logical(lane, 2), 2) + jnp.bitwise_and(
        lax.shift_right_logical(lane, 1), 1
    )
    wanted = (child == jnp.bitwise_and(row, 3)) & (lane < 32)
    chosen = stack(
        [
            jnp.where(wanted, jnp.where(row < 4, bits[b], bits[b + 1]), 0.0)
            for b in range(0, count, 2)
        ]
    ).astype(BF16)
    mask_three[...] = jnp.where(dot(chosen, every) > 0.5, 1.0, 0.0)


def level_three_tables_kernel(neighbours, pick, later, own_three, near_three):
    count = neighbours.shape[0]
    odd = on_odd_place()
    rows = times_transposed(pick[...], own_slot_rows(neighbours))
    row = iota((8, 128), 0)
    lane = iota((8, 128), 1)
    j, k = [jnp.bitwise_and(lax.shift_right_logical(row, n), 1) for n in (1, 0)]

    def block(tap, i, begin):
        c, e = tap // 3 % 3, tap % 3
        source = 2 * jnp.bitwise_and(j + c + 1, 1) + jnp.bitwise_and(k + e + 1, 1)
        wanted = (lane - source - begin).astype(F32)
        at = 8 * (2 * tap + i)
        tiles = []
        for b in range(0, count, 2):
            first, second = [rows[at : at + 8, 128 * n : 128 * (n + 1)] for n in (b, b + 1)]
            hit = jnp.where(row < 4, first, second) == wanted
            tiles.append(jnp.where(hit, 1.0, 0.0))
        return stack(tiles)

    nowhere = 16 * 4 * count
    for tap in range(27):
        for i in range(2):
            x = i + tap // 9 - 1
            if x < 0:
                begin = jnp.where(odd, nowhere, 8 * count)
            elif x > 1:
                begin = jnp.where(odd, 8 * count, nowhere)
            else:
                begin = 4 * count * x
            at = 8 * count * tap + 4 * count * i
            own_three[at : at + 4 * count, :] = block(tap, i, begin)[:, : 12 * count].astype(BF16)
    for q in range(9):
        tile = jnp.where(odd, block(q, 0, 0), block(18 + q, 1, 0))
        near_three[4 * count * q : 4 * count * (q + 1), :] = tile[:, : 4 * count].astype(BF16)


def shifted_windows(source, row):
    shifted = []
    for j in range(-1, 9):
        c, at = (0, 7) if j < 0 else (2, 0) if j > 7 else (1, j)
        left, mid, right = [source(3 * c + e, at) for e in range(3)]
        shifted.append(
            (
                pltpu.roll(jnp.where(row == 7, left, mid), 1, 0),
                mid,
                pltpu.roll(jnp.where(row == 0, right, mid), 7, 0),
            )
        )
    return [
        [stack([shifted[jr][e], shifted[jr + 4][e]]).astype(BF16) for e in range(3)]
        for jr in range(6)
    ]


def outer_kernel(
    neighbours, bits, features, kernel, reduce,
    middle, taps, face_taps, reduce_taps, partial,
    tables, windows, wrap_taps,
):
    count = features.shape[0]
    lane = iota((64, 128), 1)
    row = iota((8, 128), 0)
    numbers = slot_numbers(neighbours)

    none = jnp.zeros((64, 64), F32)
    for q in range(9):
        w = [kernel[9 * a + q].astype(F32) for a in range(3)]
        rows = slice(q * 128, (q + 1) * 128)
        taps[rows, :] = stack(
            [beside([w[2], w[1], w[0], none]), beside([none, w[2], w[1], w[0]])]
        ).astype(BF16)
        wrap_taps[rows, :] = stack(
            [beside([w[2], w[1], none, none]), beside([none, none, w[1], w[0]])]
        ).astype(BF16)
        face_taps[rows, :] = stack([beside([w[0], none]), beside([none, w[2]])]).astype(BF16)

    reduce_taps[...] = stack(
        [
            beside([reduce[4 * ci + 2 * cj], reduce[4 * ci + 2 * cj + 1]])
            for cj in range(2)
            for ci in range(2)
        ]
    )

    for pair in range(4):
        tables[pair, count] = jnp.zeros((64, 128), F32)
    for b in range(count):
        cols = [
            features[b, :, 128 * q : 128 * (q + 1)].astype(F32) * bits[q, b : b + 1]
            for q in range(4)
        ]
        rolled = [pltpu.roll(col, 64, 1) for col in cols]
        for p in (0, 2):
            m = stack(
                [
                    jnp.where(lane < 64, rolled[p], cols[p + 1]),
                    jnp.where(lane < 64, cols[p + 1], rolled[(p + 2) % 4]),
                ]
            ).T
            tables[p, b] = m[:64]
            tables[p + 1, b] = m[64:]

    for b in range(count):
        slot = [numbers[b, 9 + q] for q in range(9)]
        for pair in range(4):
            tiles = shifted_windows(lambda q, j: tables[pair, slot[q], pl.ds(8 * j, 8), :], row)
            for jr in range(6):
                for e in range(3):
                    if pair == 1:
                        middle[b, e, jr] = tiles[jr][e]
                    else:
                        windows[b, e, pair, jr] = tiles[jr][e]

    group = count // 2
    for g in range(2):
        bricks = slice(g * group, (g + 1) * group)
        rows = slice(g * group * 64, (g + 1) * group * 64)
        low, high, wrap = [
            dot(
                beside(
                    [
                        windows[bricks, e, pair, c : c + 4].reshape(group * 64, 128)
                        for c in range(3)
                        for e in range(3)
                    ]
                ),
                weights[...],
            )
            for pair, weights in ((0, taps), (2, taps), (3, wrap_taps))
        ]
        partial[0, rows] = low[:, :128] + wrap[:, 128:]
        partial[1, rows] = low[:, 128:]
        partial[2, rows] = high[:, :128]
        partial[3, rows] = high[:, 128:] + wrap[:, :128]


def masked_tiles(sums, pair_words, b, i):
    row = iota((8, 128), 0)
    tiles = {}
    for half in range(2):
        words = jnp.broadcast_to(pair_words[2 * i + half, b : b + 1, :], (8, 128))
        for jr in range(4):
            at = jr * 16 + half * 8
            tiles[4 * half + jr] = jnp.maximum(sums[at : at + 8], 0.0) * bits_of(
                words, row + 8 * jr
            )
    return [tiles[j] for j in range(8)]


def reduce_planes(groups, weights, low_sums, high_sums):
    left = stack(
        [beside([tiles[j], tiles[j + 1]]) for tiles in groups for j in (0, 2, 4, 6)]
    ).astype(BF16)
    sums = dot(left, weights[...])
    low_sums[...] = sums[:, :128]
    high_sums[...] = sums[:, 128:]
    return [
        low_sums[pl.ds(32 * g, 16, stride=2), :] + high_sums[pl.ds(32 * g + 1, 16, stride=2), :]
        for g in range(len(groups))
    ]


def faces_one_kernel(
    neighbours, from_a, from_b, face_taps, partial, reduce, pair_words, mask_two, inner,
    outer, second, to_b,
    halo, windows, low_sums, high_sums,
):
    count = outer.shape[0]
    lane = iota((64, 128), 1)
    small = iota((8, 128), 1)
    row = iota((8, 128), 0)
    odd = on_odd_place()
    slot = slot_numbers(neighbours)
    halo[count] = jnp.zeros((64, 128), F32)
    for q in range(count // 2):
        one, two = from_a[q].astype(F32), from_b[64 * q : 64 * (q + 1), :].astype(F32)
        m = stack([jnp.where(odd, one, two), jnp.where(odd, two, one)]).T
        halo[2 * q] = m[:64]
        halo[2 * q + 1] = m[64:]
    for b in range(count):
        low = [slot[b, q] for q in range(9)]
        high = [slot[b, 18 + q] for q in range(9)]

        def source(q, j):
            rows = pl.ds(8 * j, 8)
            return jnp.where(small < 64, halo[low[q], rows, :], halo[high[q], rows, :])

        tiles = shifted_windows(source, row)
        for jr in range(6):
            for e in range(3):
                windows[b, e, jr] = tiles[jr][e]
    added = dot(
        beside(
            [
                windows[:, e, c : c + 4].reshape(count * 64, 128)
                for c in range(3)
                for e in range(3)
            ]
        ),
        face_taps[...],
    )
    groups = []
    for b in range(count):
        at = slice(64 * b, 64 * (b + 1))
        for side in range(2):
            near = (lane < 64) == (side == 0)
            sums = partial[3 * side, at] + jnp.where(near, added[at], 0.0)
            groups.append(masked_tiles(sums, pair_words, b, 3 * side))
            outer[b, side] = stack(groups[-1]).astype(BF16)
    sums = reduce_planes(groups, reduce, low_sums, high_sums)
    for b in range(count):
        at = slice(16 * b, 16 * (b + 1))
        planes = [
            (jnp.maximum(sums[2 * b + side], 0.0) * mask_two[3 * side, at]).astype(BF16)
            for side in range(2)
        ]
        second[16 * b : 16 * (b + 1)] = planes[0]
        second[16 * (count + b) : 16 * (count + b + 1)] = planes[1]
        to_b[at] = jnp.where(odd, planes[1], planes[0])
    rows = 16 * count
    to_b[rows : 2 * rows] = jnp.where(odd, inner[1], inner[0])
    to_b[2 * rows :] = jnp.where(odd, inner[0], inner[1])


def inner_kernel(
    middle, taps, partial, reduce, pair_words, mask_two,
    inner, second,
    low_sums, high_sums,
):
    count = middle.shape[0]
    added = dot(
        beside(
            [
                middle[:, e, c : c + 4].reshape(count * 64, 128)
                for c in range(3)
                for e in range(3)
            ]
        ),
        taps[...],
    )
    groups = []
    for b in range(count):
        at = slice(64 * b, 64 * (b + 1))
        for i in (1, 2):
            sums = partial[i, at] + added[at, 128 * (i - 1) : 128 * i]
            groups.append(masked_tiles(sums, pair_words, b, i))
            inner[b, i - 1] = stack(groups[-1]).astype(BF16)
    sums = reduce_planes(groups, reduce, low_sums, high_sums)
    for b in range(count):
        at = slice(16 * b, 16 * (b + 1))
        for i in (1, 2):
            second[i - 1, at] = (
                jnp.maximum(sums[2 * b + i - 1], 0.0) * mask_two[i, at]
            ).astype(BF16)


def output_kernel(outer, inner, out):
    lane = iota((64, 128), 1)
    for b in range(outer.shape[0]):
        ordered = [outer[b, 0], inner[b, 0], inner[b, 1], outer[b, 1]]
        for i in (0, 2):
            m = stack(ordered[i : i + 2]).astype(F32).T
            top, bottom = m[:64], m[64:]
            out[b, :, 128 * i : 128 * (i + 1)] = jnp.where(
                lane < 64, top, pltpu.roll(bottom, 64, 1)
            ).astype(BF16)
            out[b, :, 128 * (i + 1) : 128 * (i + 2)] = jnp.where(
                lane < 64, pltpu.roll(top, 64, 1), bottom
            ).astype(BF16)


def face_part(gather, face, kernel, high):
    moved = dot(gather, face).astype(BF16)
    rows = moved.shape[0] // 9
    left = beside([moved[q * rows : (q + 1) * rows] for q in range(9)])
    weights = kernel[pl.ds(18 * high, 9)]
    return dot(left, weights.reshape(9 * weights.shape[1], weights.shape[2]))


def own_two_kernel(
    outer, inner, own_gather, gathers, from_a, kernel, first,
    partial, result, stored,
):
    copy = pltpu.make_async_copy(first, result, stored)
    copy.start()
    rows = inner.shape[1]
    planes = beside([outer[:rows], inner[0], inner[1], outer[rows:]])
    moved = dot(own_gather[...], planes).astype(BF16)
    left = beside(
        [
            stack(
                [
                    moved[q * rows : (q + 1) * rows, 128 * i : 128 * (i + 1)]
                    for i in range(4)
                ]
            )
            for q in range(9)
        ]
    )
    weights = [kernel[9 * a : 9 * (a + 1)].reshape(9 * 128, 128) for a in range(3)]
    sums = dot(left, beside(weights[:2]))
    later = dot(left[rows:], weights[2])
    high = jnp.where(on_odd_place(), 0, 1)
    near = face_part(gathers[high], from_a[...], kernel, high)
    for i in range(4):
        total = sums[i * rows : (i + 1) * rows, 128:]
        if i:
            total = total + sums[(i - 1) * rows : i * rows, :128]
        if i < 3:
            total = total + later[i * rows : (i + 1) * rows]
        if i in (0, 3):
            total = total + jnp.where(high == i // 3, near, 0.0)
        partial[i * rows : (i + 1) * rows] = total
    copy.wait()


def own_for_far_kernel(gather, to_b, kernel, part):
    rows = part.shape[0]
    part[...] = face_part(gather[...], to_b[:rows], kernel, jnp.where(on_odd_place(), 0, 1))


def child_columns(picked, pairs, planes):
    return beside(
        [
            stack(
                [
                    picked[8 * (planes * q + i) : 8 * (planes * q + i + 1), 128 * n : 128 * (n + 1)]
                    for i in range(planes)
                    for n in range(pairs)
                ]
            )
            for q in range(8)
        ]
    )


def faces_two_kernel(
    gathers, far_gather, children, far_children, partial, own_for_far, from_b, kernel, reduce,
    mask_two, mask_three, far_mask_two, far_mask_three,
    second, third, far_third,
):
    count = second.shape[0]
    rows = 16 * count
    odd = on_odd_place()
    high = jnp.where(odd, 1, 0)
    far = face_part(gathers[high], from_b[:rows], kernel, high)
    planes = []
    for i in range(4):
        sums = partial[i * rows : (i + 1) * rows]
        if i in (0, 3):
            sums = sums + jnp.where(high == i // 3, far, 0.0)
        planes.append((jnp.maximum(sums, 0.0) * mask_two[i]).astype(BF16))
    bricks = [
        stack([planes[i][16 * b : 16 * (b + 1)] for i in range(4)]) for b in range(count)
    ]
    for b in range(count):
        second[b] = bricks[b]
    picked = dot(
        children[...], beside([stack(bricks[b : b + 2]) for b in range(0, count, 2)])
    )

    moved = dot(
        far_gather[...], beside([from_b[d * rows : (d + 1) * rows] for d in range(3)])
    ).astype(BF16)
    left = [
        beside([moved[q * rows : (q + 1) * rows, 128 * d : 128 * (d + 1)] for q in range(9)])
        for d in range(3)
    ]
    toward, same, away = [
        kernel[pl.ds(begin, 9)].reshape(9 * 128, 128) for begin in (18 - 18 * high, 9, 18 * high)
    ]
    zero = dot(left[0], beside([same, toward]))
    one = dot(left[1], beside([away, same]))
    near = own_for_far[...] + zero[:, :128] + one[:, :128]
    past = zero[:, 128:] + one[:, 128:] + dot(left[2], away)
    far_planes = [
        (jnp.maximum(sums, 0.0) * far_mask_two[n * rows : (n + 1) * rows]).astype(BF16)
        for n, sums in enumerate((jnp.where(odd, near, past), jnp.where(odd, past, near)))
    ]
    far_picked = dot(
        far_children[...],
        beside(
            [
                stack(
                    [
                        plane[16 * b : 16 * (b + 1)]
                        for b in (n, n + 1)
                        for plane in far_planes
                    ]
                )
                for n in range(0, count, 2)
            ]
        ),
    )
    left = stack(
        [child_columns(picked, count // 2, 2), child_columns(far_picked, count // 2, 1)]
    ).astype(BF16)
    sums = jnp.maximum(dot(left, reduce[...].reshape(8 * 128, 256)), 0.0)
    third[...] = (sums[: 8 * count] * mask_three[...]).astype(BF16)
    far_third[...] = (sums[8 * count :] * far_mask_three[...]).astype(BF16)


def own_three_kernel(gather, third, far, kernel, second, partial, result, stored):
    copy = pltpu.make_async_copy(second, result, stored)
    copy.start()
    rows = third.shape[0]
    moved = dot(gather[...], stack([third[...], far[...]])).astype(BF16)
    left = beside([moved[q * rows : (q + 1) * rows] for q in range(27)])
    partial[...] = dot(left, kernel[...].reshape(27 * 256, 256))
    copy.wait()


def faces_three_kernel(gather, partial, from_a, kernel, mask_three, out):
    rows = from_a.shape[0]
    odd = on_odd_place()
    near = face_part(gather[...], from_a[...], kernel, jnp.where(odd, 0, 1))
    low = partial[:rows] + jnp.where(odd, near, 0.0)
    high = partial[rows:] + jnp.where(odd, 0.0, near)
    low = jnp.maximum(low, 0.0) * mask_three[:rows]
    high = jnp.maximum(high, 0.0) * mask_three[rows:]
    row = iota((8, 256), 0)
    for n in range(rows // 8):
        near, past = low[8 * n : 8 * (n + 1)], high[8 * n : 8 * (n + 1)]
        out[2 * n] = jnp.where(row < 4, near, pltpu.roll(past, 4, 0)).astype(BF16)
        out[2 * n + 1] = jnp.where(row < 4, pltpu.roll(near, 4, 0), past).astype(BF16)


def level_two_picks():
    pick = np.zeros((432, 27), np.float32)
    for tap in range(27):
        for r in range(16):
            y, z = r // 4 + tap // 3 % 3 - 1, r % 4 + tap % 3 - 1
            pick[16 * tap + r, tap // 9 * 9 + 3 * (y // 4 + 1) + z // 4 + 1] = 16
    return jnp.asarray(pick, BF16)


def level_three_picks():
    pick = np.zeros((27 * 16, 27), np.float32)
    for tap in range(27):
        for r in range(16):
            x, y, z = [
                n + d - 1
                for n, d in (
                    (r // 8, tap // 9), (r // 2 % 2, tap // 3 % 3), (r % 2, tap % 3)
                )
            ]
            pick[16 * tap + r, 9 * (x // 2 + 1) + 3 * (y // 2 + 1) + z // 2 + 1] = 4
    return jnp.asarray(pick, BF16)


def child_rows(planes):
    pick = np.zeros((8 * planes * 8, 2 * 2 * planes * 16), np.float32)
    for q in range(8):
        for r in range(8 * planes):
            x, y, z = [
                2 * n + (q >> s & 1) for n, s in ((r // 8, 2), (r // 2 % 2, 1), (r % 2, 0))
            ]
            at = 2 * planes * 16 * (r // 4 % 2) + 16 * x + 4 * y + z
            pick[8 * planes * q + r, at] = 1
    return jnp.asarray(pick, BF16)


ANY = pl.BlockSpec(memory_space=pl.ANY)
VMEM = pl.BlockSpec(memory_space=pltpu.VMEM)
DMA = pltpu.SemaphoreType.DMA


def call(kernel, cost, out_shape, scratch, *args, remain=(), store=()):
    single = not isinstance(out_shape, tuple)
    outs = (out_shape,) if single else out_shape
    specs = tuple(ANY if n in store else VMEM for n in range(len(outs)))
    return pl.pallas_call(
        kernel,
        out_shape=out_shape,
        in_specs=[ANY if n in remain else VMEM for n in range(len(args))],
        out_specs=specs[0] if single else specs,
        scratch_shapes=scratch,
        compiler_params=pltpu.CompilerParams(vmem_limit_bytes=24 * 1024 * 1024),
        cost_estimate=pl.CostEstimate(
            flops=int(cost * 10**10), bytes_accessed=10**7, transcendentals=0
        ),
    )(*args)


def swaps(tiles, count):
    within, across = [], []
    for t in range(tiles):
        for m in range(count):
            if m ^ 1 < count:
                within.append((t * count + m, t * count + (m ^ 1)))
            other = ((m - 1) ^ 1) + 1 if m else -1
            if 0 <= other < count:
                across.append((t * count + m, t * count + other))
            elif t ^ 1 < tiles:
                across.append((t * count + m, (t ^ 1) * count + m))
    return within, across


def on_device(
    features,
    neighbours,
    occupancy,
    conv_one,
    first_reduce_kernel,
    conv_two,
    second_reduce_kernel,
    conv_three,
):
    axes = ("tiles", LINE)
    within, across = swaps(lax.axis_size("tiles"), lax.axis_size(LINE))
    count = features.shape[0]
    features = jnp.swapaxes(features, 1, 2)
    shape = jax.ShapeDtypeStruct

    def exchange(to_a, to_b):
        from_b = lax.ppermute(to_b, axes, across)
        return lax.ppermute(to_a, axes, within), from_b

    blank = call(blank_kernel, 1.0, shape((2 * count, 128), F32), [])
    bits, edge_bits, pair_words, mask_two, mask_three = call(
        masks_kernel,
        0.01,
        (
            shape((4, count, 128), F32),
            shape((2, count, 128), F32),
            shape((8, count, 128), jnp.int32),
            shape((4, 16 * count, 128), F32),
            shape((8 * count, 256), F32),
        ),
        [],
        occupancy, blank,
    )
    to_b = call(
        far_edge_kernel,
        0.02,
        shape((32 * count + 2 * count, 128), BF16),
        [pltpu.VMEM((2 * count, 128), F32)],
        features, bits, neighbours, edge_bits, blank,
    )
    face = shape((count // 2, 64, 128), BF16)
    to_a = call(near_edge_kernel, 0.02, face, [], features, bits, to_b)
    from_a, message = exchange(to_a, to_b)
    middle, taps, face_taps, reduce_taps, partial = call(
        outer_kernel,
        2.0,
        (
            shape((count, 3, 6, 16, 128), BF16),
            shape((9 * 128, 256), BF16),
            shape((9 * 128, 128), BF16),
            shape((256, 256), BF16),
            shape((4, count * 64, 128), F32),
        ),
        [
            pltpu.VMEM((4, count + 1, 64, 128), F32),
            pltpu.VMEM((count, 3, 4, 6, 16, 128), BF16),
            pltpu.VMEM((9 * 128, 256), BF16),
        ],
        neighbours, bits, features, conv_one, first_reduce_kernel,
    )
    plane = shape((16 * count, 128), BF16)
    rows = shape((count, 2, 64, 128), BF16)
    sums = pltpu.VMEM((count * 64, 128), F32)
    inner, inner_two = call(
        inner_kernel,
        0.05,
        (rows, shape((2, 16 * count, 128), BF16)),
        [sums, sums],
        middle, taps, partial, reduce_taps, pair_words, mask_two,
    )
    outer, outer_two, to_b = call(
        faces_one_kernel,
        1.5,
        (rows, shape((2 * 16 * count, 128), BF16), shape((3 * 16 * count, 128), BF16)),
        [
            pltpu.VMEM((count + 1, 64, 128), F32),
            pltpu.VMEM((count, 3, 6, 16, 128), BF16),
            sums,
            sums,
        ],
        neighbours, from_a, message, face_taps, partial, reduce_taps, pair_words, mask_two,
        inner_two,
    )
    to_a = call(near_face_kernel, 0.02, plane, [], outer_two, to_b)
    from_a, from_b = exchange(to_a, to_b)

    pick = level_two_picks()
    table = shape((9 * 16 * count, 16 * count), BF16)
    own_two, sides_two = call(
        level_two_tables_kernel,
        0.05,
        (table, shape((2, 9 * 16 * count, 16 * count), BF16)),
        [],
        neighbours, pick, to_a,
    )
    far_two, toward_two, far_mask_two, far_mask_three = call(
        far_tables_kernel,
        0.05,
        (table, table, shape((2 * 16 * count, 128), F32), shape((4 * count, 256), F32)),
        [],
        message, pick, to_a,
    )
    first_level = call(output_kernel, 0.05, shape(features.shape, BF16), [], outer, inner)
    own_for_far = call(
        own_for_far_kernel,
        0.05,
        shape((16 * count, 128), F32),
        [],
        toward_two, to_b, conv_two,
    )
    partial, first_level = call(
        own_two_kernel,
        1.0,
        (shape((4 * 16 * count, 128), F32), shape(features.shape, BF16)),
        [DMA(())],
        outer_two, inner_two, own_two, sides_two, from_a, conv_two, first_level,
        store=(1,),
    )
    own_three, near_three = call(
        level_three_tables_kernel,
        0.05,
        (shape((27 * 8 * count, 12 * count), BF16), shape((9 * 4 * count, 4 * count), BF16)),
        [],
        neighbours, level_three_picks(), to_a,
    )
    face = shape((4 * count, 256), BF16)
    second_level, third, far_third = call(
        faces_two_kernel,
        1.5,
        (shape((count, 64, 128), BF16), shape((8 * count, 256), BF16), face),
        [],
        sides_two, far_two, child_rows(2), child_rows(1), partial, own_for_far, from_b, conv_two,
        second_reduce_kernel, mask_two, mask_three, far_mask_two, far_mask_three,
    )
    to_a = call(near_face_kernel, 0.02, face, [], third, far_third)
    from_a = lax.ppermute(to_a, axes, within)
    partial, second_level = call(
        own_three_kernel,
        1.0,
        (shape((8 * count, 256), F32), shape(second_level.shape, BF16)),
        [DMA(())],
        own_three, third, far_third, conv_three, second_level,
        store=(1,),
    )
    third_level = call(
        faces_three_kernel,
        1,
        shape((count, 8, 256), BF16),
        [],
        near_three, partial, from_a, conv_three, mask_three,
    )
    return jnp.swapaxes(first_level, 1, 2), second_level, third_level


def solution(mesh):
    split = P(("tiles", LINE))
    return jax.shard_map(
        on_device,
        mesh=mesh,
        in_specs=(split, split, split, P(), P(), P(), P(), P()),
        out_specs=(split, split, split),
        check_vma=False,
    )
```

```python
import jax
import jax.numpy as jnp
import numpy as np
from jax import lax
from jax.experimental import pallas as pl
from jax.experimental.pallas import tpu as pltpu
from jax.sharding import PartitionSpec as P

F32 = jnp.float32
BF16 = jnp.bfloat16
LINE = "morton"


def dot(x, y):
    return jnp.dot(x, y, preferred_element_type=F32)


def iota(shape, axis):
    return lax.broadcasted_iota(jnp.int32, shape, axis)


def stack(parts):
    return jnp.concatenate(parts, axis=0)


def beside(parts):
    return jnp.concatenate(parts, axis=1)


def bits_of(words, shift):
    return jnp.bitwise_and(lax.shift_right_logical(words, shift), 1).astype(F32)


def either(x, y):
    return jnp.bitwise_or(x, y)


def on_odd_place():
    return lax.rem(lax.axis_index(LINE), 2) == 1


def word_lanes(words, w):
    return jnp.broadcast_to(words[:, w : w + 1], (words.shape[0], 128))


def column_bits(words, column):
    lane = iota((words.shape[0], 128), 1)
    w = [word_lanes(words, 4 * column + q) for q in range(4)]
    chosen = jnp.where(
        lane < 64, jnp.where(lane < 32, w[0], w[1]), jnp.where(lane < 96, w[2], w[3])
    )
    return bits_of(chosen, jnp.bitwise_and(lane, 31))


def slot_numbers(neighbours):
    count = neighbours.shape[0]
    number = neighbours[...]
    tap = iota(number.shape, 1)
    shift = jnp.where(tap < 9, count, jnp.where(tap < 18, 0, -count))
    return jnp.where(number < 0, count, number + shift - lax.axis_index(LINE) * count)


def blank_kernel(notes):
    notes[...] = jnp.zeros(notes.shape, F32)


def masks_kernel(occupancy, blank, bits, edge_bits, pair_words, mask_two, mask_three):
    count = occupancy.shape[0]
    for q in range(4):
        bits[q] = column_bits(occupancy[...], q)
    words = [word_lanes(occupancy[...], w) for w in range(16)]
    lane = iota((count, 128), 1)
    row = iota((8, 128), 0)
    any_two = []
    for i in range(4):
        for half in range(2):
            low, high = words[4 * i + half], words[4 * i + 2 + half]
            pair_words[2 * i + half] = jnp.where(lane < 64, low, high)
            word = either(low, high)
            word = either(word, lax.shift_right_logical(word, 1))
            any_two.append(either(word, lax.shift_right_logical(word, 8)))
    two_shift = 16 * lax.shift_right_logical(row, 2) + 2 * jnp.bitwise_and(row, 3)
    for i in range(4):
        for b in range(count):
            mask_two[i, 16 * b : 16 * (b + 1)] = stack(
                [
                    bits_of(
                        jnp.broadcast_to(any_two[2 * i + half][b : b + 1], (8, 128)), two_shift
                    )
                    for half in range(2)
                ]
            )
    plane, half, m = [jnp.bitwise_and(lax.shift_right_logical(lane, n), 1) for n in (4, 3, 2)]
    for side in range(2):
        word = [any_two[4 * side + n] for n in range(4)]
        word = jnp.where(
            plane == 0, jnp.where(half == 0, word[0], word[1]), jnp.where(half == 0, word[2], word[3])
        )
        edge_bits[side] = bits_of(word, 16 * m + 2 * jnp.bitwise_and(lane, 3))
    any_three = []
    for i in range(2):
        for j in range(2):
            word = either(any_two[4 * i + j], any_two[4 * i + 2 + j])
            word = either(word, lax.shift_right_logical(word, 16))
            any_three.append(either(word, lax.shift_right_logical(word, 2)))
    for i in range(2):
        for b in range(0, count, 2):
            tile = [
                jnp.broadcast_to(any_three[2 * i + j][n : n + 1], (8, 128))
                for n in (b, b + 1)
                for j in range(2)
            ]
            tile = jnp.where(
                row < 4, jnp.where(row < 2, tile[0], tile[1]), jnp.where(row < 6, tile[2], tile[3])
            )
            mask = bits_of(tile, 4 * jnp.bitwise_and(row, 1))
            at = 4 * (count * i + b)
            mask_three[at : at + 8] = beside([mask, mask])


def edge_planes(features, bits, low_wanted):
    last = features.shape[2] - 128
    planes = []
    for q in range(features.shape[0] // 2):
        low, high = [
            [
                features[b, :, column * last : column * last + 128]
                * bits[3 * column, b : b + 1].astype(BF16)
                for b in (2 * q, 2 * q + 1)
            ]
            for column in range(2)
        ]
        lows = beside([low[0][:, :64], low[1][:, :64]])
        highs = beside([high[0][:, 64:], high[1][:, 64:]])
        planes.append(jnp.where(low_wanted, lows, highs))
    return planes


def far_edge_kernel(features, bits, neighbours, edge_bits, blank, edge, notes):
    count = features.shape[0]
    odd = on_odd_place()
    for q, plane in enumerate(edge_planes(features, bits, jnp.logical_not(odd))):
        edge[64 * q : 64 * (q + 1), :] = plane
    notes[...] = blank[...]
    notes[:count, : neighbours.shape[1]] = jnp.where(
        neighbours[...] < 0, 4 * count, slot_numbers(neighbours)
    ).astype(F32)
    notes[count:, :] = edge_bits[jnp.where(odd, 1, 0)]
    edge[32 * count :, :] = notes[...].astype(BF16)


def near_edge_kernel(features, bits, earlier, edge):
    for q, plane in enumerate(edge_planes(features, bits, on_odd_place())):
        edge[q] = plane


def near_face_kernel(planes, earlier, face):
    rows = face.shape[0]
    begin = pl.multiple_of(jnp.where(on_odd_place(), 0, rows), rows)
    face[...] = planes[pl.ds(begin, rows), :]


def slot_rows(slot):
    return stack(
        [jnp.broadcast_to(slot[b : b + 1], (128, slot.shape[1])) for b in range(slot.shape[0])]
    ).astype(BF16)


def own_slot_rows(neighbours):
    slot = jnp.where(neighbours[...] < 0, 4 * neighbours.shape[0], slot_numbers(neighbours))
    return slot_rows(slot.astype(F32))


def times_transposed(x, y):
    return lax.dot_general(x, y, (((1,), (1,)), ((), ())), preferred_element_type=F32)


def fill_level_two_tables(tables, rows, count):
    lane = iota((16, 16 * count), 1)
    row = iota((16, 16 * count), 0)
    j, k = lax.shift_right_logical(row, 2), jnp.bitwise_and(row, 3)
    for q in range(9):
        source = 4 * jnp.bitwise_and(j + q // 3 + 3, 3) + jnp.bitwise_and(k + q % 3 + 3, 3)
        wanted = (lane - source).astype(F32)
        for a, table in enumerate(tables):
            at = 16 * (9 * a + q)
            for b in range(count):
                table[16 * (count * q + b) : 16 * (count * q + b + 1), :] = jnp.where(
                    rows[at : at + 16, 128 * b : 128 * b + 16 * count] == wanted, 1.0, 0.0
                ).astype(BF16)


def level_two_tables_kernel(neighbours, pick, later, own_two, sides_two):
    rows = times_transposed(pick[...], own_slot_rows(neighbours))
    fill_level_two_tables(
        (sides_two.at[0], own_two, sides_two.at[1]), rows, neighbours.shape[0]
    )


def far_tables_kernel(message, pick, later, gather, mask_two, mask_three):
    count = gather.shape[1] // 32
    notes = message[32 * count :, :].astype(F32)
    slots = slot_rows(notes[:count, : pick.shape[1]])
    begin = pl.multiple_of(jnp.where(on_odd_place(), 0, 288), 16)
    rows = stack(
        [
            times_transposed(pick[pl.ds(begin, 144), :], slots),
            times_transposed(pick[144:288, :], slots),
        ]
    )
    width = 16 * count
    fill_level_two_tables((gather.at[:, width:], gather.at[:, :width]), rows, count)

    every = jnp.ones((128, 256), BF16)
    lane = iota((16, 128), 1)
    row = iota((16, 128), 0)
    bits = [notes[count + b : count + b + 1] for b in range(count)]
    chosen = stack(
        [
            jnp.where(lane == 16 * plane + row, jnp.broadcast_to(bits[b], (16, 128)), 0.0)
            for plane in range(2)
            for b in range(count)
        ]
    ).astype(BF16)
    mask_two[...] = dot(chosen, every[:, :128])
    lane, row = lane[:8], row[:8]
    child = jnp.bitwise_and(lax.shift_right_logical(lane, 2), 2) + jnp.bitwise_and(
        lax.shift_right_logical(lane, 1), 1
    )
    wanted = (child == jnp.bitwise_and(row, 3)) & (lane < 32)
    chosen = stack(
        [
            jnp.where(wanted, jnp.where(row < 4, bits[b], bits[b + 1]), 0.0)
            for b in range(0, count, 2)
        ]
    ).astype(BF16)
    mask_three[...] = jnp.where(dot(chosen, every) > 0.5, 1.0, 0.0)


def level_three_tables_kernel(neighbours, pick, later, own_three, near_three):
    count = neighbours.shape[0]
    odd = on_odd_place()
    rows = times_transposed(pick[...], own_slot_rows(neighbours))
    row = iota((8, 128), 0)
    lane = iota((8, 128), 1)
    j, k = [jnp.bitwise_and(lax.shift_right_logical(row, n), 1) for n in (1, 0)]

    def block(tap, i, begin):
        c, e = tap // 3 % 3, tap % 3
        source = 2 * jnp.bitwise_and(j + c + 1, 1) + jnp.bitwise_and(k + e + 1, 1)
        wanted = (lane - source - begin).astype(F32)
        at = 8 * (2 * tap + i)
        tiles = []
        for b in range(0, count, 2):
            first, second = [rows[at : at + 8, 128 * n : 128 * (n + 1)] for n in (b, b + 1)]
            hit = jnp.where(row < 4, first, second) == wanted
            tiles.append(jnp.where(hit, 1.0, 0.0))
        return stack(tiles)

    nowhere = 16 * 4 * count
    for tap in range(27):
        for i in range(2):
            x = i + tap // 9 - 1
            if x < 0:
                begin = jnp.where(odd, nowhere, 8 * count)
            elif x > 1:
                begin = jnp.where(odd, 8 * count, nowhere)
            else:
                begin = 4 * count * x
            at = 8 * count * tap + 4 * count * i
            own_three[at : at + 4 * count, :] = block(tap, i, begin)[:, : 12 * count].astype(BF16)
    for q in range(9):
        tile = jnp.where(odd, block(q, 0, 0), block(18 + q, 1, 0))
        near_three[4 * count * q : 4 * count * (q + 1), :] = tile[:, : 4 * count].astype(BF16)


def shifted_windows(source, row):
    shifted = []
    for j in range(-1, 9):
        c, at = (0, 7) if j < 0 else (2, 0) if j > 7 else (1, j)
        left, mid, right = [source(3 * c + e, at) for e in range(3)]
        shifted.append(
            (
                pltpu.roll(jnp.where(row == 7, left, mid), 1, 0),
                mid,
                pltpu.roll(jnp.where(row == 0, right, mid), 7, 0),
            )
        )
    return [
        [stack([shifted[jr][e], shifted[jr + 4][e]]).astype(BF16) for e in range(3)]
        for jr in range(6)
    ]


def outer_kernel(
    neighbours, bits, features, kernel, reduce,
    middle, taps, face_taps, reduce_taps, partial,
    tables, windows, wrap_taps,
):
    count = features.shape[0]
    row = iota((8, 128), 0)
    numbers = slot_numbers(neighbours)

    none = jnp.zeros((64, 64), BF16)
    for q in range(9):
        w = [kernel[9 * a + q] for a in range(3)]
        rows = slice(q * 128, (q + 1) * 128)
        taps[rows, :] = stack(
            [beside([w[2], w[1], w[0], none]), beside([none, w[2], w[1], w[0]])]
        )
        wrap_taps[rows, :] = stack(
            [beside([w[2], w[1], none, none]), beside([none, none, w[1], w[0]])]
        )
        face_taps[rows, :] = stack([beside([w[0], none]), beside([none, w[2]])])

    reduce_taps[...] = stack(
        [
            beside([reduce[4 * ci + 2 * cj], reduce[4 * ci + 2 * cj + 1]])
            for cj in range(2)
            for ci in range(2)
        ]
    )

    for pair in range(4):
        tables[pair, count] = jnp.zeros((64, 128), F32)
    for b in range(count):
        cols = [
            features[b, :, 128 * q : 128 * (q + 1)] * bits[q, b : b + 1].astype(BF16)
            for q in range(4)
        ]
        for p in (0, 2):
            m = stack(
                [
                    beside([cols[p][:, 64:], cols[p + 1][:, 64:]]),
                    beside([cols[p + 1][:, :64], cols[(p + 2) % 4][:, :64]]),
                ]
            ).T
            tables[p, b] = m[:64].astype(F32)
            tables[p + 1, b] = m[64:].astype(F32)

    for b in range(count):
        slot = [numbers[b, 9 + q] for q in range(9)]
        for pair in range(4):
            tiles = shifted_windows(lambda q, j: tables[pair, slot[q], pl.ds(8 * j, 8), :], row)
            for jr in range(6):
                for e in range(3):
                    if pair == 1:
                        middle[b, e, jr] = tiles[jr][e]
                    else:
                        windows[b, e, pair, jr] = tiles[jr][e]

    group = count // 2
    for g in range(2):
        bricks = slice(g * group, (g + 1) * group)
        rows = slice(g * group * 64, (g + 1) * group * 64)
        low, high, wrap = [
            dot(
                beside(
                    [
                        windows[bricks, e, pair, c : c + 4].reshape(group * 64, 128)
                        for c in range(3)
                        for e in range(3)
                    ]
                ),
                weights[...],
            )
            for pair, weights in ((0, taps), (2, taps), (3, wrap_taps))
        ]
        partial[0, rows] = low[:, :128] + wrap[:, 128:]
        partial[1, rows] = low[:, 128:]
        partial[2, rows] = high[:, :128]
        partial[3, rows] = high[:, 128:] + wrap[:, :128]


def masked_tiles(sums, pair_words, b, i):
    row = iota((8, 128), 0)
    tiles = {}
    for half in range(2):
        words = jnp.broadcast_to(pair_words[2 * i + half, b : b + 1, :], (8, 128))
        for jr in range(4):
            at = jr * 16 + half * 8
            tiles[4 * half + jr] = jnp.maximum(sums[at : at + 8], 0.0) * bits_of(
                words, row + 8 * jr
            )
    return [tiles[j] for j in range(8)]


def reduce_planes(groups, weights, low_sums, high_sums):
    left = stack(
        [beside([tiles[j], tiles[j + 1]]) for tiles in groups for j in (0, 2, 4, 6)]
    ).astype(BF16)
    sums = dot(left, weights[...])
    low_sums[...] = sums[:, :128]
    high_sums[...] = sums[:, 128:]
    return [
        low_sums[pl.ds(32 * g, 16, stride=2), :] + high_sums[pl.ds(32 * g + 1, 16, stride=2), :]
        for g in range(len(groups))
    ]


def faces_one_kernel(
    neighbours, from_a, from_b, face_taps, partial, reduce, pair_words, mask_two, inner,
    outer, second, to_b,
    halo, windows, low_sums, high_sums,
):
    count = outer.shape[0]
    lane = iota((64, 128), 1)
    small = iota((8, 128), 1)
    row = iota((8, 128), 0)
    odd = on_odd_place()
    slot = slot_numbers(neighbours)
    halo[count] = jnp.zeros((64, 128), F32)
    for q in range(count // 2):
        one, two = from_a[q], from_b[64 * q : 64 * (q + 1), :]
        m = stack([jnp.where(odd, one, two), jnp.where(odd, two, one)]).T
        halo[2 * q] = m[:64].astype(F32)
        halo[2 * q + 1] = m[64:].astype(F32)
    for b in range(count):
        low = [slot[b, q] for q in range(9)]
        high = [slot[b, 18 + q] for q in range(9)]

        def source(q, j):
            rows = pl.ds(8 * j, 8)
            return jnp.where(small < 64, halo[low[q], rows, :], halo[high[q], rows, :])

        tiles = shifted_windows(source, row)
        for jr in range(6):
            for e in range(3):
                windows[b, e, jr] = tiles[jr][e]
    added = dot(
        beside(
            [
                windows[:, e, c : c + 4].reshape(count * 64, 128)
                for c in range(3)
                for e in range(3)
            ]
        ),
        face_taps[...],
    )
    groups = []
    for b in range(count):
        at = slice(64 * b, 64 * (b + 1))
        for side in range(2):
            near = (lane < 64) == (side == 0)
            sums = partial[3 * side, at] + jnp.where(near, added[at], 0.0)
            groups.append(masked_tiles(sums, pair_words, b, 3 * side))
            outer[b, side] = stack(groups[-1]).astype(BF16)
    sums = reduce_planes(groups, reduce, low_sums, high_sums)
    for b in range(count):
        at = slice(16 * b, 16 * (b + 1))
        planes = [
            (jnp.maximum(sums[2 * b + side], 0.0) * mask_two[3 * side, at]).astype(BF16)
            for side in range(2)
        ]
        second[16 * b : 16 * (b + 1)] = planes[0]
        second[16 * (count + b) : 16 * (count + b + 1)] = planes[1]
        to_b[at] = jnp.where(odd, planes[1], planes[0])
    rows = 16 * count
    to_b[rows : 2 * rows] = jnp.where(odd, inner[1], inner[0])
    to_b[2 * rows :] = jnp.where(odd, inner[0], inner[1])


def inner_kernel(
    middle, taps, partial, reduce, pair_words, mask_two,
    inner, second,
    low_sums, high_sums,
):
    count = middle.shape[0]
    added = dot(
        beside(
            [
                middle[:, e, c : c + 4].reshape(count * 64, 128)
                for c in range(3)
                for e in range(3)
            ]
        ),
        taps[...],
    )
    groups = []
    for b in range(count):
        at = slice(64 * b, 64 * (b + 1))
        for i in (1, 2):
            sums = partial[i, at] + added[at, 128 * (i - 1) : 128 * i]
            groups.append(masked_tiles(sums, pair_words, b, i))
            inner[b, i - 1] = stack(groups[-1]).astype(BF16)
    sums = reduce_planes(groups, reduce, low_sums, high_sums)
    for b in range(count):
        at = slice(16 * b, 16 * (b + 1))
        for i in (1, 2):
            second[i - 1, at] = (
                jnp.maximum(sums[2 * b + i - 1], 0.0) * mask_two[i, at]
            ).astype(BF16)


def output_kernel(outer, inner, out):
    for b in range(outer.shape[0]):
        ordered = [outer[b, 0], inner[b, 0], inner[b, 1], outer[b, 1]]
        for i in (0, 2):
            m = stack(ordered[i : i + 2]).T
            top, bottom = m[:64], m[64:]
            out[b, :, 128 * i : 128 * (i + 1)] = beside([top[:, :64], bottom[:, :64]])
            out[b, :, 128 * (i + 1) : 128 * (i + 2)] = beside([top[:, 64:], bottom[:, 64:]])


def face_part(gather, face, kernel, high):
    moved = dot(gather, face).astype(BF16)
    rows = moved.shape[0] // 9
    left = beside([moved[q * rows : (q + 1) * rows] for q in range(9)])
    weights = kernel[pl.ds(18 * high, 9)]
    return dot(left, weights.reshape(9 * weights.shape[1], weights.shape[2]))


def own_two_kernel(
    outer, inner, own_gather, gathers, from_a, kernel, first,
    partial, result, stored,
):
    copy = pltpu.make_async_copy(first, result, stored)
    copy.start()
    rows = inner.shape[1]
    planes = beside([outer[:rows], inner[0], inner[1], outer[rows:]])
    moved = dot(own_gather[...], planes).astype(BF16)
    left = beside(
        [
            stack(
                [
                    moved[q * rows : (q + 1) * rows, 128 * i : 128 * (i + 1)]
                    for i in range(4)
                ]
            )
            for q in range(9)
        ]
    )
    weights = [kernel[9 * a : 9 * (a + 1)].reshape(9 * 128, 128) for a in range(3)]
    sums = dot(left, beside(weights[:2]))
    later = dot(left[rows:], weights[2])
    high = jnp.where(on_odd_place(), 0, 1)
    near = face_part(gathers[high], from_a[...], kernel, high)
    for i in range(4):
        total = sums[i * rows : (i + 1) * rows, 128:]
        if i:
            total = total + sums[(i - 1) * rows : i * rows, :128]
        if i < 3:
            total = total + later[i * rows : (i + 1) * rows]
        if i in (0, 3):
            total = total + jnp.where(high == i // 3, near, 0.0)
        partial[i * rows : (i + 1) * rows] = total
    copy.wait()


def child_columns(picked, pairs, planes):
    return beside(
        [
            stack(
                [
                    picked[8 * (planes * q + i) : 8 * (planes * q + i + 1), 128 * n : 128 * (n + 1)]
                    for i in range(planes)
                    for n in range(pairs)
                ]
            )
            for q in range(8)
        ]
    )


def faces_two_kernel(
    gathers, far_gather, children, far_children, partial, to_b, from_b, kernel, reduce,
    mask_two, mask_three, far_mask_two, far_mask_three,
    second, third, far_third,
):
    count = second.shape[0]
    rows = 16 * count
    odd = on_odd_place()
    high = jnp.where(odd, 1, 0)
    far = face_part(gathers[high], from_b[:rows], kernel, high)
    planes = []
    for i in range(4):
        sums = partial[i * rows : (i + 1) * rows]
        if i in (0, 3):
            sums = sums + jnp.where(high == i // 3, far, 0.0)
        planes.append((jnp.maximum(sums, 0.0) * mask_two[i]).astype(BF16))
    bricks = [
        stack([planes[i][16 * b : 16 * (b + 1)] for i in range(4)]) for b in range(count)
    ]
    for b in range(count):
        second[b] = bricks[b]
    picked = dot(
        children[...], beside([stack(bricks[b : b + 2]) for b in range(0, count, 2)])
    )

    none = jnp.zeros((rows, 128), BF16)
    planes = [from_b[d * rows : (d + 1) * rows] for d in range(3)]
    moved = dot(
        far_gather[...],
        stack([beside(planes + [none]), beside([none, none, none, to_b[:rows]])]),
    ).astype(BF16)
    left = [
        beside([moved[q * rows : (q + 1) * rows, 128 * d : 128 * (d + 1)] for q in range(9)])
        for d in range(4)
    ]
    toward, same, away = [
        kernel[pl.ds(begin, 9)].reshape(9 * 128, 128) for begin in (18 - 18 * high, 9, 18 * high)
    ]
    zero = dot(stack([left[0], left[3]]), beside([same, toward]))
    one = dot(left[1], beside([away, same]))
    near = zero[rows:, 128:] + zero[:rows, :128] + one[:, :128]
    past = zero[:rows, 128:] + one[:, 128:] + dot(left[2], away)
    far_planes = [
        (jnp.maximum(sums, 0.0) * far_mask_two[n * rows : (n + 1) * rows]).astype(BF16)
        for n, sums in enumerate((jnp.where(odd, near, past), jnp.where(odd, past, near)))
    ]
    far_picked = dot(
        far_children[...],
        beside(
            [
                stack(
                    [
                        plane[16 * b : 16 * (b + 1)]
                        for b in (n, n + 1)
                        for plane in far_planes
                    ]
                )
                for n in range(0, count, 2)
            ]
        ),
    )
    left = stack(
        [child_columns(picked, count // 2, 2), child_columns(far_picked, count // 2, 1)]
    ).astype(BF16)
    sums = jnp.maximum(dot(left, reduce[...].reshape(8 * 128, 256)), 0.0)
    third[...] = (sums[: 8 * count] * mask_three[...]).astype(BF16)
    far_third[...] = (sums[8 * count :] * far_mask_three[...]).astype(BF16)


def own_three_kernel(gather, third, far, kernel, second, partial, result, stored):
    copy = pltpu.make_async_copy(second, result, stored)
    copy.start()
    rows = third.shape[0]
    moved = dot(gather[...], stack([third[...], far[...]])).astype(BF16)
    left = beside([moved[q * rows : (q + 1) * rows] for q in range(27)])
    partial[...] = dot(left, kernel[...].reshape(27 * 256, 256))
    copy.wait()


def faces_three_kernel(gather, partial, from_a, kernel, mask_three, out):
    rows = from_a.shape[0]
    odd = on_odd_place()
    near = face_part(gather[...], from_a[...], kernel, jnp.where(odd, 0, 1))
    low = partial[:rows] + jnp.where(odd, near, 0.0)
    high = partial[rows:] + jnp.where(odd, 0.0, near)
    low = jnp.maximum(low, 0.0) * mask_three[:rows]
    high = jnp.maximum(high, 0.0) * mask_three[rows:]
    row = iota((8, 256), 0)
    for n in range(rows // 8):
        near, past = low[8 * n : 8 * (n + 1)], high[8 * n : 8 * (n + 1)]
        out[2 * n] = jnp.where(row < 4, near, pltpu.roll(past, 4, 0)).astype(BF16)
        out[2 * n + 1] = jnp.where(row < 4, pltpu.roll(near, 4, 0), past).astype(BF16)


def level_two_picks():
    pick = np.zeros((432, 27), np.float32)
    for tap in range(27):
        for r in range(16):
            y, z = r // 4 + tap // 3 % 3 - 1, r % 4 + tap % 3 - 1
            pick[16 * tap + r, tap // 9 * 9 + 3 * (y // 4 + 1) + z // 4 + 1] = 16
    return jnp.asarray(pick, BF16)


def level_three_picks():
    pick = np.zeros((27 * 16, 27), np.float32)
    for tap in range(27):
        for r in range(16):
            x, y, z = [
                n + d - 1
                for n, d in (
                    (r // 8, tap // 9), (r // 2 % 2, tap // 3 % 3), (r % 2, tap % 3)
                )
            ]
            pick[16 * tap + r, 9 * (x // 2 + 1) + 3 * (y // 2 + 1) + z // 2 + 1] = 4
    return jnp.asarray(pick, BF16)


def child_rows(planes):
    pick = np.zeros((8 * planes * 8, 2 * 2 * planes * 16), np.float32)
    for q in range(8):
        for r in range(8 * planes):
            x, y, z = [
                2 * n + (q >> s & 1) for n, s in ((r // 8, 2), (r // 2 % 2, 1), (r % 2, 0))
            ]
            at = 2 * planes * 16 * (r // 4 % 2) + 16 * x + 4 * y + z
            pick[8 * planes * q + r, at] = 1
    return jnp.asarray(pick, BF16)


ANY = pl.BlockSpec(memory_space=pl.ANY)
VMEM = pl.BlockSpec(memory_space=pltpu.VMEM)
DMA = pltpu.SemaphoreType.DMA


def call(kernel, cost, out_shape, scratch, *args, remain=(), store=()):
    single = not isinstance(out_shape, tuple)
    outs = (out_shape,) if single else out_shape
    specs = tuple(ANY if n in store else VMEM for n in range(len(outs)))
    return pl.pallas_call(
        kernel,
        out_shape=out_shape,
        in_specs=[ANY if n in remain else VMEM for n in range(len(args))],
        out_specs=specs[0] if single else specs,
        scratch_shapes=scratch,
        compiler_params=pltpu.CompilerParams(vmem_limit_bytes=24 * 1024 * 1024),
        cost_estimate=pl.CostEstimate(
            flops=int(cost * 10**10), bytes_accessed=10**7, transcendentals=0
        ),
    )(*args)


def swaps(tiles, count):
    within, across = [], []
    for t in range(tiles):
        for m in range(count):
            if m ^ 1 < count:
                within.append((t * count + m, t * count + (m ^ 1)))
            other = ((m - 1) ^ 1) + 1 if m else -1
            if 0 <= other < count:
                across.append((t * count + m, t * count + other))
            elif t ^ 1 < tiles:
                across.append((t * count + m, (t ^ 1) * count + m))
    return within, across


def on_device(
    features,
    neighbours,
    occupancy,
    conv_one,
    first_reduce_kernel,
    conv_two,
    second_reduce_kernel,
    conv_three,
):
    axes = ("tiles", LINE)
    within, across = swaps(lax.axis_size("tiles"), lax.axis_size(LINE))
    count = features.shape[0]
    features = jnp.swapaxes(features, 1, 2)
    shape = jax.ShapeDtypeStruct

    def exchange(to_a, to_b):
        from_b = lax.ppermute(to_b, axes, across)
        return lax.ppermute(to_a, axes, within), from_b

    blank = call(blank_kernel, 1.0, shape((2 * count, 128), F32), [])
    bits, edge_bits, pair_words, mask_two, mask_three = call(
        masks_kernel,
        0.01,
        (
            shape((4, count, 128), F32),
            shape((2, count, 128), F32),
            shape((8, count, 128), jnp.int32),
            shape((4, 16 * count, 128), F32),
            shape((8 * count, 256), F32),
        ),
        [],
        occupancy, blank,
    )
    to_b = call(
        far_edge_kernel,
        0.02,
        shape((32 * count + 2 * count, 128), BF16),
        [pltpu.VMEM((2 * count, 128), F32)],
        features, bits, neighbours, edge_bits, blank,
    )
    face = shape((count // 2, 64, 128), BF16)
    to_a = call(near_edge_kernel, 0.02, face, [], features, bits, to_b)
    from_a, message = exchange(to_a, to_b)
    middle, taps, face_taps, reduce_taps, partial = call(
        outer_kernel,
        2.0,
        (
            shape((count, 3, 6, 16, 128), BF16),
            shape((9 * 128, 256), BF16),
            shape((9 * 128, 128), BF16),
            shape((256, 256), BF16),
            shape((4, count * 64, 128), F32),
        ),
        [
            pltpu.VMEM((4, count + 1, 64, 128), F32),
            pltpu.VMEM((count, 3, 4, 6, 16, 128), BF16),
            pltpu.VMEM((9 * 128, 256), BF16),
        ],
        neighbours, bits, features, conv_one, first_reduce_kernel,
    )
    plane = shape((16 * count, 128), BF16)
    rows = shape((count, 2, 64, 128), BF16)
    sums = pltpu.VMEM((count * 64, 128), F32)
    inner, inner_two = call(
        inner_kernel,
        0.05,
        (rows, shape((2, 16 * count, 128), BF16)),
        [sums, sums],
        middle, taps, partial, reduce_taps, pair_words, mask_two,
    )
    outer, outer_two, to_b = call(
        faces_one_kernel,
        1.5,
        (rows, shape((2 * 16 * count, 128), BF16), shape((3 * 16 * count, 128), BF16)),
        [
            pltpu.VMEM((count + 1, 64, 128), F32),
            pltpu.VMEM((count, 3, 6, 16, 128), BF16),
            sums,
            sums,
        ],
        neighbours, from_a, message, face_taps, partial, reduce_taps, pair_words, mask_two,
        inner_two,
    )
    to_a = call(near_face_kernel, 0.02, plane, [], outer_two, to_b)
    from_a, from_b = exchange(to_a, to_b)

    pick = level_two_picks()
    table = shape((9 * 16 * count, 16 * count), BF16)
    own_two, sides_two = call(
        level_two_tables_kernel,
        0.05,
        (table, shape((2, 9 * 16 * count, 16 * count), BF16)),
        [],
        neighbours, pick, to_a,
    )
    far_two, far_mask_two, far_mask_three = call(
        far_tables_kernel,
        0.05,
        (
            shape((9 * 16 * count, 32 * count), BF16),
            shape((2 * 16 * count, 128), F32),
            shape((4 * count, 256), F32),
        ),
        [],
        message, pick, to_a,
    )
    first_level = call(output_kernel, 0.05, shape(features.shape, BF16), [], outer, inner)
    partial, first_level = call(
        own_two_kernel,
        1.0,
        (shape((4 * 16 * count, 128), F32), shape(features.shape, BF16)),
        [DMA(())],
        outer_two, inner_two, own_two, sides_two, from_a, conv_two, first_level,
        store=(1,),
    )
    own_three, near_three = call(
        level_three_tables_kernel,
        0.05,
        (shape((27 * 8 * count, 12 * count), BF16), shape((9 * 4 * count, 4 * count), BF16)),
        [],
        neighbours, level_three_picks(), to_a,
    )
    face = shape((4 * count, 256), BF16)
    second_level, third, far_third = call(
        faces_two_kernel,
        1.5,
        (shape((count, 64, 128), BF16), shape((8 * count, 256), BF16), face),
        [],
        sides_two, far_two, child_rows(2), child_rows(1), partial, to_b, from_b, conv_two,
        second_reduce_kernel, mask_two, mask_three, far_mask_two, far_mask_three,
    )
    to_a = call(near_face_kernel, 0.02, face, [], third, far_third)
    from_a = lax.ppermute(to_a, axes, within)
    partial, second_level = call(
        own_three_kernel,
        1.0,
        (shape((8 * count, 256), F32), shape(second_level.shape, BF16)),
        [DMA(())],
        own_three, third, far_third, conv_three, second_level,
        store=(1,),
    )
    third_level = call(
        faces_three_kernel,
        1,
        shape((count, 8, 256), BF16),
        [],
        near_three, partial, from_a, conv_three, mask_three,
    )
    return jnp.swapaxes(first_level, 1, 2), second_level, third_level


def solution(mesh):
    split = P(("tiles", LINE))
    return jax.shard_map(
        on_device,
        mesh=mesh,
        in_specs=(split, split, split, P(), P(), P(), P(), P()),
        out_specs=(split, split, split),
        check_vma=False,
    )
```

```python
import jax
import jax.numpy as jnp
import numpy as np
from jax import lax
from jax.experimental import pallas as pl
from jax.experimental.pallas import tpu as pltpu
from jax.sharding import PartitionSpec as P

F32 = jnp.float32
BF16 = jnp.bfloat16
LINE = "morton"


def dot(x, y):
    return jnp.dot(x, y, preferred_element_type=F32)


def iota(shape, axis):
    return lax.broadcasted_iota(jnp.int32, shape, axis)


def stack(parts):
    return jnp.concatenate(parts, axis=0)


def beside(parts):
    return jnp.concatenate(parts, axis=1)


def bits_of(words, shift):
    return jnp.bitwise_and(lax.shift_right_logical(words, shift), 1).astype(F32)


def either(x, y):
    return jnp.bitwise_or(x, y)


def on_odd_place():
    return lax.rem(lax.axis_index(LINE), 2) == 1


def word_lanes(words, w):
    return jnp.broadcast_to(words[:, w : w + 1], (words.shape[0], 128))


def column_bits(words, column):
    lane = iota((words.shape[0], 128), 1)
    w = [word_lanes(words, 4 * column + q) for q in range(4)]
    chosen = jnp.where(
        lane < 64, jnp.where(lane < 32, w[0], w[1]), jnp.where(lane < 96, w[2], w[3])
    )
    return bits_of(chosen, jnp.bitwise_and(lane, 31))


def slot_numbers(neighbours):
    count = neighbours.shape[0]
    number = neighbours[...]
    tap = iota(number.shape, 1)
    shift = jnp.where(tap < 9, count, jnp.where(tap < 18, 0, -count))
    return jnp.where(number < 0, count, number + shift - lax.axis_index(LINE) * count)


def blank_kernel(notes):
    notes[...] = jnp.zeros(notes.shape, F32)


def masks_kernel(occupancy, blank, bits, edge_bits, pair_words, mask_two, mask_three):
    count = occupancy.shape[0]
    for q in range(4):
        bits[q] = column_bits(occupancy[...], q)
    words = [word_lanes(occupancy[...], w) for w in range(16)]
    lane = iota((count, 128), 1)
    row = iota((8, 128), 0)
    any_two = []
    for i in range(4):
        for half in range(2):
            low, high = words[4 * i + half], words[4 * i + 2 + half]
            pair_words[2 * i + half] = jnp.where(lane < 64, low, high)
            word = either(low, high)
            word = either(word, lax.shift_right_logical(word, 1))
            any_two.append(either(word, lax.shift_right_logical(word, 8)))
    two_shift = 16 * lax.shift_right_logical(row, 2) + 2 * jnp.bitwise_and(row, 3)
    for i in range(4):
        for b in range(count):
            mask_two[i, 16 * b : 16 * (b + 1)] = stack(
                [
                    bits_of(
                        jnp.broadcast_to(any_two[2 * i + half][b : b + 1], (8, 128)), two_shift
                    )
                    for half in range(2)
                ]
            )
    plane, half, m = [jnp.bitwise_and(lax.shift_right_logical(lane, n), 1) for n in (4, 3, 2)]
    for side in range(2):
        word = [any_two[4 * side + n] for n in range(4)]
        word = jnp.where(
            plane == 0, jnp.where(half == 0, word[0], word[1]), jnp.where(half == 0, word[2], word[3])
        )
        edge_bits[side] = bits_of(word, 16 * m + 2 * jnp.bitwise_and(lane, 3))
    any_three = []
    for i in range(2):
        for j in range(2):
            word = either(any_two[4 * i + j], any_two[4 * i + 2 + j])
            word = either(word, lax.shift_right_logical(word, 16))
            any_three.append(either(word, lax.shift_right_logical(word, 2)))
    for i in range(2):
        for b in range(0, count, 2):
            tile = [
                jnp.broadcast_to(any_three[2 * i + j][n : n + 1], (8, 128))
                for n in (b, b + 1)
                for j in range(2)
            ]
            tile = jnp.where(
                row < 4, jnp.where(row < 2, tile[0], tile[1]), jnp.where(row < 6, tile[2], tile[3])
            )
            mask = bits_of(tile, 4 * jnp.bitwise_and(row, 1))
            at = 4 * (count * i + b)
            mask_three[at : at + 8] = beside([mask, mask])


def edge_planes(features, bits, low_wanted):
    last = features.shape[2] - 128
    planes = []
    for q in range(features.shape[0] // 2):
        low, high = [
            [
                features[b, :, column * last : column * last + 128]
                * bits[3 * column, b : b + 1].astype(BF16)
                for b in (2 * q, 2 * q + 1)
            ]
            for column in range(2)
        ]
        lows = beside([low[0][:, :64], low[1][:, :64]])
        highs = beside([high[0][:, 64:], high[1][:, 64:]])
        planes.append(jnp.where(low_wanted, lows, highs))
    return planes


def far_edge_kernel(features, bits, neighbours, edge_bits, blank, edge, notes):
    count = features.shape[0]
    odd = on_odd_place()
    for q, plane in enumerate(edge_planes(features, bits, jnp.logical_not(odd))):
        edge[64 * q : 64 * (q + 1), :] = plane
    notes[...] = blank[...]
    notes[:count, : neighbours.shape[1]] = jnp.where(
        neighbours[...] < 0, 4 * count, slot_numbers(neighbours)
    ).astype(F32)
    notes[count:, :] = edge_bits[jnp.where(odd, 1, 0)]
    edge[32 * count :, :] = notes[...].astype(BF16)


def near_edge_kernel(features, bits, earlier, edge):
    for q, plane in enumerate(edge_planes(features, bits, on_odd_place())):
        edge[q] = plane


def near_face_kernel(planes, earlier, face):
    rows = face.shape[0]
    begin = pl.multiple_of(jnp.where(on_odd_place(), 0, rows), rows)
    face[...] = planes[pl.ds(begin, rows), :]


def slot_rows(slot):
    return stack(
        [jnp.broadcast_to(slot[b : b + 1], (128, slot.shape[1])) for b in range(slot.shape[0])]
    ).astype(BF16)


def own_slot_rows(neighbours):
    slot = jnp.where(neighbours[...] < 0, 4 * neighbours.shape[0], slot_numbers(neighbours))
    return slot_rows(slot.astype(F32))


def times_transposed(x, y):
    return lax.dot_general(x, y, (((1,), (1,)), ((), ())), preferred_element_type=F32)


def fill_level_two_tables(tables, rows, count):
    lane = iota((16, 16 * count), 1)
    row = iota((16, 16 * count), 0)
    j, k = lax.shift_right_logical(row, 2), jnp.bitwise_and(row, 3)
    for q in range(9):
        source = 4 * jnp.bitwise_and(j + q // 3 + 3, 3) + jnp.bitwise_and(k + q % 3 + 3, 3)
        wanted = (lane - source).astype(F32)
        for a, table in enumerate(tables):
            at = 16 * (9 * a + q)
            for b in range(count):
                table[16 * (count * q + b) : 16 * (count * q + b + 1), :] = jnp.where(
                    rows[at : at + 16, 128 * b : 128 * b + 16 * count] == wanted, 1.0, 0.0
                ).astype(BF16)


def level_two_tables_kernel(neighbours, pick, later, own_two, sides_two):
    rows = times_transposed(pick[...], own_slot_rows(neighbours))
    fill_level_two_tables(
        (sides_two.at[0], own_two, sides_two.at[1]), rows, neighbours.shape[0]
    )


def far_tables_kernel(message, pick, later, gather, mask_two, mask_three):
    count = gather.shape[1] // 32
    notes = message[32 * count :, :].astype(F32)
    slots = slot_rows(notes[:count, : pick.shape[1]])
    begin = pl.multiple_of(jnp.where(on_odd_place(), 0, 288), 16)
    rows = stack(
        [
            times_transposed(pick[pl.ds(begin, 144), :], slots),
            times_transposed(pick[144:288, :], slots),
        ]
    )
    width = 16 * count
    fill_level_two_tables((gather.at[:, width:], gather.at[:, :width]), rows, count)

    every = jnp.ones((128, 256), BF16)
    lane = iota((16, 128), 1)
    row = iota((16, 128), 0)
    bits = [notes[count + b : count + b + 1] for b in range(count)]
    chosen = stack(
        [
            jnp.where(lane == 16 * plane + row, jnp.broadcast_to(bits[b], (16, 128)), 0.0)
            for plane in range(2)
            for b in range(count)
        ]
    ).astype(BF16)
    mask_two[...] = dot(chosen, every[:, :128])
    lane, row = lane[:8], row[:8]
    child = jnp.bitwise_and(lax.shift_right_logical(lane, 2), 2) + jnp.bitwise_and(
        lax.shift_right_logical(lane, 1), 1
    )
    wanted = (child == jnp.bitwise_and(row, 3)) & (lane < 32)
    chosen = stack(
        [
            jnp.where(wanted, jnp.where(row < 4, bits[b], bits[b + 1]), 0.0)
            for b in range(0, count, 2)
        ]
    ).astype(BF16)
    mask_three[...] = jnp.where(dot(chosen, every) > 0.5, 1.0, 0.0)


def level_three_tables_kernel(neighbours, pick, later, own_three, near_three):
    count = neighbours.shape[0]
    odd = on_odd_place()
    rows = times_transposed(pick[...], own_slot_rows(neighbours))
    row = iota((8, 128), 0)
    lane = iota((8, 128), 1)
    j, k = [jnp.bitwise_and(lax.shift_right_logical(row, n), 1) for n in (1, 0)]

    def block(tap, i, begin):
        c, e = tap // 3 % 3, tap % 3
        source = 2 * jnp.bitwise_and(j + c + 1, 1) + jnp.bitwise_and(k + e + 1, 1)
        wanted = (lane - source - begin).astype(F32)
        at = 8 * (2 * tap + i)
        tiles = []
        for b in range(0, count, 2):
            first, second = [rows[at : at + 8, 128 * n : 128 * (n + 1)] for n in (b, b + 1)]
            hit = jnp.where(row < 4, first, second) == wanted
            tiles.append(jnp.where(hit, 1.0, 0.0))
        return stack(tiles)

    nowhere = 16 * 4 * count
    for tap in range(27):
        for i in range(2):
            x = i + tap // 9 - 1
            if x < 0:
                begin = jnp.where(odd, nowhere, 8 * count)
            elif x > 1:
                begin = jnp.where(odd, 8 * count, nowhere)
            else:
                begin = 4 * count * x
            at = 8 * count * tap + 4 * count * i
            own_three[at : at + 4 * count, :] = block(tap, i, begin)[:, : 12 * count].astype(BF16)
    for q in range(9):
        tile = jnp.where(odd, block(q, 0, 0), block(18 + q, 1, 0))
        near_three[4 * count * q : 4 * count * (q + 1), :] = tile[:, : 4 * count].astype(BF16)


def shifted_windows(source, row):
    shifted = []
    for j in range(-1, 9):
        c, at = (0, 7) if j < 0 else (2, 0) if j > 7 else (1, j)
        left, mid, right = [source(3 * c + e, at) for e in range(3)]
        shifted.append(
            (
                pltpu.roll(jnp.where(row == 7, left, mid), 1, 0),
                mid,
                pltpu.roll(jnp.where(row == 0, right, mid), 7, 0),
            )
        )
    return [
        [stack([shifted[jr][e], shifted[jr + 4][e]]).astype(BF16) for e in range(3)]
        for jr in range(6)
    ]


def outer_kernel(
    neighbours, bits, features, kernel, reduce,
    middle, taps, face_taps, reduce_taps, partial,
    tables, windows, wrap_taps,
):
    count = features.shape[0]
    row = iota((8, 128), 0)
    numbers = slot_numbers(neighbours)

    none = jnp.zeros((64, 64), BF16)
    for q in range(9):
        w = [kernel[9 * a + q] for a in range(3)]
        rows = slice(q * 128, (q + 1) * 128)
        taps[rows, :] = stack(
            [beside([w[2], w[1], w[0], none]), beside([none, w[2], w[1], w[0]])]
        )
        wrap_taps[rows, :] = stack(
            [beside([w[2], w[1], none, none]), beside([none, none, w[1], w[0]])]
        )
        face_taps[rows, :] = stack([beside([w[0], none]), beside([none, w[2]])])

    reduce_taps[...] = stack(
        [
            beside([reduce[4 * ci + 2 * cj], reduce[4 * ci + 2 * cj + 1]])
            for cj in range(2)
            for ci in range(2)
        ]
    )

    for pair in range(4):
        tables[pair, count] = jnp.zeros((64, 128), F32)
    for b in range(count):
        cols = [
            features[b, :, 128 * q : 128 * (q + 1)] * bits[q, b : b + 1].astype(BF16)
            for q in range(4)
        ]
        for p in (0, 2):
            m = stack(
                [
                    beside([cols[p][:, 64:], cols[p + 1][:, 64:]]),
                    beside([cols[p + 1][:, :64], cols[(p + 2) % 4][:, :64]]),
                ]
            ).T
            tables[p, b] = m[:64].astype(F32)
            tables[p + 1, b] = m[64:].astype(F32)

    for b in range(count):
        slot = [numbers[b, 9 + q] for q in range(9)]
        for pair in range(4):
            tiles = shifted_windows(lambda q, j: tables[pair, slot[q], pl.ds(8 * j, 8), :], row)
            for jr in range(6):
                for e in range(3):
                    if pair == 1:
                        middle[b, e, jr] = tiles[jr][e]
                    else:
                        windows[b, e, pair, jr] = tiles[jr][e]

    group = count // 2
    for g in range(2):
        bricks = slice(g * group, (g + 1) * group)
        rows = slice(g * group * 64, (g + 1) * group * 64)
        low, high, wrap = [
            dot(
                beside(
                    [
                        windows[bricks, e, pair, c : c + 4].reshape(group * 64, 128)
                        for c in range(3)
                        for e in range(3)
                    ]
                ),
                weights[...],
            )
            for pair, weights in ((0, taps), (2, taps), (3, wrap_taps))
        ]
        partial[0, rows] = low[:, :128] + wrap[:, 128:]
        partial[1, rows] = low[:, 128:]
        partial[2, rows] = high[:, :128]
        partial[3, rows] = high[:, 128:] + wrap[:, :128]


def masked_tiles(sums, pair_words, b, i):
    row = iota((8, 128), 0)
    tiles = {}
    for half in range(2):
        words = jnp.broadcast_to(pair_words[2 * i + half, b : b + 1, :], (8, 128))
        for jr in range(4):
            at = jr * 16 + half * 8
            tiles[4 * half + jr] = jnp.maximum(sums[at : at + 8], 0.0) * bits_of(
                words, row + 8 * jr
            )
    return [tiles[j] for j in range(8)]


def reduce_planes(groups, weights, low_sums, high_sums):
    left = stack(
        [beside([tiles[j], tiles[j + 1]]) for tiles in groups for j in (0, 2, 4, 6)]
    ).astype(BF16)
    sums = dot(left, weights[...])
    low_sums[: sums.shape[0], :] = sums[:, :128]
    high_sums[: sums.shape[0], :] = sums[:, 128:]
    return [
        low_sums[pl.ds(32 * g, 16, stride=2), :] + high_sums[pl.ds(32 * g + 1, 16, stride=2), :]
        for g in range(len(groups))
    ]


def faces_one_kernel(
    neighbours, from_a, from_b, face_taps, partial, reduce, pair_words, mask_two, inner,
    outer, second, to_b,
    halo, windows, low_sums, high_sums,
):
    count = outer.shape[0]
    lane = iota((64, 128), 1)
    small = iota((8, 128), 1)
    row = iota((8, 128), 0)
    odd = on_odd_place()
    slot = slot_numbers(neighbours)
    halo[count] = jnp.zeros((64, 128), F32)
    for q in range(count // 2):
        one, two = from_a[q], from_b[64 * q : 64 * (q + 1), :]
        m = stack([jnp.where(odd, one, two), jnp.where(odd, two, one)]).T
        halo[2 * q] = m[:64].astype(F32)
        halo[2 * q + 1] = m[64:].astype(F32)
    for b in range(count):
        low = [slot[b, q] for q in range(9)]
        high = [slot[b, 18 + q] for q in range(9)]

        def source(q, j):
            rows = pl.ds(8 * j, 8)
            return jnp.where(small < 64, halo[low[q], rows, :], halo[high[q], rows, :])

        tiles = shifted_windows(source, row)
        for jr in range(6):
            for e in range(3):
                windows[b, e, jr] = tiles[jr][e]
    added = dot(
        beside(
            [
                windows[:, e, c : c + 4].reshape(count * 64, 128)
                for c in range(3)
                for e in range(3)
            ]
        ),
        face_taps[...],
    )
    groups = []
    for b in range(count):
        at = slice(64 * b, 64 * (b + 1))
        for side in range(2):
            near = (lane < 64) == (side == 0)
            sums = partial[3 * side, at] + jnp.where(near, added[at], 0.0)
            groups.append(masked_tiles(sums, pair_words, b, 3 * side))
            outer[b, side] = stack(groups[-1]).astype(BF16)
    sums = reduce_planes(groups, reduce, low_sums, high_sums)
    for b in range(count):
        at = slice(16 * b, 16 * (b + 1))
        planes = [
            (jnp.maximum(sums[2 * b + side], 0.0) * mask_two[3 * side, at]).astype(BF16)
            for side in range(2)
        ]
        second[16 * b : 16 * (b + 1)] = planes[0]
        second[16 * (count + b) : 16 * (count + b + 1)] = planes[1]
        to_b[at] = jnp.where(odd, planes[1], planes[0])
    rows = 16 * count
    to_b[rows : 2 * rows] = jnp.where(odd, inner[1], inner[0])
    to_b[2 * rows :] = jnp.where(odd, inner[0], inner[1])


def inner_kernel(
    middle, taps, partial, reduce, pair_words, mask_two,
    inner, second,
    low_sums, high_sums,
):
    count = middle.shape[0]
    added = dot(
        beside(
            [
                middle[:, e, c : c + 4].reshape(count * 64, 128)
                for c in range(3)
                for e in range(3)
            ]
        ),
        taps[...],
    )
    groups = []
    for b in range(count):
        at = slice(64 * b, 64 * (b + 1))
        for i in (1, 2):
            sums = partial[i, at] + added[at, 128 * (i - 1) : 128 * i]
            groups.append(masked_tiles(sums, pair_words, b, i))
            inner[b, i - 1] = stack(groups[-1]).astype(BF16)
    sums = reduce_planes(groups, reduce, low_sums, high_sums)
    for b in range(count):
        at = slice(16 * b, 16 * (b + 1))
        for i in (1, 2):
            second[i - 1, at] = (
                jnp.maximum(sums[2 * b + i - 1], 0.0) * mask_two[i, at]
            ).astype(BF16)


def output_kernel(outer, inner, out):
    for b in range(outer.shape[0]):
        ordered = [outer[b, 0], inner[b, 0], inner[b, 1], outer[b, 1]]
        for i in (0, 2):
            m = stack(ordered[i : i + 2]).T
            top, bottom = m[:64], m[64:]
            out[b, :, 128 * i : 128 * (i + 1)] = beside([top[:, :64], bottom[:, :64]])
            out[b, :, 128 * (i + 1) : 128 * (i + 2)] = beside([top[:, 64:], bottom[:, 64:]])


def face_part(gather, face, kernel, high):
    moved = dot(gather, face).astype(BF16)
    rows = moved.shape[0] // 9
    left = beside([moved[q * rows : (q + 1) * rows] for q in range(9)])
    weights = kernel[pl.ds(18 * high, 9)]
    return dot(left, weights.reshape(9 * weights.shape[1], weights.shape[2]))


def own_two_kernel(
    outer, inner, own_gather, gathers, from_a, kernel, first,
    partial, result, stored,
):
    copy = pltpu.make_async_copy(first, result, stored)
    copy.start()
    rows = inner.shape[1]
    planes = beside([outer[:rows], inner[0], inner[1], outer[rows:]])
    moved = dot(own_gather[...], planes).astype(BF16)
    left = beside(
        [
            stack(
                [
                    moved[q * rows : (q + 1) * rows, 128 * i : 128 * (i + 1)]
                    for i in range(4)
                ]
            )
            for q in range(9)
        ]
    )
    weights = [kernel[9 * a : 9 * (a + 1)].reshape(9 * 128, 128) for a in range(3)]
    sums = dot(left, beside(weights[:2]))
    later = dot(left[rows:], weights[2])
    high = jnp.where(on_odd_place(), 0, 1)
    near = face_part(gathers[high], from_a[...], kernel, high)
    for i in range(4):
        total = sums[i * rows : (i + 1) * rows, 128:]
        if i:
            total = total + sums[(i - 1) * rows : i * rows, :128]
        if i < 3:
            total = total + later[i * rows : (i + 1) * rows]
        if i in (0, 3):
            total = total + jnp.where(high == i // 3, near, 0.0)
        partial[i * rows : (i + 1) * rows] = total
    copy.wait()


def child_columns(picked, pairs, planes):
    return beside(
        [
            stack(
                [
                    picked[8 * (planes * q + i) : 8 * (planes * q + i + 1), 128 * n : 128 * (n + 1)]
                    for i in range(planes)
                    for n in range(pairs)
                ]
            )
            for q in range(8)
        ]
    )


def faces_two_kernel(
    gathers, far_gather, children, far_children, partial, to_b, from_b, kernel, reduce,
    mask_two, mask_three, far_mask_two, far_mask_three,
    second, third, far_third,
):
    count = second.shape[0]
    rows = 16 * count
    odd = on_odd_place()
    high = jnp.where(odd, 1, 0)
    none = jnp.zeros((rows, 128), BF16)
    sent = [from_b[d * rows : (d + 1) * rows] for d in range(3)]
    moved = dot(
        far_gather[...],
        stack([beside(sent + [none]), beside([none, none, none, to_b[:rows]])]),
    ).astype(BF16)
    left = [
        beside([moved[q * rows : (q + 1) * rows, 128 * d : 128 * (d + 1)] for q in range(9)])
        for d in range(4)
    ]
    moved = dot(gathers[high], sent[0]).astype(BF16)
    left.append(beside([moved[q * rows : (q + 1) * rows] for q in range(9)]))
    toward, same, away = [
        kernel[pl.ds(begin, 9)].reshape(9 * 128, 128) for begin in (18 - 18 * high, 9, 18 * high)
    ]
    zero = dot(stack([left[0], left[3]]), beside([same, toward]))
    one = dot(left[1], beside([away, same]))
    near = zero[rows:, 128:] + zero[:rows, :128] + one[:, :128]
    two = dot(stack([left[2], left[4]]), away)
    past = zero[:rows, 128:] + one[:, 128:] + two[:rows]
    far = two[rows:]
    planes = []
    for i in range(4):
        sums = partial[i * rows : (i + 1) * rows]
        if i in (0, 3):
            sums = sums + jnp.where(high == i // 3, far, 0.0)
        planes.append((jnp.maximum(sums, 0.0) * mask_two[i]).astype(BF16))
    bricks = [
        stack([planes[i][16 * b : 16 * (b + 1)] for i in range(4)]) for b in range(count)
    ]
    for b in range(count):
        second[b] = bricks[b]
    picked = dot(
        children[...], beside([stack(bricks[b : b + 2]) for b in range(0, count, 2)])
    )

    far_planes = [
        (jnp.maximum(sums, 0.0) * far_mask_two[n * rows : (n + 1) * rows]).astype(BF16)
        for n, sums in enumerate((jnp.where(odd, near, past), jnp.where(odd, past, near)))
    ]
    far_picked = dot(
        far_children[...],
        beside(
            [
                stack(
                    [
                        plane[16 * b : 16 * (b + 1)]
                        for b in (n, n + 1)
                        for plane in far_planes
                    ]
                )
                for n in range(0, count, 2)
            ]
        ),
    )
    left = stack(
        [child_columns(picked, count // 2, 2), child_columns(far_picked, count // 2, 1)]
    ).astype(BF16)
    sums = jnp.maximum(dot(left, reduce[...].reshape(8 * 128, 256)), 0.0)
    third[...] = (sums[: 8 * count] * mask_three[...]).astype(BF16)
    far_third[...] = (sums[8 * count :] * far_mask_three[...]).astype(BF16)


def own_three_kernel(gather, third, far, kernel, second, partial, result, stored):
    copy = pltpu.make_async_copy(second, result, stored)
    copy.start()
    rows = third.shape[0]
    moved = dot(gather[...], stack([third[...], far[...]])).astype(BF16)
    left = beside([moved[q * rows : (q + 1) * rows] for q in range(27)])
    partial[...] = dot(left, kernel[...].reshape(27 * 256, 256))
    copy.wait()


def faces_three_kernel(gather, partial, from_a, kernel, mask_three, out):
    rows = from_a.shape[0]
    odd = on_odd_place()
    near = face_part(gather[...], from_a[...], kernel, jnp.where(odd, 0, 1))
    low = partial[:rows] + jnp.where(odd, near, 0.0)
    high = partial[rows:] + jnp.where(odd, 0.0, near)
    low = jnp.maximum(low, 0.0) * mask_three[:rows]
    high = jnp.maximum(high, 0.0) * mask_three[rows:]
    row = iota((8, 256), 0)
    for n in range(rows // 8):
        near, past = low[8 * n : 8 * (n + 1)], high[8 * n : 8 * (n + 1)]
        out[2 * n] = jnp.where(row < 4, near, pltpu.roll(past, 4, 0)).astype(BF16)
        out[2 * n + 1] = jnp.where(row < 4, pltpu.roll(near, 4, 0), past).astype(BF16)


def level_two_picks():
    pick = np.zeros((432, 27), np.float32)
    for tap in range(27):
        for r in range(16):
            y, z = r // 4 + tap // 3 % 3 - 1, r % 4 + tap % 3 - 1
            pick[16 * tap + r, tap // 9 * 9 + 3 * (y // 4 + 1) + z // 4 + 1] = 16
    return jnp.asarray(pick, BF16)


def level_three_picks():
    pick = np.zeros((27 * 16, 27), np.float32)
    for tap in range(27):
        for r in range(16):
            x, y, z = [
                n + d - 1
                for n, d in (
                    (r // 8, tap // 9), (r // 2 % 2, tap // 3 % 3), (r % 2, tap % 3)
                )
            ]
            pick[16 * tap + r, 9 * (x // 2 + 1) + 3 * (y // 2 + 1) + z // 2 + 1] = 4
    return jnp.asarray(pick, BF16)


def child_rows(planes):
    pick = np.zeros((8 * planes * 8, 2 * 2 * planes * 16), np.float32)
    for q in range(8):
        for r in range(8 * planes):
            x, y, z = [
                2 * n + (q >> s & 1) for n, s in ((r // 8, 2), (r // 2 % 2, 1), (r % 2, 0))
            ]
            at = 2 * planes * 16 * (r // 4 % 2) + 16 * x + 4 * y + z
            pick[8 * planes * q + r, at] = 1
    return jnp.asarray(pick, BF16)


ANY = pl.BlockSpec(memory_space=pl.ANY)
VMEM = pl.BlockSpec(memory_space=pltpu.VMEM)
DMA = pltpu.SemaphoreType.DMA


def call(kernel, cost, out_shape, scratch, *args, remain=(), store=()):
    single = not isinstance(out_shape, tuple)
    outs = (out_shape,) if single else out_shape
    specs = tuple(ANY if n in store else VMEM for n in range(len(outs)))
    return pl.pallas_call(
        kernel,
        out_shape=out_shape,
        in_specs=[ANY if n in remain else VMEM for n in range(len(args))],
        out_specs=specs[0] if single else specs,
        scratch_shapes=scratch,
        compiler_params=pltpu.CompilerParams(vmem_limit_bytes=24 * 1024 * 1024),
        cost_estimate=pl.CostEstimate(
            flops=int(cost * 10**10), bytes_accessed=10**7, transcendentals=0
        ),
    )(*args)


def swaps(tiles, count):
    within, across = [], []
    for t in range(tiles):
        for m in range(count):
            if m ^ 1 < count:
                within.append((t * count + m, t * count + (m ^ 1)))
            other = ((m - 1) ^ 1) + 1 if m else -1
            if 0 <= other < count:
                across.append((t * count + m, t * count + other))
            elif t ^ 1 < tiles:
                across.append((t * count + m, (t ^ 1) * count + m))
    return within, across


def on_device(
    features,
    neighbours,
    occupancy,
    conv_one,
    first_reduce_kernel,
    conv_two,
    second_reduce_kernel,
    conv_three,
):
    axes = ("tiles", LINE)
    within, across = swaps(lax.axis_size("tiles"), lax.axis_size(LINE))
    count = features.shape[0]
    features = jnp.swapaxes(features, 1, 2)
    shape = jax.ShapeDtypeStruct

    def exchange(to_a, to_b):
        from_b = lax.ppermute(to_b, axes, across)
        return lax.ppermute(to_a, axes, within), from_b

    blank = call(blank_kernel, 1.0, shape((2 * count, 128), F32), [])
    bits, edge_bits, pair_words, mask_two, mask_three = call(
        masks_kernel,
        0.01,
        (
            shape((4, count, 128), F32),
            shape((2, count, 128), F32),
            shape((8, count, 128), jnp.int32),
            shape((4, 16 * count, 128), F32),
            shape((8 * count, 256), F32),
        ),
        [],
        occupancy, blank,
    )
    to_b = call(
        far_edge_kernel,
        0.02,
        shape((32 * count + 2 * count, 128), BF16),
        [pltpu.VMEM((2 * count, 128), F32)],
        features, bits, neighbours, edge_bits, blank,
    )
    face = shape((count // 2, 64, 128), BF16)
    to_a = call(near_edge_kernel, 0.02, face, [], features, bits, to_b)
    from_a, message = exchange(to_a, to_b)
    middle, taps, face_taps, reduce_taps, partial = call(
        outer_kernel,
        2.0,
        (
            shape((count, 3, 6, 16, 128), BF16),
            shape((9 * 128, 256), BF16),
            shape((9 * 128, 128), BF16),
            shape((256, 256), BF16),
            shape((4, count * 64, 128), F32),
        ),
        [
            pltpu.VMEM((4, count + 1, 64, 128), F32),
            pltpu.VMEM((count, 3, 4, 6, 16, 128), BF16),
            pltpu.VMEM((9 * 128, 256), BF16),
        ],
        neighbours, bits, features, conv_one, first_reduce_kernel,
    )
    plane = shape((16 * count, 128), BF16)
    rows = shape((count, 2, 64, 128), BF16)
    sums = pltpu.VMEM((count * 64 + 8, 128), F32)
    inner, inner_two = call(
        inner_kernel,
        0.05,
        (rows, shape((2, 16 * count, 128), BF16)),
        [sums, sums],
        middle, taps, partial, reduce_taps, pair_words, mask_two,
    )
    outer, outer_two, to_b = call(
        faces_one_kernel,
        1.5,
        (rows, shape((2 * 16 * count, 128), BF16), shape((3 * 16 * count, 128), BF16)),
        [
            pltpu.VMEM((count + 1, 64, 128), F32),
            pltpu.VMEM((count, 3, 6, 16, 128), BF16),
            sums,
            sums,
        ],
        neighbours, from_a, message, face_taps, partial, reduce_taps, pair_words, mask_two,
        inner_two,
    )
    to_a = call(near_face_kernel, 0.02, plane, [], outer_two, to_b)
    from_a, from_b = exchange(to_a, to_b)

    pick = level_two_picks()
    table = shape((9 * 16 * count, 16 * count), BF16)
    own_two, sides_two = call(
        level_two_tables_kernel,
        0.05,
        (table, shape((2, 9 * 16 * count, 16 * count), BF16)),
        [],
        neighbours, pick, to_a,
    )
    far_two, far_mask_two, far_mask_three = call(
        far_tables_kernel,
        0.05,
        (
            shape((9 * 16 * count, 32 * count), BF16),
            shape((2 * 16 * count, 128), F32),
            shape((4 * count, 256), F32),
        ),
        [],
        message, pick, to_a,
    )
    first_level = call(output_kernel, 0.05, shape(features.shape, BF16), [], outer, inner)
    partial, first_level = call(
        own_two_kernel,
        1.0,
        (shape((4 * 16 * count, 128), F32), shape(features.shape, BF16)),
        [DMA(())],
        outer_two, inner_two, own_two, sides_two, from_a, conv_two, first_level,
        store=(1,),
    )
    own_three, near_three = call(
        level_three_tables_kernel,
        0.05,
        (shape((27 * 8 * count, 12 * count), BF16), shape((9 * 4 * count, 4 * count), BF16)),
        [],
        neighbours, level_three_picks(), to_a,
    )
    face = shape((4 * count, 256), BF16)
    second_level, third, far_third = call(
        faces_two_kernel,
        1.5,
        (shape((count, 64, 128), BF16), shape((8 * count, 256), BF16), face),
        [],
        sides_two, far_two, child_rows(2), child_rows(1), partial, to_b, from_b, conv_two,
        second_reduce_kernel, mask_two, mask_three, far_mask_two, far_mask_three,
    )
    to_a = call(near_face_kernel, 0.02, face, [], third, far_third)
    from_a = lax.ppermute(to_a, axes, within)
    partial, second_level = call(
        own_three_kernel,
        1.0,
        (shape((8 * count, 256), F32), shape(second_level.shape, BF16)),
        [DMA(())],
        own_three, third, far_third, conv_three, second_level,
        store=(1,),
    )
    third_level = call(
        faces_three_kernel,
        1,
        shape((count, 8, 256), BF16),
        [],
        near_three, partial, from_a, conv_three, mask_three,
    )
    return jnp.swapaxes(first_level, 1, 2), second_level, third_level


def solution(mesh):
    split = P(("tiles", LINE))
    return jax.shard_map(
        on_device,
        mesh=mesh,
        in_specs=(split, split, split, P(), P(), P(), P(), P()),
        out_specs=(split, split, split),
        check_vma=False,
    )
```

```python
import jax
import jax.numpy as jnp
import numpy as np
from jax import lax
from jax.experimental import pallas as pl
from jax.experimental.pallas import tpu as pltpu
from jax.sharding import PartitionSpec as P

F32 = jnp.float32
BF16 = jnp.bfloat16
LINE = "morton"


def dot(x, y):
    return jnp.dot(x, y, preferred_element_type=F32)


def iota(shape, axis):
    return lax.broadcasted_iota(jnp.int32, shape, axis)


def stack(parts):
    return jnp.concatenate(parts, axis=0)


def beside(parts):
    return jnp.concatenate(parts, axis=1)


def bits_of(words, shift):
    return jnp.bitwise_and(lax.shift_right_logical(words, shift), 1).astype(F32)


def either(x, y):
    return jnp.bitwise_or(x, y)


def on_odd_place():
    return lax.rem(lax.axis_index(LINE), 2) == 1


def word_lanes(words, w):
    return jnp.broadcast_to(words[:, w : w + 1], (words.shape[0], 128))


def column_bits(words, column):
    lane = iota((words.shape[0], 128), 1)
    w = [word_lanes(words, 4 * column + q) for q in range(4)]
    chosen = jnp.where(
        lane < 64, jnp.where(lane < 32, w[0], w[1]), jnp.where(lane < 96, w[2], w[3])
    )
    return bits_of(chosen, jnp.bitwise_and(lane, 31))


def slot_numbers(neighbours):
    count = neighbours.shape[0]
    number = neighbours[...]
    tap = iota(number.shape, 1)
    shift = jnp.where(tap < 9, count, jnp.where(tap < 18, 0, -count))
    return jnp.where(number < 0, count, number + shift - lax.axis_index(LINE) * count)


def blank_kernel(notes):
    notes[...] = jnp.zeros(notes.shape, F32)


def masks_kernel(occupancy, blank, bits, edge_bits, pair_words, mask_two, mask_three):
    count = occupancy.shape[0]
    for q in range(4):
        bits[q] = column_bits(occupancy[...], q)
    words = [word_lanes(occupancy[...], w) for w in range(16)]
    lane = iota((count, 128), 1)
    row = iota((8, 128), 0)
    any_two = []
    for i in range(4):
        for half in range(2):
            low, high = words[4 * i + half], words[4 * i + 2 + half]
            pair_words[2 * i + half] = jnp.where(lane < 64, low, high)
            word = either(low, high)
            word = either(word, lax.shift_right_logical(word, 1))
            any_two.append(either(word, lax.shift_right_logical(word, 8)))
    two_shift = 16 * lax.shift_right_logical(row, 2) + 2 * jnp.bitwise_and(row, 3)
    for i in range(4):
        for b in range(count):
            mask_two[i, 16 * b : 16 * (b + 1)] = stack(
                [
                    bits_of(
                        jnp.broadcast_to(any_two[2 * i + half][b : b + 1], (8, 128)), two_shift
                    )
                    for half in range(2)
                ]
            )
    plane, half, m = [jnp.bitwise_and(lax.shift_right_logical(lane, n), 1) for n in (4, 3, 2)]
    for side in range(2):
        word = [any_two[4 * side + n] for n in range(4)]
        word = jnp.where(
            plane == 0, jnp.where(half == 0, word[0], word[1]), jnp.where(half == 0, word[2], word[3])
        )
        edge_bits[side] = bits_of(word, 16 * m + 2 * jnp.bitwise_and(lane, 3))
    any_three = []
    for i in range(2):
        for j in range(2):
            word = either(any_two[4 * i + j], any_two[4 * i + 2 + j])
            word = either(word, lax.shift_right_logical(word, 16))
            any_three.append(either(word, lax.shift_right_logical(word, 2)))
    for i in range(2):
        for b in range(0, count, 2):
            tile = [
                jnp.broadcast_to(any_three[2 * i + j][n : n + 1], (8, 128))
                for n in (b, b + 1)
                for j in range(2)
            ]
            tile = jnp.where(
                row < 4, jnp.where(row < 2, tile[0], tile[1]), jnp.where(row < 6, tile[2], tile[3])
            )
            mask = bits_of(tile, 4 * jnp.bitwise_and(row, 1))
            at = 4 * (count * i + b)
            mask_three[at : at + 8] = beside([mask, mask])


def edge_planes(features, bits, low_wanted):
    last = features.shape[2] - 128
    planes = []
    for q in range(features.shape[0] // 2):
        low, high = [
            [
                features[b, :, column * last : column * last + 128]
                * bits[3 * column, b : b + 1].astype(BF16)
                for b in (2 * q, 2 * q + 1)
            ]
            for column in range(2)
        ]
        lows = beside([low[0][:, :64], low[1][:, :64]])
        highs = beside([high[0][:, 64:], high[1][:, 64:]])
        planes.append(jnp.where(low_wanted, lows, highs))
    return planes


def far_edge_kernel(features, bits, neighbours, edge_bits, blank, edge, notes):
    count = features.shape[0]
    odd = on_odd_place()
    for q, plane in enumerate(edge_planes(features, bits, jnp.logical_not(odd))):
        edge[64 * q : 64 * (q + 1), :] = plane
    notes[...] = blank[...]
    notes[:count, : neighbours.shape[1]] = jnp.where(
        neighbours[...] < 0, 4 * count, slot_numbers(neighbours)
    ).astype(F32)
    notes[count:, :] = edge_bits[jnp.where(odd, 1, 0)]
    edge[32 * count :, :] = notes[...].astype(BF16)


def near_edge_kernel(features, bits, earlier, edge):
    for q, plane in enumerate(edge_planes(features, bits, on_odd_place())):
        edge[q] = plane


def near_face_kernel(planes, earlier, face):
    rows = face.shape[0]
    begin = pl.multiple_of(jnp.where(on_odd_place(), 0, rows), rows)
    face[...] = planes[pl.ds(begin, rows), :]


def slot_rows(slot):
    return stack(
        [jnp.broadcast_to(slot[b : b + 1], (128, slot.shape[1])) for b in range(slot.shape[0])]
    ).astype(BF16)


def own_slot_rows(neighbours):
    slot = jnp.where(neighbours[...] < 0, 4 * neighbours.shape[0], slot_numbers(neighbours))
    return slot_rows(slot.astype(F32))


def times_transposed(x, y):
    return lax.dot_general(x, y, (((1,), (1,)), ((), ())), preferred_element_type=F32)


def fill_level_two_tables(tables, rows, count):
    lane = iota((16, 16 * count), 1)
    row = iota((16, 16 * count), 0)
    j, k = lax.shift_right_logical(row, 2), jnp.bitwise_and(row, 3)
    for q in range(9):
        source = 4 * jnp.bitwise_and(j + q // 3 + 3, 3) + jnp.bitwise_and(k + q % 3 + 3, 3)
        wanted = (lane - source).astype(F32)
        for a, table in enumerate(tables):
            at = 16 * (9 * a + q)
            for b in range(count):
                table[16 * (count * q + b) : 16 * (count * q + b + 1), :] = jnp.where(
                    rows[at : at + 16, 128 * b : 128 * b + 16 * count] == wanted, 1.0, 0.0
                ).astype(BF16)


def level_two_tables_kernel(neighbours, pick, later, own_two, sides_two):
    rows = times_transposed(pick[...], own_slot_rows(neighbours))
    fill_level_two_tables(
        (sides_two.at[0], own_two, sides_two.at[1]), rows, neighbours.shape[0]
    )


def far_tables_kernel(message, pick, later, gather, mask_two, mask_three):
    count = gather.shape[1] // 32
    notes = message[32 * count :, :].astype(F32)
    slots = slot_rows(notes[:count, : pick.shape[1]])
    begin = pl.multiple_of(jnp.where(on_odd_place(), 0, 288), 16)
    rows = stack(
        [
            times_transposed(pick[pl.ds(begin, 144), :], slots),
            times_transposed(pick[144:288, :], slots),
        ]
    )
    width = 16 * count
    fill_level_two_tables((gather.at[:, width:], gather.at[:, :width]), rows, count)

    every = jnp.ones((128, 256), BF16)
    lane = iota((16, 128), 1)
    row = iota((16, 128), 0)
    bits = [notes[count + b : count + b + 1] for b in range(count)]
    chosen = stack(
        [
            jnp.where(lane == 16 * plane + row, jnp.broadcast_to(bits[b], (16, 128)), 0.0)
            for plane in range(2)
            for b in range(count)
        ]
    ).astype(BF16)
    mask_two[...] = dot(chosen, every[:, :128])
    lane, row = lane[:8], row[:8]
    child = jnp.bitwise_and(lax.shift_right_logical(lane, 2), 2) + jnp.bitwise_and(
        lax.shift_right_logical(lane, 1), 1
    )
    wanted = (child == jnp.bitwise_and(row, 3)) & (lane < 32)
    chosen = stack(
        [
            jnp.where(wanted, jnp.where(row < 4, bits[b], bits[b + 1]), 0.0)
            for b in range(0, count, 2)
        ]
    ).astype(BF16)
    mask_three[...] = jnp.where(dot(chosen, every) > 0.5, 1.0, 0.0)


def level_three_tables_kernel(neighbours, pick, later, own_three, near_three):
    count = neighbours.shape[0]
    odd = on_odd_place()
    rows = times_transposed(pick[...], own_slot_rows(neighbours))
    row = iota((8, 128), 0)
    lane = iota((8, 128), 1)
    j, k = [jnp.bitwise_and(lax.shift_right_logical(row, n), 1) for n in (1, 0)]

    def block(tap, i, begin):
        c, e = tap // 3 % 3, tap % 3
        source = 2 * jnp.bitwise_and(j + c + 1, 1) + jnp.bitwise_and(k + e + 1, 1)
        wanted = (lane - source - begin).astype(F32)
        at = 8 * (2 * tap + i)
        tiles = []
        for b in range(0, count, 2):
            first, second = [rows[at : at + 8, 128 * n : 128 * (n + 1)] for n in (b, b + 1)]
            hit = jnp.where(row < 4, first, second) == wanted
            tiles.append(jnp.where(hit, 1.0, 0.0))
        return stack(tiles)

    nowhere = 16 * 4 * count
    for tap in range(27):
        for i in range(2):
            x = i + tap // 9 - 1
            if x < 0:
                begin = jnp.where(odd, nowhere, 8 * count)
            elif x > 1:
                begin = jnp.where(odd, 8 * count, nowhere)
            else:
                begin = 4 * count * x
            at = 8 * count * tap + 4 * count * i
            own_three[at : at + 4 * count, :] = block(tap, i, begin)[:, : 12 * count].astype(BF16)
    for q in range(9):
        tile = jnp.where(odd, block(q, 0, 0), block(18 + q, 1, 0))
        near_three[4 * count * q : 4 * count * (q + 1), :] = tile[:, : 4 * count].astype(BF16)


def shifted_windows(source, row):
    shifted = []
    for j in range(-1, 9):
        c, at = (0, 7) if j < 0 else (2, 0) if j > 7 else (1, j)
        left, mid, right = [source(3 * c + e, at) for e in range(3)]
        shifted.append(
            (
                pltpu.roll(jnp.where(row == 7, left, mid), 1, 0),
                mid,
                pltpu.roll(jnp.where(row == 0, right, mid), 7, 0),
            )
        )
    return [
        [stack([shifted[jr][e], shifted[jr + 4][e]]).astype(BF16) for e in range(3)]
        for jr in range(6)
    ]


def outer_kernel(
    neighbours, bits, features, kernel, reduce,
    middle, taps, face_taps, reduce_taps, partial,
    tables, windows, wrap_taps,
):
    count = features.shape[0]
    row = iota((8, 128), 0)
    numbers = slot_numbers(neighbours)

    none = jnp.zeros((64, 64), BF16)
    for q in range(9):
        w = [kernel[9 * a + q] for a in range(3)]
        rows = slice(q * 128, (q + 1) * 128)
        taps[rows, :] = stack(
            [beside([w[2], w[1], w[0], none]), beside([none, w[2], w[1], w[0]])]
        )
        wrap_taps[rows, :] = stack(
            [beside([w[2], w[1], none, none]), beside([none, none, w[1], w[0]])]
        )
        face_taps[rows, :] = stack([beside([w[0], none]), beside([none, w[2]])])

    reduce_taps[...] = stack(
        [
            beside([reduce[4 * ci + 2 * cj], reduce[4 * ci + 2 * cj + 1]])
            for cj in range(2)
            for ci in range(2)
        ]
    )

    for pair in range(4):
        tables[pair, count] = jnp.zeros((64, 128), F32)
    for b in range(count):
        cols = [
            features[b, :, 128 * q : 128 * (q + 1)] * bits[q, b : b + 1].astype(BF16)
            for q in range(4)
        ]
        for p in (0, 2):
            m = stack(
                [
                    beside([cols[p][:, 64:], cols[p + 1][:, 64:]]),
                    beside([cols[p + 1][:, :64], cols[(p + 2) % 4][:, :64]]),
                ]
            ).T
            tables[p, b] = m[:64].astype(F32)
            tables[p + 1, b] = m[64:].astype(F32)

    for b in range(count):
        slot = [numbers[b, 9 + q] for q in range(9)]
        for pair in range(4):
            tiles = shifted_windows(lambda q, j: tables[pair, slot[q], pl.ds(8 * j, 8), :], row)
            for jr in range(6):
                for e in range(3):
                    if pair == 1:
                        middle[b, e, jr] = tiles[jr][e]
                    else:
                        windows[b, e, pair, jr] = tiles[jr][e]

    group = count // 2
    for g in range(2):
        bricks = slice(g * group, (g + 1) * group)
        rows = slice(g * group * 64, (g + 1) * group * 64)
        low, high, wrap = [
            dot(
                beside(
                    [
                        windows[bricks, e, pair, c : c + 4].reshape(group * 64, 128)
                        for c in range(3)
                        for e in range(3)
                    ]
                ),
                weights[...],
            )
            for pair, weights in ((0, taps), (2, taps), (3, wrap_taps))
        ]
        partial[0, rows] = low[:, :128] + wrap[:, 128:]
        partial[1, rows] = low[:, 128:]
        partial[2, rows] = high[:, :128]
        partial[3, rows] = high[:, 128:] + wrap[:, :128]


def masked_tiles(sums, pair_words, b, i):
    row = iota((8, 128), 0)
    tiles = {}
    for half in range(2):
        words = jnp.broadcast_to(pair_words[2 * i + half, b : b + 1, :], (8, 128))
        for jr in range(4):
            at = jr * 16 + half * 8
            tiles[4 * half + jr] = jnp.maximum(sums[at : at + 8], 0.0) * bits_of(
                words, row + 8 * jr
            )
    return [tiles[j] for j in range(8)]


def reduce_planes(groups, weights, low_sums, high_sums):
    left = stack(
        [beside([tiles[j], tiles[j + 1]]) for tiles in groups for j in (0, 2, 4, 6)]
    ).astype(BF16)
    sums = dot(left, weights[...])
    low_sums[: sums.shape[0], :] = sums[:, :128]
    high_sums[: sums.shape[0], :] = sums[:, 128:]
    return [
        low_sums[pl.ds(32 * g, 16, stride=2), :] + high_sums[pl.ds(32 * g + 1, 16, stride=2), :]
        for g in range(len(groups))
    ]


def faces_one_kernel(
    neighbours, from_a, from_b, face_taps, partial, reduce, pair_words, mask_two, inner,
    outer, second, to_b,
    halo, windows, low_sums, high_sums,
):
    count = outer.shape[0]
    lane = iota((64, 128), 1)
    small = iota((8, 128), 1)
    row = iota((8, 128), 0)
    odd = on_odd_place()
    slot = slot_numbers(neighbours)
    halo[count] = jnp.zeros((64, 128), F32)
    for q in range(count // 2):
        one, two = from_a[q], from_b[64 * q : 64 * (q + 1), :]
        m = stack([jnp.where(odd, one, two), jnp.where(odd, two, one)]).T
        halo[2 * q] = m[:64].astype(F32)
        halo[2 * q + 1] = m[64:].astype(F32)
    for b in range(count):
        low = [slot[b, q] for q in range(9)]
        high = [slot[b, 18 + q] for q in range(9)]

        def source(q, j):
            rows = pl.ds(8 * j, 8)
            return jnp.where(small < 64, halo[low[q], rows, :], halo[high[q], rows, :])

        tiles = shifted_windows(source, row)
        for jr in range(6):
            for e in range(3):
                windows[b, e, jr] = tiles[jr][e]
    added = dot(
        beside(
            [
                windows[:, e, c : c + 4].reshape(count * 64, 128)
                for c in range(3)
                for e in range(3)
            ]
        ),
        face_taps[...],
    )
    groups = []
    for b in range(count):
        at = slice(64 * b, 64 * (b + 1))
        for side in range(2):
            near = (lane < 64) == (side == 0)
            sums = partial[3 * side, at] + jnp.where(near, added[at], 0.0)
            groups.append(masked_tiles(sums, pair_words, b, 3 * side))
            outer[b, side] = stack(groups[-1]).astype(BF16)
    sums = reduce_planes(groups, reduce, low_sums, high_sums)
    for b in range(count):
        at = slice(16 * b, 16 * (b + 1))
        planes = [
            (jnp.maximum(sums[2 * b + side], 0.0) * mask_two[3 * side, at]).astype(BF16)
            for side in range(2)
        ]
        second[16 * b : 16 * (b + 1)] = planes[0]
        second[16 * (count + b) : 16 * (count + b + 1)] = planes[1]
        to_b[at] = jnp.where(odd, planes[1], planes[0])
    rows = 16 * count
    to_b[rows : 2 * rows] = jnp.where(odd, inner[1], inner[0])
    to_b[2 * rows :] = jnp.where(odd, inner[0], inner[1])


def inner_kernel(
    middle, taps, partial, reduce, pair_words, mask_two,
    inner, second,
    low_sums, high_sums,
):
    count = middle.shape[0]
    added = dot(
        beside(
            [
                middle[:, e, c : c + 4].reshape(count * 64, 128)
                for c in range(3)
                for e in range(3)
            ]
        ),
        taps[...],
    )
    groups = []
    for b in range(count):
        at = slice(64 * b, 64 * (b + 1))
        for i in (1, 2):
            sums = partial[i, at] + added[at, 128 * (i - 1) : 128 * i]
            groups.append(masked_tiles(sums, pair_words, b, i))
            inner[b, i - 1] = stack(groups[-1]).astype(BF16)
    sums = reduce_planes(groups, reduce, low_sums, high_sums)
    for b in range(count):
        at = slice(16 * b, 16 * (b + 1))
        for i in (1, 2):
            second[i - 1, at] = (
                jnp.maximum(sums[2 * b + i - 1], 0.0) * mask_two[i, at]
            ).astype(BF16)


def output_kernel(outer, inner, out):
    for b in range(outer.shape[0]):
        ordered = [outer[b, 0], inner[b, 0], inner[b, 1], outer[b, 1]]
        for i in (0, 2):
            m = stack(ordered[i : i + 2]).T
            top, bottom = m[:64], m[64:]
            out[b, :, 128 * i : 128 * (i + 1)] = beside([top[:, :64], bottom[:, :64]])
            out[b, :, 128 * (i + 1) : 128 * (i + 2)] = beside([top[:, 64:], bottom[:, 64:]])


def face_part(gather, face, kernel, high):
    moved = dot(gather, face).astype(BF16)
    rows = moved.shape[0] // 9
    left = beside([moved[q * rows : (q + 1) * rows] for q in range(9)])
    weights = kernel[pl.ds(18 * high, 9)]
    return dot(left, weights.reshape(9 * weights.shape[1], weights.shape[2]))


def own_two_kernel(
    outer, inner, own_gather, gathers, from_a, kernel, first,
    partial, result, stored,
):
    copy = pltpu.make_async_copy(first, result, stored)
    copy.start()
    rows = inner.shape[1]
    planes = beside([outer[:rows], inner[0], inner[1], outer[rows:]])
    moved = dot(own_gather[...], planes).astype(BF16)
    left = beside(
        [
            stack(
                [
                    moved[q * rows : (q + 1) * rows, 128 * i : 128 * (i + 1)]
                    for i in range(4)
                ]
            )
            for q in range(9)
        ]
    )
    weights = [kernel[9 * a : 9 * (a + 1)].reshape(9 * 128, 128) for a in range(3)]
    sums = dot(left, beside(weights[:2]))
    later = dot(left[rows:], weights[2])
    high = jnp.where(on_odd_place(), 0, 1)
    near = face_part(gathers[high], from_a[...], kernel, high)
    for i in range(4):
        total = sums[i * rows : (i + 1) * rows, 128:]
        if i:
            total = total + sums[(i - 1) * rows : i * rows, :128]
        if i < 3:
            total = total + later[i * rows : (i + 1) * rows]
        if i in (0, 3):
            total = total + jnp.where(high == i // 3, near, 0.0)
        partial[i * rows : (i + 1) * rows] = total
    copy.wait()


def child_columns(picked, pairs, planes):
    return beside(
        [
            stack(
                [
                    picked[8 * (planes * q + i) : 8 * (planes * q + i + 1), 128 * n : 128 * (n + 1)]
                    for i in range(planes)
                    for n in range(pairs)
                ]
            )
            for q in range(8)
        ]
    )


def faces_two_kernel(
    gathers, far_gather, children, far_children, partial, to_b, from_b, kernel, reduce,
    mask_two, mask_three, far_mask_two, far_mask_three,
    second, third, far_third,
):
    count = second.shape[0]
    rows = 16 * count
    odd = on_odd_place()
    high = jnp.where(odd, 1, 0)
    none = jnp.zeros((rows, 128), BF16)
    sent = [from_b[d * rows : (d + 1) * rows] for d in range(3)]
    moved = dot(
        far_gather[...],
        stack([beside(sent + [none]), beside([none, none, none, to_b[:rows]])]),
    ).astype(BF16)
    left = [
        beside([moved[q * rows : (q + 1) * rows, 128 * d : 128 * (d + 1)] for q in range(9)])
        for d in range(4)
    ]
    moved = dot(gathers[high], sent[0]).astype(BF16)
    left.append(beside([moved[q * rows : (q + 1) * rows] for q in range(9)]))
    toward, same, away = [
        kernel[pl.ds(begin, 9)].reshape(9 * 128, 128) for begin in (18 - 18 * high, 9, 18 * high)
    ]
    zero = dot(stack([left[0], left[3]]), beside([same, toward]))
    one = dot(left[1], beside([away, same]))
    near = zero[rows:, 128:] + zero[:rows, :128] + one[:, :128]
    two = dot(stack([left[2], left[4]]), away)
    past = zero[:rows, 128:] + one[:, 128:] + two[:rows]
    far = two[rows:]
    planes = []
    for i in range(4):
        sums = partial[i * rows : (i + 1) * rows]
        if i in (0, 3):
            sums = sums + jnp.where(high == i // 3, far, 0.0)
        planes.append((jnp.maximum(sums, 0.0) * mask_two[i]).astype(BF16))
    bricks = [
        stack([planes[i][16 * b : 16 * (b + 1)] for i in range(4)]) for b in range(count)
    ]
    for b in range(count):
        second[b] = bricks[b]
    picked = dot(
        children[...], beside([stack(bricks[b : b + 2]) for b in range(0, count, 2)])
    )

    far_planes = [
        (jnp.maximum(sums, 0.0) * far_mask_two[n * rows : (n + 1) * rows]).astype(BF16)
        for n, sums in enumerate((jnp.where(odd, near, past), jnp.where(odd, past, near)))
    ]
    far_picked = dot(
        far_children[...],
        beside(
            [
                stack(
                    [
                        plane[16 * b : 16 * (b + 1)]
                        for b in (n, n + 1)
                        for plane in far_planes
                    ]
                )
                for n in range(0, count, 2)
            ]
        ),
    )
    left = stack(
        [child_columns(picked, count // 2, 2), child_columns(far_picked, count // 2, 1)]
    ).astype(BF16)
    sums = jnp.maximum(dot(left, reduce[...].reshape(8 * 128, 256)), 0.0)
    third[...] = (sums[: 8 * count] * mask_three[...]).astype(BF16)
    far_third[...] = (sums[8 * count :] * far_mask_three[...]).astype(BF16)


def own_three_kernel(gather, third, far, kernel, second, partial, result, stored):
    copy = pltpu.make_async_copy(second, result, stored)
    copy.start()
    rows = third.shape[0]
    moved = dot(gather[...], stack([third[...], far[...]])).astype(BF16)
    left = beside([moved[q * rows : (q + 1) * rows] for q in range(27)])
    partial[...] = dot(left, kernel[...].reshape(27 * 256, 256))
    copy.wait()


def faces_three_kernel(gather, partial, from_a, kernel, mask_three, out):
    rows = from_a.shape[0]
    odd = on_odd_place()
    near = face_part(gather[...], from_a[...], kernel, jnp.where(odd, 0, 1))
    low = partial[:rows] + jnp.where(odd, near, 0.0)
    high = partial[rows:] + jnp.where(odd, 0.0, near)
    low = jnp.maximum(low, 0.0) * mask_three[:rows]
    high = jnp.maximum(high, 0.0) * mask_three[rows:]
    row = iota((8, 256), 0)
    for n in range(rows // 8):
        near, past = low[8 * n : 8 * (n + 1)], high[8 * n : 8 * (n + 1)]
        out[2 * n] = jnp.where(row < 4, near, pltpu.roll(past, 4, 0)).astype(BF16)
        out[2 * n + 1] = jnp.where(row < 4, pltpu.roll(near, 4, 0), past).astype(BF16)


def level_two_picks():
    pick = np.zeros((432, 27), np.float32)
    for tap in range(27):
        for r in range(16):
            y, z = r // 4 + tap // 3 % 3 - 1, r % 4 + tap % 3 - 1
            pick[16 * tap + r, tap // 9 * 9 + 3 * (y // 4 + 1) + z // 4 + 1] = 16
    return jnp.asarray(pick, BF16)


def level_three_picks():
    pick = np.zeros((27 * 16, 27), np.float32)
    for tap in range(27):
        for r in range(16):
            x, y, z = [
                n + d - 1
                for n, d in (
                    (r // 8, tap // 9), (r // 2 % 2, tap // 3 % 3), (r % 2, tap % 3)
                )
            ]
            pick[16 * tap + r, 9 * (x // 2 + 1) + 3 * (y // 2 + 1) + z // 2 + 1] = 4
    return jnp.asarray(pick, BF16)


def child_rows(planes):
    pick = np.zeros((8 * planes * 8, 2 * 2 * planes * 16), np.float32)
    for q in range(8):
        for r in range(8 * planes):
            x, y, z = [
                2 * n + (q >> s & 1) for n, s in ((r // 8, 2), (r // 2 % 2, 1), (r % 2, 0))
            ]
            at = 2 * planes * 16 * (r // 4 % 2) + 16 * x + 4 * y + z
            pick[8 * planes * q + r, at] = 1
    return jnp.asarray(pick, BF16)


ANY = pl.BlockSpec(memory_space=pl.ANY)
VMEM = pl.BlockSpec(memory_space=pltpu.VMEM)
DMA = pltpu.SemaphoreType.DMA


def call(kernel, cost, out_shape, scratch, *args, remain=(), store=()):
    single = not isinstance(out_shape, tuple)
    outs = (out_shape,) if single else out_shape
    specs = tuple(ANY if n in store else VMEM for n in range(len(outs)))
    return pl.pallas_call(
        kernel,
        out_shape=out_shape,
        in_specs=[ANY if n in remain else VMEM for n in range(len(args))],
        out_specs=specs[0] if single else specs,
        scratch_shapes=scratch,
        compiler_params=pltpu.CompilerParams(vmem_limit_bytes=24 * 1024 * 1024),
        cost_estimate=pl.CostEstimate(
            flops=int(cost * 10**10), bytes_accessed=10**7, transcendentals=0
        ),
    )(*args)


def swaps(tiles, count):
    within, across = [], []
    for t in range(tiles):
        for m in range(count):
            if m ^ 1 < count:
                within.append((t * count + m, t * count + (m ^ 1)))
            other = ((m - 1) ^ 1) + 1 if m else -1
            if 0 <= other < count:
                across.append((t * count + m, t * count + other))
            elif t ^ 1 < tiles:
                across.append((t * count + m, (t ^ 1) * count + m))
    return within, across


def on_device(
    features,
    neighbours,
    occupancy,
    conv_one,
    first_reduce_kernel,
    conv_two,
    second_reduce_kernel,
    conv_three,
):
    axes = ("tiles", LINE)
    within, across = swaps(lax.axis_size("tiles"), lax.axis_size(LINE))
    count = features.shape[0]
    features = jnp.swapaxes(features, 1, 2)
    shape = jax.ShapeDtypeStruct

    def exchange(to_a, to_b):
        from_b = lax.ppermute(to_b, axes, across)
        return lax.ppermute(to_a, axes, within), from_b

    blank = call(blank_kernel, 1.0, shape((2 * count, 128), F32), [])
    bits, edge_bits, pair_words, mask_two, mask_three = call(
        masks_kernel,
        0.01,
        (
            shape((4, count, 128), F32),
            shape((2, count, 128), F32),
            shape((8, count, 128), jnp.int32),
            shape((4, 16 * count, 128), F32),
            shape((8 * count, 256), F32),
        ),
        [],
        occupancy, blank,
    )
    to_b = call(
        far_edge_kernel,
        0.02,
        shape((32 * count + 2 * count, 128), BF16),
        [pltpu.VMEM((2 * count, 128), F32)],
        features, bits, neighbours, edge_bits, blank,
    )
    face = shape((count // 2, 64, 128), BF16)
    to_a = call(near_edge_kernel, 0.02, face, [], features, bits, to_b)
    from_a, message = exchange(to_a, to_b)
    middle, taps, face_taps, reduce_taps, partial = call(
        outer_kernel,
        2.0,
        (
            shape((count, 3, 6, 16, 128), BF16),
            shape((9 * 128, 256), BF16),
            shape((9 * 128, 128), BF16),
            shape((256, 256), BF16),
            shape((4, count * 64, 128), F32),
        ),
        [
            pltpu.VMEM((4, count + 1, 64, 128), F32),
            pltpu.VMEM((count, 3, 4, 6, 16, 128), BF16),
            pltpu.VMEM((9 * 128, 256), BF16),
        ],
        neighbours, bits, features, conv_one, first_reduce_kernel,
    )
    plane = shape((16 * count, 128), BF16)
    rows = shape((count, 2, 64, 128), BF16)
    sums = pltpu.VMEM((count * 64 + 8, 128), F32)
    inner, inner_two = call(
        inner_kernel,
        0.05,
        (rows, shape((2, 16 * count, 128), BF16)),
        [sums, sums],
        middle, taps, partial, reduce_taps, pair_words, mask_two,
    )
    outer, outer_two, to_b = call(
        faces_one_kernel,
        1.5,
        (rows, shape((2 * 16 * count, 128), BF16), shape((3 * 16 * count, 128), BF16)),
        [
            pltpu.VMEM((count + 1, 64, 128), F32),
            pltpu.VMEM((count, 3, 6, 16, 128), BF16),
            sums,
            sums,
        ],
        neighbours, from_a, message, face_taps, partial, reduce_taps, pair_words, mask_two,
        inner_two,
    )
    to_a = call(near_face_kernel, 0.02, plane, [], outer_two, to_b)
    from_a, from_b = exchange(to_a, to_b)

    pick = level_two_picks()
    table = shape((9 * 16 * count, 16 * count), BF16)
    own_two, sides_two = call(
        level_two_tables_kernel,
        0.05,
        (table, shape((2, 9 * 16 * count, 16 * count), BF16)),
        [],
        neighbours, pick, to_a,
    )
    far_two, far_mask_two, far_mask_three = call(
        far_tables_kernel,
        0.05,
        (
            shape((9 * 16 * count, 32 * count), BF16),
            shape((2 * 16 * count, 128), F32),
            shape((4 * count, 256), F32),
        ),
        [],
        message, pick, to_a,
    )
    first_level = call(output_kernel, 0.05, shape(features.shape, BF16), [], outer, inner)
    partial, first_level = call(
        own_two_kernel,
        1.0,
        (shape((4 * 16 * count, 128), F32), shape(features.shape, BF16)),
        [DMA(())],
        outer_two, inner_two, own_two, sides_two, from_a, conv_two, first_level,
        store=(1,),
    )
    own_three, near_three = call(
        level_three_tables_kernel,
        0.05,
        (shape((27 * 8 * count, 12 * count), BF16), shape((9 * 4 * count, 4 * count), BF16)),
        [],
        neighbours, level_three_picks(), to_a,
    )
    face = shape((4 * count, 256), BF16)
    second_level, third, far_third = call(
        faces_two_kernel,
        0.05,
        (shape((count, 64, 128), BF16), shape((8 * count, 256), BF16), face),
        [],
        sides_two, far_two, child_rows(2), child_rows(1), partial, to_b, from_b, conv_two,
        second_reduce_kernel, mask_two, mask_three, far_mask_two, far_mask_three,
    )
    to_a = call(near_face_kernel, 0.02, face, [], third, far_third)
    from_a = lax.ppermute(to_a, axes, within)
    partial, second_level = call(
        own_three_kernel,
        1.0,
        (shape((8 * count, 256), F32), shape(second_level.shape, BF16)),
        [DMA(())],
        own_three, third, far_third, conv_three, second_level,
        store=(1,),
    )
    third_level = call(
        faces_three_kernel,
        1,
        shape((count, 8, 256), BF16),
        [],
        near_three, partial, from_a, conv_three, mask_three,
    )
    return jnp.swapaxes(first_level, 1, 2), second_level, third_level


def solution(mesh):
    split = P(("tiles", LINE))
    return jax.shard_map(
        on_device,
        mesh=mesh,
        in_specs=(split, split, split, P(), P(), P(), P(), P()),
        out_specs=(split, split, split),
        check_vma=False,
    )
```

```python
import jax
import jax.numpy as jnp
import numpy as np
from jax import lax
from jax.experimental import pallas as pl
from jax.experimental.pallas import tpu as pltpu
from jax.sharding import PartitionSpec as P

F32 = jnp.float32
BF16 = jnp.bfloat16
LINE = "morton"


def dot(x, y):
    return jnp.dot(x, y, preferred_element_type=F32)


def iota(shape, axis):
    return lax.broadcasted_iota(jnp.int32, shape, axis)


def stack(parts):
    return jnp.concatenate(parts, axis=0)


def beside(parts):
    return jnp.concatenate(parts, axis=1)


def bits_of(words, shift):
    return jnp.bitwise_and(lax.shift_right_logical(words, shift), 1).astype(F32)


def either(x, y):
    return jnp.bitwise_or(x, y)


def on_odd_place():
    return lax.rem(lax.axis_index(LINE), 2) == 1


def word_lanes(words, w):
    return jnp.broadcast_to(words[:, w : w + 1], (words.shape[0], 128))


def column_bits(words, column):
    lane = iota((words.shape[0], 128), 1)
    w = [word_lanes(words, 4 * column + q) for q in range(4)]
    chosen = jnp.where(
        lane < 64, jnp.where(lane < 32, w[0], w[1]), jnp.where(lane < 96, w[2], w[3])
    )
    return bits_of(chosen, jnp.bitwise_and(lane, 31))


def slot_numbers(neighbours):
    count = neighbours.shape[0]
    number = neighbours[...]
    tap = iota(number.shape, 1)
    shift = jnp.where(tap < 9, count, jnp.where(tap < 18, 0, -count))
    return jnp.where(number < 0, count, number + shift - lax.axis_index(LINE) * count)


def blank_kernel(notes):
    notes[...] = jnp.zeros(notes.shape, F32)


def masks_kernel(occupancy, blank, bits, edge_bits, pair_words, mask_two, mask_three):
    count = occupancy.shape[0]
    for q in range(4):
        bits[q] = column_bits(occupancy[...], q)
    words = [word_lanes(occupancy[...], w) for w in range(16)]
    lane = iota((count, 128), 1)
    row = iota((8, 128), 0)
    any_two = []
    for i in range(4):
        for half in range(2):
            low, high = words[4 * i + half], words[4 * i + 2 + half]
            pair_words[2 * i + half] = jnp.where(lane < 64, low, high)
            word = either(low, high)
            word = either(word, lax.shift_right_logical(word, 1))
            any_two.append(either(word, lax.shift_right_logical(word, 8)))
    two_shift = 16 * lax.shift_right_logical(row, 2) + 2 * jnp.bitwise_and(row, 3)
    for i in range(4):
        for b in range(count):
            mask_two[i, 16 * b : 16 * (b + 1)] = stack(
                [
                    bits_of(
                        jnp.broadcast_to(any_two[2 * i + half][b : b + 1], (8, 128)), two_shift
                    )
                    for half in range(2)
                ]
            )
    plane, half, m = [jnp.bitwise_and(lax.shift_right_logical(lane, n), 1) for n in (4, 3, 2)]
    for side in range(2):
        word = [any_two[4 * side + n] for n in range(4)]
        word = jnp.where(
            plane == 0, jnp.where(half == 0, word[0], word[1]), jnp.where(half == 0, word[2], word[3])
        )
        edge_bits[side] = bits_of(word, 16 * m + 2 * jnp.bitwise_and(lane, 3))
    any_three = []
    for i in range(2):
        for j in range(2):
            word = either(any_two[4 * i + j], any_two[4 * i + 2 + j])
            word = either(word, lax.shift_right_logical(word, 16))
            any_three.append(either(word, lax.shift_right_logical(word, 2)))
    for i in range(2):
        for b in range(0, count, 2):
            tile = [
                jnp.broadcast_to(any_three[2 * i + j][n : n + 1], (8, 128))
                for n in (b, b + 1)
                for j in range(2)
            ]
            tile = jnp.where(
                row < 4, jnp.where(row < 2, tile[0], tile[1]), jnp.where(row < 6, tile[2], tile[3])
            )
            mask = bits_of(tile, 4 * jnp.bitwise_and(row, 1))
            at = 4 * (count * i + b)
            mask_three[at : at + 8] = beside([mask, mask])


def edge_planes(features, bits, low_wanted):
    last = features.shape[2] - 128
    planes = []
    for q in range(features.shape[0] // 2):
        low, high = [
            [
                features[b, :, column * last : column * last + 128]
                * bits[3 * column, b : b + 1].astype(BF16)
                for b in (2 * q, 2 * q + 1)
            ]
            for column in range(2)
        ]
        lows = beside([low[0][:, :64], low[1][:, :64]])
        highs = beside([high[0][:, 64:], high[1][:, 64:]])
        planes.append(jnp.where(low_wanted, lows, highs))
    return planes


def far_edge_kernel(features, bits, neighbours, edge_bits, blank, edge, notes):
    count = features.shape[0]
    odd = on_odd_place()
    for q, plane in enumerate(edge_planes(features, bits, jnp.logical_not(odd))):
        edge[64 * q : 64 * (q + 1), :] = plane
    notes[...] = blank[...]
    notes[:count, : neighbours.shape[1]] = jnp.where(
        neighbours[...] < 0, 4 * count, slot_numbers(neighbours)
    ).astype(F32)
    notes[count:, :] = edge_bits[jnp.where(odd, 1, 0)]
    edge[32 * count :, :] = notes[...].astype(BF16)


def near_edge_kernel(features, bits, earlier, edge):
    for q, plane in enumerate(edge_planes(features, bits, on_odd_place())):
        edge[q] = plane


def near_face_kernel(planes, earlier, face):
    rows = face.shape[0]
    begin = pl.multiple_of(jnp.where(on_odd_place(), 0, rows), rows)
    face[...] = planes[pl.ds(begin, rows), :]


def slot_rows(slot):
    return stack(
        [jnp.broadcast_to(slot[b : b + 1], (128, slot.shape[1])) for b in range(slot.shape[0])]
    ).astype(BF16)


def own_slot_rows(neighbours):
    slot = jnp.where(neighbours[...] < 0, 4 * neighbours.shape[0], slot_numbers(neighbours))
    return slot_rows(slot.astype(F32))


def times_transposed(x, y):
    return lax.dot_general(x, y, (((1,), (1,)), ((), ())), preferred_element_type=F32)


def fill_level_two_tables(tables, rows, count):
    lane = iota((16, 16 * count), 1)
    row = iota((16, 16 * count), 0)
    j, k = lax.shift_right_logical(row, 2), jnp.bitwise_and(row, 3)
    for q in range(9):
        source = 4 * jnp.bitwise_and(j + q // 3 + 3, 3) + jnp.bitwise_and(k + q % 3 + 3, 3)
        wanted = (lane - source).astype(F32)
        for a, table in enumerate(tables):
            at = 16 * (9 * a + q)
            for b in range(count):
                table[16 * (count * q + b) : 16 * (count * q + b + 1), :] = jnp.where(
                    rows[at : at + 16, 128 * b : 128 * b + 16 * count] == wanted, 1.0, 0.0
                ).astype(BF16)


def level_two_tables_kernel(neighbours, pick, later, own_two, sides_two):
    rows = times_transposed(pick[...], own_slot_rows(neighbours))
    fill_level_two_tables(
        (sides_two.at[0], own_two, sides_two.at[1]), rows, neighbours.shape[0]
    )


def far_tables_kernel(message, pick, later, gather, mask_two, mask_three):
    count = gather.shape[1] // 32
    notes = message[32 * count :, :].astype(F32)
    slots = slot_rows(notes[:count, : pick.shape[1]])
    begin = pl.multiple_of(jnp.where(on_odd_place(), 0, 288), 16)
    rows = stack(
        [
            times_transposed(pick[pl.ds(begin, 144), :], slots),
            times_transposed(pick[144:288, :], slots),
        ]
    )
    width = 16 * count
    fill_level_two_tables((gather.at[:, width:], gather.at[:, :width]), rows, count)

    every = jnp.ones((128, 256), BF16)
    lane = iota((16, 128), 1)
    row = iota((16, 128), 0)
    bits = [notes[count + b : count + b + 1] for b in range(count)]
    chosen = stack(
        [
            jnp.where(lane == 16 * plane + row, jnp.broadcast_to(bits[b], (16, 128)), 0.0)
            for plane in range(2)
            for b in range(count)
        ]
    ).astype(BF16)
    mask_two[...] = dot(chosen, every[:, :128])
    lane, row = lane[:8], row[:8]
    child = jnp.bitwise_and(lax.shift_right_logical(lane, 2), 2) + jnp.bitwise_and(
        lax.shift_right_logical(lane, 1), 1
    )
    wanted = (child == jnp.bitwise_and(row, 3)) & (lane < 32)
    chosen = stack(
        [
            jnp.where(wanted, jnp.where(row < 4, bits[b], bits[b + 1]), 0.0)
            for b in range(0, count, 2)
        ]
    ).astype(BF16)
    mask_three[...] = jnp.where(dot(chosen, every) > 0.5, 1.0, 0.0)


def level_three_tables_kernel(neighbours, pick, later, own_three, near_three):
    count = neighbours.shape[0]
    odd = on_odd_place()
    rows = times_transposed(pick[...], own_slot_rows(neighbours))
    row = iota((8, 128), 0)
    lane = iota((8, 128), 1)
    j, k = [jnp.bitwise_and(lax.shift_right_logical(row, n), 1) for n in (1, 0)]

    def block(tap, i, begin):
        c, e = tap // 3 % 3, tap % 3
        source = 2 * jnp.bitwise_and(j + c + 1, 1) + jnp.bitwise_and(k + e + 1, 1)
        wanted = (lane - source - begin).astype(F32)
        at = 8 * (2 * tap + i)
        tiles = []
        for b in range(0, count, 2):
            first, second = [rows[at : at + 8, 128 * n : 128 * (n + 1)] for n in (b, b + 1)]
            hit = jnp.where(row < 4, first, second) == wanted
            tiles.append(jnp.where(hit, 1.0, 0.0))
        return stack(tiles)

    nowhere = 16 * 4 * count
    for tap in range(27):
        for i in range(2):
            x = i + tap // 9 - 1
            if x < 0:
                begin = jnp.where(odd, nowhere, 8 * count)
            elif x > 1:
                begin = jnp.where(odd, 8 * count, nowhere)
            else:
                begin = 4 * count * x
            at = 8 * count * tap + 4 * count * i
            own_three[at : at + 4 * count, :] = block(tap, i, begin)[:, : 12 * count].astype(BF16)
    for q in range(9):
        tile = jnp.where(odd, block(q, 0, 0), block(18 + q, 1, 0))
        near_three[4 * count * q : 4 * count * (q + 1), :] = tile[:, : 4 * count].astype(BF16)


def shifted_windows(source, row):
    shifted = []
    for j in range(-1, 9):
        c, at = (0, 7) if j < 0 else (2, 0) if j > 7 else (1, j)
        left, mid, right = [source(3 * c + e, at) for e in range(3)]
        shifted.append(
            (
                pltpu.roll(jnp.where(row == 7, left, mid), 1, 0),
                mid,
                pltpu.roll(jnp.where(row == 0, right, mid), 7, 0),
            )
        )
    return [
        [stack([shifted[jr][e], shifted[jr + 4][e]]).astype(BF16) for e in range(3)]
        for jr in range(6)
    ]


def outer_kernel(
    neighbours, bits, features, kernel, reduce,
    middle, taps, face_taps, reduce_taps, partial,
    tables, windows, wrap_taps,
):
    count = features.shape[0]
    row = iota((8, 128), 0)
    numbers = slot_numbers(neighbours)

    none = jnp.zeros((64, 64), BF16)
    for q in range(9):
        w = [kernel[9 * a + q] for a in range(3)]
        rows = slice(q * 128, (q + 1) * 128)
        taps[rows, :] = stack(
            [beside([w[2], w[1], w[0], none]), beside([none, w[2], w[1], w[0]])]
        )
        wrap_taps[rows, :] = stack(
            [beside([w[2], w[1], none, none]), beside([none, none, w[1], w[0]])]
        )
        face_taps[rows, :] = stack([beside([w[0], none]), beside([none, w[2]])])

    reduce_taps[...] = stack(
        [
            beside([reduce[4 * ci + 2 * cj], reduce[4 * ci + 2 * cj + 1]])
            for cj in range(2)
            for ci in range(2)
        ]
    )

    for pair in range(4):
        tables[pair, count] = jnp.zeros((64, 128), F32)
    for b in range(count):
        cols = [
            features[b, :, 128 * q : 128 * (q + 1)] * bits[q, b : b + 1].astype(BF16)
            for q in range(4)
        ]
        for p in (0, 2):
            m = stack(
                [
                    beside([cols[p][:, 64:], cols[p + 1][:, 64:]]),
                    beside([cols[p + 1][:, :64], cols[(p + 2) % 4][:, :64]]),
                ]
            ).T
            tables[p, b] = m[:64].astype(F32)
            tables[p + 1, b] = m[64:].astype(F32)

    for b in range(count):
        slot = [numbers[b, 9 + q] for q in range(9)]
        for pair in range(4):
            tiles = shifted_windows(lambda q, j: tables[pair, slot[q], pl.ds(8 * j, 8), :], row)
            for jr in range(6):
                for e in range(3):
                    if pair == 1:
                        middle[b, e, jr] = tiles[jr][e]
                    else:
                        windows[b, e, pair, jr] = tiles[jr][e]

    group = count // 2
    for g in range(2):
        bricks = slice(g * group, (g + 1) * group)
        rows = slice(g * group * 64, (g + 1) * group * 64)
        low, high, wrap = [
            dot(
                beside(
                    [
                        windows[bricks, e, pair, c : c + 4].reshape(group * 64, 128)
                        for c in range(3)
                        for e in range(3)
                    ]
                ),
                weights[...],
            )
            for pair, weights in ((0, taps), (2, taps), (3, wrap_taps))
        ]
        partial[0, rows] = low[:, :128] + wrap[:, 128:]
        partial[1, rows] = low[:, 128:]
        partial[2, rows] = high[:, :128]
        partial[3, rows] = high[:, 128:] + wrap[:, :128]


def masked_tiles(sums, pair_words, b, i):
    row = iota((8, 128), 0)
    tiles = {}
    for half in range(2):
        words = jnp.broadcast_to(pair_words[2 * i + half, b : b + 1, :], (8, 128))
        for jr in range(4):
            at = jr * 16 + half * 8
            tiles[4 * half + jr] = jnp.maximum(sums[at : at + 8], 0.0) * bits_of(
                words, row + 8 * jr
            )
    return [tiles[j] for j in range(8)]


def reduce_planes(groups, weights, low_sums, high_sums):
    left = stack(
        [beside([tiles[j], tiles[j + 1]]) for tiles in groups for j in (0, 2, 4, 6)]
    ).astype(BF16)
    sums = dot(left, weights[...])
    low_sums[: sums.shape[0], :] = sums[:, :128]
    high_sums[: sums.shape[0], :] = sums[:, 128:]
    return [
        low_sums[pl.ds(32 * g, 16, stride=2), :] + high_sums[pl.ds(32 * g + 1, 16, stride=2), :]
        for g in range(len(groups))
    ]


def faces_one_kernel(
    neighbours, from_a, from_b, face_taps, partial, reduce, pair_words, mask_two, inner,
    outer, second, to_b,
    halo, windows, low_sums, high_sums,
):
    count = outer.shape[0]
    lane = iota((64, 128), 1)
    small = iota((8, 128), 1)
    row = iota((8, 128), 0)
    odd = on_odd_place()
    slot = slot_numbers(neighbours)
    halo[count] = jnp.zeros((64, 128), F32)
    for q in range(count // 2):
        one, two = from_a[q], from_b[64 * q : 64 * (q + 1), :]
        m = stack([jnp.where(odd, one, two), jnp.where(odd, two, one)]).T
        halo[2 * q] = m[:64].astype(F32)
        halo[2 * q + 1] = m[64:].astype(F32)
    for b in range(count):
        low = [slot[b, q] for q in range(9)]
        high = [slot[b, 18 + q] for q in range(9)]

        def source(q, j):
            rows = pl.ds(8 * j, 8)
            return jnp.where(small < 64, halo[low[q], rows, :], halo[high[q], rows, :])

        tiles = shifted_windows(source, row)
        for jr in range(6):
            for e in range(3):
                windows[b, e, jr] = tiles[jr][e]
    added = dot(
        beside(
            [
                windows[:, e, c : c + 4].reshape(count * 64, 128)
                for c in range(3)
                for e in range(3)
            ]
        ),
        face_taps[...],
    )
    groups = []
    for b in range(count):
        at = slice(64 * b, 64 * (b + 1))
        for side in range(2):
            near = (lane < 64) == (side == 0)
            sums = partial[3 * side, at] + jnp.where(near, added[at], 0.0)
            groups.append(masked_tiles(sums, pair_words, b, 3 * side))
            outer[b, side] = stack(groups[-1]).astype(BF16)
    sums = reduce_planes(groups, reduce, low_sums, high_sums)
    for b in range(count):
        at = slice(16 * b, 16 * (b + 1))
        planes = [
            (jnp.maximum(sums[2 * b + side], 0.0) * mask_two[3 * side, at]).astype(BF16)
            for side in range(2)
        ]
        second[16 * b : 16 * (b + 1)] = planes[0]
        second[16 * (count + b) : 16 * (count + b + 1)] = planes[1]
        to_b[at] = jnp.where(odd, planes[1], planes[0])
    rows = 16 * count
    to_b[rows : 2 * rows] = jnp.where(odd, inner[1], inner[0])
    to_b[2 * rows :] = jnp.where(odd, inner[0], inner[1])


def inner_kernel(
    middle, taps, partial, reduce, pair_words, mask_two,
    inner, second,
    low_sums, high_sums,
):
    count = middle.shape[0]
    added = dot(
        beside(
            [
                middle[:, e, c : c + 4].reshape(count * 64, 128)
                for c in range(3)
                for e in range(3)
            ]
        ),
        taps[...],
    )
    groups = []
    for b in range(count):
        at = slice(64 * b, 64 * (b + 1))
        for i in (1, 2):
            sums = partial[i, at] + added[at, 128 * (i - 1) : 128 * i]
            groups.append(masked_tiles(sums, pair_words, b, i))
            inner[b, i - 1] = stack(groups[-1]).astype(BF16)
    sums = reduce_planes(groups, reduce, low_sums, high_sums)
    for b in range(count):
        at = slice(16 * b, 16 * (b + 1))
        for i in (1, 2):
            second[i - 1, at] = (
                jnp.maximum(sums[2 * b + i - 1], 0.0) * mask_two[i, at]
            ).astype(BF16)


def output_kernel(outer, inner, out):
    for b in range(outer.shape[0]):
        ordered = [outer[b, 0], inner[b, 0], inner[b, 1], outer[b, 1]]
        for i in (0, 2):
            m = stack(ordered[i : i + 2]).T
            top, bottom = m[:64], m[64:]
            out[b, :, 128 * i : 128 * (i + 1)] = beside([top[:, :64], bottom[:, :64]])
            out[b, :, 128 * (i + 1) : 128 * (i + 2)] = beside([top[:, 64:], bottom[:, 64:]])


def face_part(gather, face, kernel, high):
    moved = dot(gather, face).astype(BF16)
    rows = moved.shape[0] // 9
    left = beside([moved[q * rows : (q + 1) * rows] for q in range(9)])
    weights = kernel[pl.ds(18 * high, 9)]
    return dot(left, weights.reshape(9 * weights.shape[1], weights.shape[2]))


def own_two_kernel(
    outer, inner, own_gather, gathers, from_a, kernel, first,
    partial, result, stored,
):
    copy = pltpu.make_async_copy(first, result, stored)
    copy.start()
    rows = inner.shape[1]
    planes = beside([outer[:rows], inner[0], inner[1], outer[rows:]])
    sides = stack([own_gather[: 4 * rows], own_gather[5 * rows :]])
    moved = dot(sides, planes).astype(BF16)
    taps = [moved[q * rows : (q + 1) * rows] for q in range(8)]
    taps.insert(4, planes)
    left = beside(
        [stack([tap[:, 128 * i : 128 * (i + 1)] for i in range(4)]) for tap in taps]
    )
    weights = [kernel[9 * a : 9 * (a + 1)].reshape(9 * 128, 128) for a in range(3)]
    sums = dot(left, beside(weights[:2]))
    later = dot(left[rows:], weights[2])
    high = jnp.where(on_odd_place(), 0, 1)
    near = face_part(gathers[high], from_a[...], kernel, high)
    for i in range(4):
        total = sums[i * rows : (i + 1) * rows, 128:]
        if i:
            total = total + sums[(i - 1) * rows : i * rows, :128]
        if i < 3:
            total = total + later[i * rows : (i + 1) * rows]
        if i in (0, 3):
            total = total + jnp.where(high == i // 3, near, 0.0)
        partial[i * rows : (i + 1) * rows] = total
    copy.wait()


def child_columns(picked, pairs, planes):
    return beside(
        [
            stack(
                [
                    picked[8 * (planes * q + i) : 8 * (planes * q + i + 1), 128 * n : 128 * (n + 1)]
                    for i in range(planes)
                    for n in range(pairs)
                ]
            )
            for q in range(8)
        ]
    )


def faces_two_kernel(
    gathers, far_gather, children, far_children, partial, to_b, from_b, kernel, reduce,
    mask_two, mask_three, far_mask_two, far_mask_three,
    second, third, far_third,
):
    count = second.shape[0]
    rows = 16 * count
    odd = on_odd_place()
    high = jnp.where(odd, 1, 0)
    none = jnp.zeros((rows, 128), BF16)
    sent = [from_b[d * rows : (d + 1) * rows] for d in range(3)]
    moved = dot(
        far_gather[...],
        stack([beside(sent + [none]), beside([none, none, none, to_b[:rows]])]),
    ).astype(BF16)
    left = [
        beside([moved[q * rows : (q + 1) * rows, 128 * d : 128 * (d + 1)] for q in range(9)])
        for d in range(4)
    ]
    moved = dot(gathers[high], sent[0]).astype(BF16)
    left.append(beside([moved[q * rows : (q + 1) * rows] for q in range(9)]))
    toward, same, away = [
        kernel[pl.ds(begin, 9)].reshape(9 * 128, 128) for begin in (18 - 18 * high, 9, 18 * high)
    ]
    zero = dot(stack([left[0], left[3]]), beside([same, toward]))
    one = dot(left[1], beside([away, same]))
    near = zero[rows:, 128:] + zero[:rows, :128] + one[:, :128]
    two = dot(stack([left[2], left[4]]), away)
    past = zero[:rows, 128:] + one[:, 128:] + two[:rows]
    far = two[rows:]
    planes = []
    for i in range(4):
        sums = partial[i * rows : (i + 1) * rows]
        if i in (0, 3):
            sums = sums + jnp.where(high == i // 3, far, 0.0)
        planes.append((jnp.maximum(sums, 0.0) * mask_two[i]).astype(BF16))
    bricks = [
        stack([planes[i][16 * b : 16 * (b + 1)] for i in range(4)]) for b in range(count)
    ]
    for b in range(count):
        second[b] = bricks[b]
    picked = dot(
        children[...], beside([stack(bricks[b : b + 2]) for b in range(0, count, 2)])
    )

    far_planes = [
        (jnp.maximum(sums, 0.0) * far_mask_two[n * rows : (n + 1) * rows]).astype(BF16)
        for n, sums in enumerate((jnp.where(odd, near, past), jnp.where(odd, past, near)))
    ]
    far_picked = dot(
        far_children[...],
        beside(
            [
                stack(
                    [
                        plane[16 * b : 16 * (b + 1)]
                        for b in (n, n + 1)
                        for plane in far_planes
                    ]
                )
                for n in range(0, count, 2)
            ]
        ),
    )
    left = stack(
        [child_columns(picked, count // 2, 2), child_columns(far_picked, count // 2, 1)]
    ).astype(BF16)
    sums = jnp.maximum(dot(left, reduce[...].reshape(8 * 128, 256)), 0.0)
    third[...] = (sums[: 8 * count] * mask_three[...]).astype(BF16)
    far_third[...] = (sums[8 * count :] * far_mask_three[...]).astype(BF16)


def own_three_kernel(gather, third, far, kernel, second, partial, result, stored):
    copy = pltpu.make_async_copy(second, result, stored)
    copy.start()
    rows = third.shape[0]
    moved = dot(gather[...], stack([third[...], far[...]])).astype(BF16)
    left = beside([moved[q * rows : (q + 1) * rows] for q in range(27)])
    partial[...] = dot(left, kernel[...].reshape(27 * 256, 256))
    copy.wait()


def faces_three_kernel(gather, partial, from_a, kernel, mask_three, out):
    rows = from_a.shape[0]
    odd = on_odd_place()
    near = face_part(gather[...], from_a[...], kernel, jnp.where(odd, 0, 1))
    low = partial[:rows] + jnp.where(odd, near, 0.0)
    high = partial[rows:] + jnp.where(odd, 0.0, near)
    low = jnp.maximum(low, 0.0) * mask_three[:rows]
    high = jnp.maximum(high, 0.0) * mask_three[rows:]
    row = iota((8, 256), 0)
    for n in range(rows // 8):
        near, past = low[8 * n : 8 * (n + 1)], high[8 * n : 8 * (n + 1)]
        out[2 * n] = jnp.where(row < 4, near, pltpu.roll(past, 4, 0)).astype(BF16)
        out[2 * n + 1] = jnp.where(row < 4, pltpu.roll(near, 4, 0), past).astype(BF16)


def level_two_picks():
    pick = np.zeros((432, 27), np.float32)
    for tap in range(27):
        for r in range(16):
            y, z = r // 4 + tap // 3 % 3 - 1, r % 4 + tap % 3 - 1
            pick[16 * tap + r, tap // 9 * 9 + 3 * (y // 4 + 1) + z // 4 + 1] = 16
    return jnp.asarray(pick, BF16)


def level_three_picks():
    pick = np.zeros((27 * 16, 27), np.float32)
    for tap in range(27):
        for r in range(16):
            x, y, z = [
                n + d - 1
                for n, d in (
                    (r // 8, tap // 9), (r // 2 % 2, tap // 3 % 3), (r % 2, tap % 3)
                )
            ]
            pick[16 * tap + r, 9 * (x // 2 + 1) + 3 * (y // 2 + 1) + z // 2 + 1] = 4
    return jnp.asarray(pick, BF16)


def child_rows(planes):
    pick = np.zeros((8 * planes * 8, 2 * 2 * planes * 16), np.float32)
    for q in range(8):
        for r in range(8 * planes):
            x, y, z = [
                2 * n + (q >> s & 1) for n, s in ((r // 8, 2), (r // 2 % 2, 1), (r % 2, 0))
            ]
            at = 2 * planes * 16 * (r // 4 % 2) + 16 * x + 4 * y + z
            pick[8 * planes * q + r, at] = 1
    return jnp.asarray(pick, BF16)


ANY = pl.BlockSpec(memory_space=pl.ANY)
VMEM = pl.BlockSpec(memory_space=pltpu.VMEM)
DMA = pltpu.SemaphoreType.DMA


def call(kernel, cost, out_shape, scratch, *args, remain=(), store=()):
    single = not isinstance(out_shape, tuple)
    outs = (out_shape,) if single else out_shape
    specs = tuple(ANY if n in store else VMEM for n in range(len(outs)))
    return pl.pallas_call(
        kernel,
        out_shape=out_shape,
        in_specs=[ANY if n in remain else VMEM for n in range(len(args))],
        out_specs=specs[0] if single else specs,
        scratch_shapes=scratch,
        compiler_params=pltpu.CompilerParams(vmem_limit_bytes=24 * 1024 * 1024),
        cost_estimate=pl.CostEstimate(
            flops=int(cost * 10**10), bytes_accessed=10**7, transcendentals=0
        ),
    )(*args)


def swaps(tiles, count):
    within, across = [], []
    for t in range(tiles):
        for m in range(count):
            if m ^ 1 < count:
                within.append((t * count + m, t * count + (m ^ 1)))
            other = ((m - 1) ^ 1) + 1 if m else -1
            if 0 <= other < count:
                across.append((t * count + m, t * count + other))
            elif t ^ 1 < tiles:
                across.append((t * count + m, (t ^ 1) * count + m))
    return within, across


def on_device(
    features,
    neighbours,
    occupancy,
    conv_one,
    first_reduce_kernel,
    conv_two,
    second_reduce_kernel,
    conv_three,
):
    axes = ("tiles", LINE)
    within, across = swaps(lax.axis_size("tiles"), lax.axis_size(LINE))
    count = features.shape[0]
    features = jnp.swapaxes(features, 1, 2)
    shape = jax.ShapeDtypeStruct

    def exchange(to_a, to_b):
        from_b = lax.ppermute(to_b, axes, across)
        return lax.ppermute(to_a, axes, within), from_b

    blank = call(blank_kernel, 1.0, shape((2 * count, 128), F32), [])
    bits, edge_bits, pair_words, mask_two, mask_three = call(
        masks_kernel,
        0.01,
        (
            shape((4, count, 128), F32),
            shape((2, count, 128), F32),
            shape((8, count, 128), jnp.int32),
            shape((4, 16 * count, 128), F32),
            shape((8 * count, 256), F32),
        ),
        [],
        occupancy, blank,
    )
    to_b = call(
        far_edge_kernel,
        0.02,
        shape((32 * count + 2 * count, 128), BF16),
        [pltpu.VMEM((2 * count, 128), F32)],
        features, bits, neighbours, edge_bits, blank,
    )
    face = shape((count // 2, 64, 128), BF16)
    to_a = call(near_edge_kernel, 0.02, face, [], features, bits, to_b)
    from_a, message = exchange(to_a, to_b)
    middle, taps, face_taps, reduce_taps, partial = call(
        outer_kernel,
        2.0,
        (
            shape((count, 3, 6, 16, 128), BF16),
            shape((9 * 128, 256), BF16),
            shape((9 * 128, 128), BF16),
            shape((256, 256), BF16),
            shape((4, count * 64, 128), F32),
        ),
        [
            pltpu.VMEM((4, count + 1, 64, 128), F32),
            pltpu.VMEM((count, 3, 4, 6, 16, 128), BF16),
            pltpu.VMEM((9 * 128, 256), BF16),
        ],
        neighbours, bits, features, conv_one, first_reduce_kernel,
    )
    plane = shape((16 * count, 128), BF16)
    rows = shape((count, 2, 64, 128), BF16)
    sums = pltpu.VMEM((count * 64 + 8, 128), F32)
    inner, inner_two = call(
        inner_kernel,
        0.05,
        (rows, shape((2, 16 * count, 128), BF16)),
        [sums, sums],
        middle, taps, partial, reduce_taps, pair_words, mask_two,
    )
    outer, outer_two, to_b = call(
        faces_one_kernel,
        1.5,
        (rows, shape((2 * 16 * count, 128), BF16), shape((3 * 16 * count, 128), BF16)),
        [
            pltpu.VMEM((count + 1, 64, 128), F32),
            pltpu.VMEM((count, 3, 6, 16, 128), BF16),
            sums,
            sums,
        ],
        neighbours, from_a, message, face_taps, partial, reduce_taps, pair_words, mask_two,
        inner_two,
    )
    to_a = call(near_face_kernel, 0.02, plane, [], outer_two, to_b)
    from_a, from_b = exchange(to_a, to_b)

    pick = level_two_picks()
    table = shape((9 * 16 * count, 16 * count), BF16)
    own_two, sides_two = call(
        level_two_tables_kernel,
        0.05,
        (table, shape((2, 9 * 16 * count, 16 * count), BF16)),
        [],
        neighbours, pick, to_a,
    )
    far_two, far_mask_two, far_mask_three = call(
        far_tables_kernel,
        0.05,
        (
            shape((9 * 16 * count, 32 * count), BF16),
            shape((2 * 16 * count, 128), F32),
            shape((4 * count, 256), F32),
        ),
        [],
        message, pick, to_a,
    )
    first_level = call(output_kernel, 0.05, shape(features.shape, BF16), [], outer, inner)
    partial, first_level = call(
        own_two_kernel,
        1.0,
        (shape((4 * 16 * count, 128), F32), shape(features.shape, BF16)),
        [DMA(())],
        outer_two, inner_two, own_two, sides_two, from_a, conv_two, first_level,
        store=(1,),
    )
    own_three, near_three = call(
        level_three_tables_kernel,
        0.05,
        (shape((27 * 8 * count, 12 * count), BF16), shape((9 * 4 * count, 4 * count), BF16)),
        [],
        neighbours, level_three_picks(), to_a,
    )
    face = shape((4 * count, 256), BF16)
    second_level, third, far_third = call(
        faces_two_kernel,
        1.5,
        (shape((count, 64, 128), BF16), shape((8 * count, 256), BF16), face),
        [],
        sides_two, far_two, child_rows(2), child_rows(1), partial, to_b, from_b, conv_two,
        second_reduce_kernel, mask_two, mask_three, far_mask_two, far_mask_three,
    )
    to_a = call(near_face_kernel, 0.02, face, [], third, far_third)
    from_a = lax.ppermute(to_a, axes, within)
    partial, second_level = call(
        own_three_kernel,
        1.0,
        (shape((8 * count, 256), F32), shape(second_level.shape, BF16)),
        [DMA(())],
        own_three, third, far_third, conv_three, second_level,
        store=(1,),
    )
    third_level = call(
        faces_three_kernel,
        1,
        shape((count, 8, 256), BF16),
        [],
        near_three, partial, from_a, conv_three, mask_three,
    )
    return jnp.swapaxes(first_level, 1, 2), second_level, third_level


def solution(mesh):
    split = P(("tiles", LINE))
    return jax.shard_map(
        on_device,
        mesh=mesh,
        in_specs=(split, split, split, P(), P(), P(), P(), P()),
        out_specs=(split, split, split),
        check_vma=False,
    )
```

```python
import jax
import jax.numpy as jnp
import numpy as np
from jax import lax
from jax.experimental import pallas as pl
from jax.experimental.pallas import tpu as pltpu
from jax.sharding import PartitionSpec as P

F32 = jnp.float32
BF16 = jnp.bfloat16
LINE = "morton"


def dot(x, y):
    return jnp.dot(x, y, preferred_element_type=F32)


def iota(shape, axis):
    return lax.broadcasted_iota(jnp.int32, shape, axis)


def stack(parts):
    return jnp.concatenate(parts, axis=0)


def beside(parts):
    return jnp.concatenate(parts, axis=1)


def bits_of(words, shift):
    return jnp.bitwise_and(lax.shift_right_logical(words, shift), 1).astype(F32)


def either(x, y):
    return jnp.bitwise_or(x, y)


def on_odd_place():
    return lax.rem(lax.axis_index(LINE), 2) == 1


def word_lanes(words, w):
    return jnp.broadcast_to(words[:, w : w + 1], (words.shape[0], 128))


def column_bits(words, column):
    lane = iota((words.shape[0], 128), 1)
    w = [word_lanes(words, 4 * column + q) for q in range(4)]
    chosen = jnp.where(
        lane < 64, jnp.where(lane < 32, w[0], w[1]), jnp.where(lane < 96, w[2], w[3])
    )
    return bits_of(chosen, jnp.bitwise_and(lane, 31))


def slot_numbers(neighbours):
    count = neighbours.shape[0]
    number = neighbours[...]
    tap = iota(number.shape, 1)
    shift = jnp.where(tap < 9, count, jnp.where(tap < 18, 0, -count))
    return jnp.where(number < 0, count, number + shift - lax.axis_index(LINE) * count)


def blank_kernel(notes):
    notes[...] = jnp.zeros(notes.shape, F32)


def masks_kernel(occupancy, blank, bits, edge_bits, pair_words, mask_two, mask_three):
    count = occupancy.shape[0]
    for q in range(4):
        bits[q] = column_bits(occupancy[...], q)
    words = [word_lanes(occupancy[...], w) for w in range(16)]
    lane = iota((count, 128), 1)
    row = iota((8, 128), 0)
    any_two = []
    for i in range(4):
        for half in range(2):
            low, high = words[4 * i + half], words[4 * i + 2 + half]
            pair_words[2 * i + half] = jnp.where(lane < 64, low, high)
            word = either(low, high)
            word = either(word, lax.shift_right_logical(word, 1))
            any_two.append(either(word, lax.shift_right_logical(word, 8)))
    two_shift = 16 * lax.shift_right_logical(row, 2) + 2 * jnp.bitwise_and(row, 3)
    for i in range(4):
        for b in range(count):
            mask_two[i, 16 * b : 16 * (b + 1)] = stack(
                [
                    bits_of(
                        jnp.broadcast_to(any_two[2 * i + half][b : b + 1], (8, 128)), two_shift
                    )
                    for half in range(2)
                ]
            )
    plane, half, m = [jnp.bitwise_and(lax.shift_right_logical(lane, n), 1) for n in (4, 3, 2)]
    for side in range(2):
        word = [any_two[4 * side + n] for n in range(4)]
        word = jnp.where(
            plane == 0, jnp.where(half == 0, word[0], word[1]), jnp.where(half == 0, word[2], word[3])
        )
        edge_bits[side] = bits_of(word, 16 * m + 2 * jnp.bitwise_and(lane, 3))
    any_three = []
    for i in range(2):
        for j in range(2):
            word = either(any_two[4 * i + j], any_two[4 * i + 2 + j])
            word = either(word, lax.shift_right_logical(word, 16))
            any_three.append(either(word, lax.shift_right_logical(word, 2)))
    for i in range(2):
        for b in range(0, count, 2):
            tile = [
                jnp.broadcast_to(any_three[2 * i + j][n : n + 1], (8, 128))
                for n in (b, b + 1)
                for j in range(2)
            ]
            tile = jnp.where(
                row < 4, jnp.where(row < 2, tile[0], tile[1]), jnp.where(row < 6, tile[2], tile[3])
            )
            mask = bits_of(tile, 4 * jnp.bitwise_and(row, 1))
            at = 4 * (count * i + b)
            mask_three[at : at + 8] = beside([mask, mask])


def edge_planes(features, bits, low_wanted):
    last = features.shape[2] - 128
    planes = []
    for q in range(features.shape[0] // 2):
        low, high = [
            [
                features[b, :, column * last : column * last + 128]
                * bits[3 * column, b : b + 1].astype(BF16)
                for b in (2 * q, 2 * q + 1)
            ]
            for column in range(2)
        ]
        lows = beside([low[0][:, :64], low[1][:, :64]])
        highs = beside([high[0][:, 64:], high[1][:, 64:]])
        planes.append(jnp.where(low_wanted, lows, highs))
    return planes


def far_edge_kernel(features, bits, neighbours, edge_bits, blank, edge, notes):
    count = features.shape[0]
    odd = on_odd_place()
    for q, plane in enumerate(edge_planes(features, bits, jnp.logical_not(odd))):
        edge[64 * q : 64 * (q + 1), :] = plane
    notes[...] = blank[...]
    notes[:count, : neighbours.shape[1]] = jnp.where(
        neighbours[...] < 0, 4 * count, slot_numbers(neighbours)
    ).astype(F32)
    notes[count:, :] = edge_bits[jnp.where(odd, 1, 0)]
    edge[32 * count :, :] = notes[...].astype(BF16)


def near_edge_kernel(features, bits, earlier, edge):
    for q, plane in enumerate(edge_planes(features, bits, on_odd_place())):
        edge[q] = plane


def near_face_kernel(planes, earlier, face):
    rows = face.shape[0]
    begin = pl.multiple_of(jnp.where(on_odd_place(), 0, rows), rows)
    face[...] = planes[pl.ds(begin, rows), :]


def slot_rows(slot):
    return stack(
        [jnp.broadcast_to(slot[b : b + 1], (128, slot.shape[1])) for b in range(slot.shape[0])]
    ).astype(BF16)


def own_slot_rows(neighbours):
    slot = jnp.where(neighbours[...] < 0, 4 * neighbours.shape[0], slot_numbers(neighbours))
    return slot_rows(slot.astype(F32))


def times_transposed(x, y):
    return lax.dot_general(x, y, (((1,), (1,)), ((), ())), preferred_element_type=F32)


def fill_level_two_tables(tables, rows, count):
    lane = iota((16, 16 * count), 1)
    row = iota((16, 16 * count), 0)
    j, k = lax.shift_right_logical(row, 2), jnp.bitwise_and(row, 3)
    for q in range(9):
        source = 4 * jnp.bitwise_and(j + q // 3 + 3, 3) + jnp.bitwise_and(k + q % 3 + 3, 3)
        wanted = (lane - source).astype(F32)
        for a, table in enumerate(tables):
            at = 16 * (9 * a + q)
            for b in range(count):
                table[16 * (count * q + b) : 16 * (count * q + b + 1), :] = jnp.where(
                    rows[at : at + 16, 128 * b : 128 * b + 16 * count] == wanted, 1.0, 0.0
                ).astype(BF16)


def level_two_tables_kernel(neighbours, pick, later, own_two, sides_two):
    rows = times_transposed(pick[...], own_slot_rows(neighbours))
    fill_level_two_tables(
        (sides_two.at[0], own_two, sides_two.at[1]), rows, neighbours.shape[0]
    )


def far_tables_kernel(message, pick, later, gather, mask_two, mask_three):
    count = gather.shape[1] // 32
    notes = message[32 * count :, :].astype(F32)
    slots = slot_rows(notes[:count, : pick.shape[1]])
    begin = pl.multiple_of(jnp.where(on_odd_place(), 0, 288), 16)
    rows = stack(
        [
            times_transposed(pick[pl.ds(begin, 144), :], slots),
            times_transposed(pick[144:288, :], slots),
        ]
    )
    width = 16 * count
    fill_level_two_tables((gather.at[:, width:], gather.at[:, :width]), rows, count)

    every = jnp.ones((128, 256), BF16)
    lane = iota((16, 128), 1)
    row = iota((16, 128), 0)
    bits = [notes[count + b : count + b + 1] for b in range(count)]
    chosen = stack(
        [
            jnp.where(lane == 16 * plane + row, jnp.broadcast_to(bits[b], (16, 128)), 0.0)
            for plane in range(2)
            for b in range(count)
        ]
    ).astype(BF16)
    mask_two[...] = dot(chosen, every[:, :128])
    lane, row = lane[:8], row[:8]
    child = jnp.bitwise_and(lax.shift_right_logical(lane, 2), 2) + jnp.bitwise_and(
        lax.shift_right_logical(lane, 1), 1
    )
    wanted = (child == jnp.bitwise_and(row, 3)) & (lane < 32)
    chosen = stack(
        [
            jnp.where(wanted, jnp.where(row < 4, bits[b], bits[b + 1]), 0.0)
            for b in range(0, count, 2)
        ]
    ).astype(BF16)
    mask_three[...] = jnp.where(dot(chosen, every) > 0.5, 1.0, 0.0)


def level_three_tables_kernel(neighbours, pick, later, own_three, near_three):
    count = neighbours.shape[0]
    odd = on_odd_place()
    rows = times_transposed(pick[...], own_slot_rows(neighbours))
    row = iota((8, 128), 0)
    lane = iota((8, 128), 1)
    j, k = [jnp.bitwise_and(lax.shift_right_logical(row, n), 1) for n in (1, 0)]

    def block(tap, i, begin):
        c, e = tap // 3 % 3, tap % 3
        source = 2 * jnp.bitwise_and(j + c + 1, 1) + jnp.bitwise_and(k + e + 1, 1)
        wanted = (lane - source - begin).astype(F32)
        at = 8 * (2 * tap + i)
        tiles = []
        for b in range(0, count, 2):
            first, second = [rows[at : at + 8, 128 * n : 128 * (n + 1)] for n in (b, b + 1)]
            hit = jnp.where(row < 4, first, second) == wanted
            tiles.append(jnp.where(hit, 1.0, 0.0))
        return stack(tiles)

    nowhere = 16 * 4 * count
    for tap in range(27):
        for i in range(2):
            x = i + tap // 9 - 1
            if x < 0:
                begin = jnp.where(odd, nowhere, 8 * count)
            elif x > 1:
                begin = jnp.where(odd, 8 * count, nowhere)
            else:
                begin = 4 * count * x
            at = 8 * count * tap + 4 * count * i
            own_three[at : at + 4 * count, :] = block(tap, i, begin)[:, : 12 * count].astype(BF16)
    for q in range(9):
        tile = jnp.where(odd, block(q, 0, 0), block(18 + q, 1, 0))
        near_three[4 * count * q : 4 * count * (q + 1), :] = tile[:, : 4 * count].astype(BF16)


def shifted_windows(source, row):
    shifted = []
    for j in range(-1, 9):
        c, at = (0, 7) if j < 0 else (2, 0) if j > 7 else (1, j)
        left, mid, right = [source(3 * c + e, at) for e in range(3)]
        shifted.append(
            (
                pltpu.roll(jnp.where(row == 7, left, mid), 1, 0),
                mid,
                pltpu.roll(jnp.where(row == 0, right, mid), 7, 0),
            )
        )
    return [
        [stack([shifted[jr][e], shifted[jr + 4][e]]).astype(BF16) for e in range(3)]
        for jr in range(6)
    ]


def outer_kernel(
    neighbours, bits, features, kernel, reduce,
    middle, taps, face_taps, reduce_taps, partial,
    tables, windows, wrap_taps,
):
    count = features.shape[0]
    row = iota((8, 128), 0)
    numbers = slot_numbers(neighbours)

    none = jnp.zeros((64, 64), BF16)
    for q in range(9):
        w = [kernel[9 * a + q] for a in range(3)]
        rows = slice(q * 128, (q + 1) * 128)
        taps[rows, :] = stack(
            [beside([w[2], w[1], w[0], none]), beside([none, w[2], w[1], w[0]])]
        )
        wrap_taps[rows, :] = stack(
            [beside([w[2], w[1], none, none]), beside([none, none, w[1], w[0]])]
        )
        face_taps[rows, :] = stack([beside([w[0], none]), beside([none, w[2]])])

    reduce_taps[...] = stack(
        [
            beside([reduce[4 * ci + 2 * cj], reduce[4 * ci + 2 * cj + 1]])
            for cj in range(2)
            for ci in range(2)
        ]
    )

    for pair in range(4):
        tables[pair, count] = jnp.zeros((64, 128), F32)
    for b in range(count):
        cols = [
            features[b, :, 128 * q : 128 * (q + 1)] * bits[q, b : b + 1].astype(BF16)
            for q in range(4)
        ]
        for p in (0, 2):
            m = stack(
                [
                    beside([cols[p][:, 64:], cols[p + 1][:, 64:]]),
                    beside([cols[p + 1][:, :64], cols[(p + 2) % 4][:, :64]]),
                ]
            ).T
            tables[p, b] = m[:64].astype(F32)
            tables[p + 1, b] = m[64:].astype(F32)

    for b in range(count):
        slot = [numbers[b, 9 + q] for q in range(9)]
        for pair in range(4):
            tiles = shifted_windows(lambda q, j: tables[pair, slot[q], pl.ds(8 * j, 8), :], row)
            for jr in range(6):
                for e in range(3):
                    if pair == 1:
                        middle[b, e, jr] = tiles[jr][e]
                    else:
                        windows[b, e, pair, jr] = tiles[jr][e]

    columns = [
        beside(
            [
                windows[:, e, pair, c : c + 4].reshape(count * 64, 128)
                for c in range(3)
                for e in range(3)
            ]
        )
        for pair in (0, 2, 3)
    ]
    both = dot(stack(columns[:2]), taps[...])
    wrap = dot(columns[2], wrap_taps[...])
    low, high = both[: count * 64], both[count * 64 :]
    partial[0] = low[:, :128] + wrap[:, 128:]
    partial[1] = low[:, 128:]
    partial[2] = high[:, :128]
    partial[3] = high[:, 128:] + wrap[:, :128]


def masked_tiles(sums, pair_words, b, i):
    row = iota((8, 128), 0)
    tiles = {}
    for half in range(2):
        words = jnp.broadcast_to(pair_words[2 * i + half, b : b + 1, :], (8, 128))
        for jr in range(4):
            at = jr * 16 + half * 8
            tiles[4 * half + jr] = jnp.maximum(sums[at : at + 8], 0.0) * bits_of(
                words, row + 8 * jr
            )
    return [tiles[j] for j in range(8)]


def reduce_planes(groups, weights, low_sums, high_sums):
    left = stack(
        [beside([tiles[j], tiles[j + 1]]) for tiles in groups for j in (0, 2, 4, 6)]
    ).astype(BF16)
    sums = dot(left, weights[...])
    low_sums[: sums.shape[0], :] = sums[:, :128]
    high_sums[: sums.shape[0], :] = sums[:, 128:]
    return [
        low_sums[pl.ds(32 * g, 16, stride=2), :] + high_sums[pl.ds(32 * g + 1, 16, stride=2), :]
        for g in range(len(groups))
    ]


def faces_one_kernel(
    neighbours, from_a, from_b, face_taps, partial, reduce, pair_words, mask_two, inner,
    outer, second, to_b,
    halo, windows, low_sums, high_sums,
):
    count = outer.shape[0]
    lane = iota((64, 128), 1)
    small = iota((8, 128), 1)
    row = iota((8, 128), 0)
    odd = on_odd_place()
    slot = slot_numbers(neighbours)
    halo[count] = jnp.zeros((64, 128), F32)
    for q in range(count // 2):
        one, two = from_a[q], from_b[64 * q : 64 * (q + 1), :]
        m = stack([jnp.where(odd, one, two), jnp.where(odd, two, one)]).T
        halo[2 * q] = m[:64].astype(F32)
        halo[2 * q + 1] = m[64:].astype(F32)
    for b in range(count):
        low = [slot[b, q] for q in range(9)]
        high = [slot[b, 18 + q] for q in range(9)]

        def source(q, j):
            rows = pl.ds(8 * j, 8)
            return jnp.where(small < 64, halo[low[q], rows, :], halo[high[q], rows, :])

        tiles = shifted_windows(source, row)
        for jr in range(6):
            for e in range(3):
                windows[b, e, jr] = tiles[jr][e]
    added = dot(
        beside(
            [
                windows[:, e, c : c + 4].reshape(count * 64, 128)
                for c in range(3)
                for e in range(3)
            ]
        ),
        face_taps[...],
    )
    groups = []
    for b in range(count):
        at = slice(64 * b, 64 * (b + 1))
        for side in range(2):
            near = (lane < 64) == (side == 0)
            sums = partial[3 * side, at] + jnp.where(near, added[at], 0.0)
            groups.append(masked_tiles(sums, pair_words, b, 3 * side))
            outer[b, side] = stack(groups[-1]).astype(BF16)
    sums = reduce_planes(groups, reduce, low_sums, high_sums)
    for b in range(count):
        at = slice(16 * b, 16 * (b + 1))
        planes = [
            (jnp.maximum(sums[2 * b + side], 0.0) * mask_two[3 * side, at]).astype(BF16)
            for side in range(2)
        ]
        second[16 * b : 16 * (b + 1)] = planes[0]
        second[16 * (count + b) : 16 * (count + b + 1)] = planes[1]
        to_b[at] = jnp.where(odd, planes[1], planes[0])
    rows = 16 * count
    to_b[rows : 2 * rows] = jnp.where(odd, inner[1], inner[0])
    to_b[2 * rows :] = jnp.where(odd, inner[0], inner[1])


def inner_kernel(
    middle, taps, partial, reduce, pair_words, mask_two,
    inner, second,
    low_sums, high_sums,
):
    count = middle.shape[0]
    added = dot(
        beside(
            [
                middle[:, e, c : c + 4].reshape(count * 64, 128)
                for c in range(3)
                for e in range(3)
            ]
        ),
        taps[...],
    )
    groups = []
    for b in range(count):
        at = slice(64 * b, 64 * (b + 1))
        for i in (1, 2):
            sums = partial[i, at] + added[at, 128 * (i - 1) : 128 * i]
            groups.append(masked_tiles(sums, pair_words, b, i))
            inner[b, i - 1] = stack(groups[-1]).astype(BF16)
    sums = reduce_planes(groups, reduce, low_sums, high_sums)
    for b in range(count):
        at = slice(16 * b, 16 * (b + 1))
        for i in (1, 2):
            second[i - 1, at] = (
                jnp.maximum(sums[2 * b + i - 1], 0.0) * mask_two[i, at]
            ).astype(BF16)


def output_kernel(outer, inner, out):
    for b in range(outer.shape[0]):
        ordered = [outer[b, 0], inner[b, 0], inner[b, 1], outer[b, 1]]
        for i in (0, 2):
            m = stack(ordered[i : i + 2]).T
            top, bottom = m[:64], m[64:]
            out[b, :, 128 * i : 128 * (i + 1)] = beside([top[:, :64], bottom[:, :64]])
            out[b, :, 128 * (i + 1) : 128 * (i + 2)] = beside([top[:, 64:], bottom[:, 64:]])


def face_part(gather, face, kernel, high):
    moved = dot(gather, face).astype(BF16)
    rows = moved.shape[0] // 9
    left = beside([moved[q * rows : (q + 1) * rows] for q in range(9)])
    weights = kernel[pl.ds(18 * high, 9)]
    return dot(left, weights.reshape(9 * weights.shape[1], weights.shape[2]))


def own_two_kernel(
    outer, inner, own_gather, gathers, from_a, kernel, first,
    partial, result, stored,
):
    copy = pltpu.make_async_copy(first, result, stored)
    copy.start()
    rows = inner.shape[1]
    planes = beside([outer[:rows], inner[0], inner[1], outer[rows:]])
    sides = stack([own_gather[: 4 * rows], own_gather[5 * rows :]])
    moved = dot(sides, planes).astype(BF16)
    taps = [moved[q * rows : (q + 1) * rows] for q in range(8)]
    taps.insert(4, planes)
    left = beside(
        [stack([tap[:, 128 * i : 128 * (i + 1)] for i in range(4)]) for tap in taps]
    )
    weights = [kernel[9 * a : 9 * (a + 1)].reshape(9 * 128, 128) for a in range(3)]
    sums = dot(left, beside(weights[:2]))
    later = dot(left[rows:], weights[2])
    high = jnp.where(on_odd_place(), 0, 1)
    near = face_part(gathers[high], from_a[...], kernel, high)
    for i in range(4):
        total = sums[i * rows : (i + 1) * rows, 128:]
        if i:
            total = total + sums[(i - 1) * rows : i * rows, :128]
        if i < 3:
            total = total + later[i * rows : (i + 1) * rows]
        if i in (0, 3):
            total = total + jnp.where(high == i // 3, near, 0.0)
        partial[i * rows : (i + 1) * rows] = total
    copy.wait()


def child_columns(picked, pairs, planes):
    return beside(
        [
            stack(
                [
                    picked[8 * (planes * q + i) : 8 * (planes * q + i + 1), 128 * n : 128 * (n + 1)]
                    for i in range(planes)
                    for n in range(pairs)
                ]
            )
            for q in range(8)
        ]
    )


def faces_two_kernel(
    gathers, far_gather, children, far_children, partial, to_b, from_b, kernel, reduce,
    mask_two, mask_three, far_mask_two, far_mask_three,
    second, third, far_third,
):
    count = second.shape[0]
    rows = 16 * count
    odd = on_odd_place()
    high = jnp.where(odd, 1, 0)
    none = jnp.zeros((rows, 128), BF16)
    sent = [from_b[d * rows : (d + 1) * rows] for d in range(3)]
    moved = dot(
        far_gather[...],
        stack([beside(sent + [none]), beside([none, none, none, to_b[:rows]])]),
    ).astype(BF16)
    left = [
        beside([moved[q * rows : (q + 1) * rows, 128 * d : 128 * (d + 1)] for q in range(9)])
        for d in range(4)
    ]
    moved = dot(gathers[high], sent[0]).astype(BF16)
    left.append(beside([moved[q * rows : (q + 1) * rows] for q in range(9)]))
    toward, same, away = [
        kernel[pl.ds(begin, 9)].reshape(9 * 128, 128) for begin in (18 - 18 * high, 9, 18 * high)
    ]
    zero = dot(stack([left[0], left[3]]), beside([same, toward]))
    one = dot(left[1], beside([away, same]))
    near = zero[rows:, 128:] + zero[:rows, :128] + one[:, :128]
    two = dot(stack([left[2], left[4]]), away)
    past = zero[:rows, 128:] + one[:, 128:] + two[:rows]
    far = two[rows:]
    planes = []
    for i in range(4):
        sums = partial[i * rows : (i + 1) * rows]
        if i in (0, 3):
            sums = sums + jnp.where(high == i // 3, far, 0.0)
        planes.append((jnp.maximum(sums, 0.0) * mask_two[i]).astype(BF16))
    bricks = [
        stack([planes[i][16 * b : 16 * (b + 1)] for i in range(4)]) for b in range(count)
    ]
    for b in range(count):
        second[b] = bricks[b]
    picked = dot(
        children[...], beside([stack(bricks[b : b + 2]) for b in range(0, count, 2)])
    )

    far_planes = [
        (jnp.maximum(sums, 0.0) * far_mask_two[n * rows : (n + 1) * rows]).astype(BF16)
        for n, sums in enumerate((jnp.where(odd, near, past), jnp.where(odd, past, near)))
    ]
    far_picked = dot(
        far_children[...],
        beside(
            [
                stack(
                    [
                        plane[16 * b : 16 * (b + 1)]
                        for b in (n, n + 1)
                        for plane in far_planes
                    ]
                )
                for n in range(0, count, 2)
            ]
        ),
    )
    left = stack(
        [child_columns(picked, count // 2, 2), child_columns(far_picked, count // 2, 1)]
    ).astype(BF16)
    sums = jnp.maximum(dot(left, reduce[...].reshape(8 * 128, 256)), 0.0)
    third[...] = (sums[: 8 * count] * mask_three[...]).astype(BF16)
    far_third[...] = (sums[8 * count :] * far_mask_three[...]).astype(BF16)


def own_three_kernel(gather, third, far, kernel, second, partial, result, stored):
    copy = pltpu.make_async_copy(second, result, stored)
    copy.start()
    rows = third.shape[0]
    moved = dot(gather[...], stack([third[...], far[...]])).astype(BF16)
    left = beside([moved[q * rows : (q + 1) * rows] for q in range(27)])
    partial[...] = dot(left, kernel[...].reshape(27 * 256, 256))
    copy.wait()


def faces_three_kernel(gather, partial, from_a, kernel, mask_three, out):
    rows = from_a.shape[0]
    odd = on_odd_place()
    near = face_part(gather[...], from_a[...], kernel, jnp.where(odd, 0, 1))
    low = partial[:rows] + jnp.where(odd, near, 0.0)
    high = partial[rows:] + jnp.where(odd, 0.0, near)
    low = jnp.maximum(low, 0.0) * mask_three[:rows]
    high = jnp.maximum(high, 0.0) * mask_three[rows:]
    row = iota((8, 256), 0)
    for n in range(rows // 8):
        near, past = low[8 * n : 8 * (n + 1)], high[8 * n : 8 * (n + 1)]
        out[2 * n] = jnp.where(row < 4, near, pltpu.roll(past, 4, 0)).astype(BF16)
        out[2 * n + 1] = jnp.where(row < 4, pltpu.roll(near, 4, 0), past).astype(BF16)


def level_two_picks():
    pick = np.zeros((432, 27), np.float32)
    for tap in range(27):
        for r in range(16):
            y, z = r // 4 + tap // 3 % 3 - 1, r % 4 + tap % 3 - 1
            pick[16 * tap + r, tap // 9 * 9 + 3 * (y // 4 + 1) + z // 4 + 1] = 16
    return jnp.asarray(pick, BF16)


def level_three_picks():
    pick = np.zeros((27 * 16, 27), np.float32)
    for tap in range(27):
        for r in range(16):
            x, y, z = [
                n + d - 1
                for n, d in (
                    (r // 8, tap // 9), (r // 2 % 2, tap // 3 % 3), (r % 2, tap % 3)
                )
            ]
            pick[16 * tap + r, 9 * (x // 2 + 1) + 3 * (y // 2 + 1) + z // 2 + 1] = 4
    return jnp.asarray(pick, BF16)


def child_rows(planes):
    pick = np.zeros((8 * planes * 8, 2 * 2 * planes * 16), np.float32)
    for q in range(8):
        for r in range(8 * planes):
            x, y, z = [
                2 * n + (q >> s & 1) for n, s in ((r // 8, 2), (r // 2 % 2, 1), (r % 2, 0))
            ]
            at = 2 * planes * 16 * (r // 4 % 2) + 16 * x + 4 * y + z
            pick[8 * planes * q + r, at] = 1
    return jnp.asarray(pick, BF16)


ANY = pl.BlockSpec(memory_space=pl.ANY)
VMEM = pl.BlockSpec(memory_space=pltpu.VMEM)
DMA = pltpu.SemaphoreType.DMA


def call(kernel, cost, out_shape, scratch, *args, remain=(), store=()):
    single = not isinstance(out_shape, tuple)
    outs = (out_shape,) if single else out_shape
    specs = tuple(ANY if n in store else VMEM for n in range(len(outs)))
    return pl.pallas_call(
        kernel,
        out_shape=out_shape,
        in_specs=[ANY if n in remain else VMEM for n in range(len(args))],
        out_specs=specs[0] if single else specs,
        scratch_shapes=scratch,
        compiler_params=pltpu.CompilerParams(vmem_limit_bytes=24 * 1024 * 1024),
        cost_estimate=pl.CostEstimate(
            flops=int(cost * 10**10), bytes_accessed=10**7, transcendentals=0
        ),
    )(*args)


def swaps(tiles, count):
    within, across = [], []
    for t in range(tiles):
        for m in range(count):
            if m ^ 1 < count:
                within.append((t * count + m, t * count + (m ^ 1)))
            other = ((m - 1) ^ 1) + 1 if m else -1
            if 0 <= other < count:
                across.append((t * count + m, t * count + other))
            elif t ^ 1 < tiles:
                across.append((t * count + m, (t ^ 1) * count + m))
    return within, across


def on_device(
    features,
    neighbours,
    occupancy,
    conv_one,
    first_reduce_kernel,
    conv_two,
    second_reduce_kernel,
    conv_three,
):
    axes = ("tiles", LINE)
    within, across = swaps(lax.axis_size("tiles"), lax.axis_size(LINE))
    count = features.shape[0]
    features = jnp.swapaxes(features, 1, 2)
    shape = jax.ShapeDtypeStruct

    def exchange(to_a, to_b):
        from_b = lax.ppermute(to_b, axes, across)
        return lax.ppermute(to_a, axes, within), from_b

    blank = call(blank_kernel, 1.0, shape((2 * count, 128), F32), [])
    bits, edge_bits, pair_words, mask_two, mask_three = call(
        masks_kernel,
        0.01,
        (
            shape((4, count, 128), F32),
            shape((2, count, 128), F32),
            shape((8, count, 128), jnp.int32),
            shape((4, 16 * count, 128), F32),
            shape((8 * count, 256), F32),
        ),
        [],
        occupancy, blank,
    )
    to_b = call(
        far_edge_kernel,
        0.02,
        shape((32 * count + 2 * count, 128), BF16),
        [pltpu.VMEM((2 * count, 128), F32)],
        features, bits, neighbours, edge_bits, blank,
    )
    face = shape((count // 2, 64, 128), BF16)
    to_a = call(near_edge_kernel, 0.02, face, [], features, bits, to_b)
    from_a, message = exchange(to_a, to_b)
    middle, taps, face_taps, reduce_taps, partial = call(
        outer_kernel,
        2.0,
        (
            shape((count, 3, 6, 16, 128), BF16),
            shape((9 * 128, 256), BF16),
            shape((9 * 128, 128), BF16),
            shape((256, 256), BF16),
            shape((4, count * 64, 128), F32),
        ),
        [
            pltpu.VMEM((4, count + 1, 64, 128), F32),
            pltpu.VMEM((count, 3, 4, 6, 16, 128), BF16),
            pltpu.VMEM((9 * 128, 256), BF16),
        ],
        neighbours, bits, features, conv_one, first_reduce_kernel,
    )
    plane = shape((16 * count, 128), BF16)
    rows = shape((count, 2, 64, 128), BF16)
    sums = pltpu.VMEM((count * 64 + 8, 128), F32)
    inner, inner_two = call(
        inner_kernel,
        0.05,
        (rows, shape((2, 16 * count, 128), BF16)),
        [sums, sums],
        middle, taps, partial, reduce_taps, pair_words, mask_two,
    )
    outer, outer_two, to_b = call(
        faces_one_kernel,
        1.5,
        (rows, shape((2 * 16 * count, 128), BF16), shape((3 * 16 * count, 128), BF16)),
        [
            pltpu.VMEM((count + 1, 64, 128), F32),
            pltpu.VMEM((count, 3, 6, 16, 128), BF16),
            sums,
            sums,
        ],
        neighbours, from_a, message, face_taps, partial, reduce_taps, pair_words, mask_two,
        inner_two,
    )
    to_a = call(near_face_kernel, 0.02, plane, [], outer_two, to_b)
    from_a, from_b = exchange(to_a, to_b)

    pick = level_two_picks()
    table = shape((9 * 16 * count, 16 * count), BF16)
    own_two, sides_two = call(
        level_two_tables_kernel,
        0.05,
        (table, shape((2, 9 * 16 * count, 16 * count), BF16)),
        [],
        neighbours, pick, to_a,
    )
    far_two, far_mask_two, far_mask_three = call(
        far_tables_kernel,
        0.05,
        (
            shape((9 * 16 * count, 32 * count), BF16),
            shape((2 * 16 * count, 128), F32),
            shape((4 * count, 256), F32),
        ),
        [],
        message, pick, to_a,
    )
    first_level = call(output_kernel, 0.05, shape(features.shape, BF16), [], outer, inner)
    partial, first_level = call(
        own_two_kernel,
        1.0,
        (shape((4 * 16 * count, 128), F32), shape(features.shape, BF16)),
        [DMA(())],
        outer_two, inner_two, own_two, sides_two, from_a, conv_two, first_level,
        store=(1,),
    )
    own_three, near_three = call(
        level_three_tables_kernel,
        0.05,
        (shape((27 * 8 * count, 12 * count), BF16), shape((9 * 4 * count, 4 * count), BF16)),
        [],
        neighbours, level_three_picks(), to_a,
    )
    face = shape((4 * count, 256), BF16)
    second_level, third, far_third = call(
        faces_two_kernel,
        0.05,
        (shape((count, 64, 128), BF16), shape((8 * count, 256), BF16), face),
        [],
        sides_two, far_two, child_rows(2), child_rows(1), partial, to_b, from_b, conv_two,
        second_reduce_kernel, mask_two, mask_three, far_mask_two, far_mask_three,
    )
    to_a = call(near_face_kernel, 0.02, face, [], third, far_third)
    from_a = lax.ppermute(to_a, axes, within)
    partial, second_level = call(
        own_three_kernel,
        1.0,
        (shape((8 * count, 256), F32), shape(second_level.shape, BF16)),
        [DMA(())],
        own_three, third, far_third, conv_three, second_level,
        store=(1,),
    )
    third_level = call(
        faces_three_kernel,
        1,
        shape((count, 8, 256), BF16),
        [],
        near_three, partial, from_a, conv_three, mask_three,
    )
    return jnp.swapaxes(first_level, 1, 2), second_level, third_level


def solution(mesh):
    split = P(("tiles", LINE))
    return jax.shard_map(
        on_device,
        mesh=mesh,
        in_specs=(split, split, split, P(), P(), P(), P(), P()),
        out_specs=(split, split, split),
        check_vma=False,
    )
```
